128 devices in a mesh: pat: 16 (over y, x), obj: 8 (over z, core).
Axes of the slice: x: 4, y: 4, z: 4, core: 2. Of those that a mesh axis runs over, the one named last changes fastest.
Arguments:
- object_field: float32 [2, 1024, 16384], P(None, None, 'obj'), may hold values from -4 to 4
- probe: float32 [2, 256, 256], replicated, may hold values from -6 to 6
- amplitude: float32 [1024, 256, 256], P(('pat', 'obj')), may hold values from 0.1 to 3
- tile_owner: int32 [1024, 1], P(('pat', 'obj')), may hold values from 0 to 7; in each aligned block of 8 rows (0 to 7, 8 to 15, ...) at most 2 rows name the same one
- row_start: int32 [1024], P(('pat', 'obj')), may hold values from 0 to 768, as said below
- col_start: int32 [1024], P(('pat', 'obj')), may hold values from 0 to 1792
Outputs:
- object_grad: float32 [2, 1024, 16384], P(None, 'pat', 'obj')
- probe_grad: float32 [2, 256, 256], replicated
The draws below stay inside these ranges and needn't reach their ends.
Inputs may be any that keep to these rules, and one draw needn't show every extreme that they name: `tile_owner`: among the patterns of one device at most 2 name the same tile, and in some device some tile is named by exactly 2. `row_start`: every pattern held by the devices of index g along pat starts its window at row min(g * 64 + e, 768) for some e with 0 <= e < 64.
All inputs are finite; a program needn't handle non-finite values.
Results may differ from the reference program's by a relative error of at most 0.0001.
Values sent between devices are 32-bit elements; how exact they have to be, the bound alone decides.
A program may use at most 192 MiB of HBM per device.

```python
import math
import jax
import jax.numpy as jnp
import numpy as np
from jax import lax

PATCH = 256
ROWS = 1024
TILE_W = 2048
PAT_DEV = 8
CAP = 2
WIDTH = 16384
PATTERNS = 1024
N_PAT = 16
N_OBJ = 8


def draw_row_start(key, part):
    key = jax.random.fold_in(key, 5)
    strip = ROWS // N_PAT
    position = jnp.arange(PATTERNS, dtype=jnp.int32)
    group = position // (PATTERNS // N_PAT)
    extra = jax.random.randint(key, (PATTERNS,), 0, strip, dtype=jnp.int32)
    return jnp.minimum(group * strip + extra, ROWS - PATCH).astype(jnp.int32)


def plant(array, key, low, high):
    longest = array.shape.index(max(array.shape))
    spots = []
    for shift in (0, 1):
        where = [jax.random.randint(jax.random.fold_in(key, axis), (), 0, length) for axis, length in enumerate(array.shape)]
        where[longest] = (where[longest] + shift) % array.shape[longest]
        spots.append(tuple(where))
    return array.at[spots[0]].set(low).at[spots[1]].set(high)


def block_levels(key, shape, shards, low, high):
    factor_of = 1.0
    for axis_at, shards_of in shards:
        steps = jax.random.uniform(jax.random.fold_in(jax.random.fold_in(key, 6), axis_at), (shards_of,), jnp.float32, low / len(shards), high / len(shards))
        factor_of = factor_of * jnp.repeat(jnp.exp(steps), shape[axis_at] // shards_of).reshape((-1,) + (1,) * (len(shape) - 1 - axis_at))
    return factor_of


def shared_out(stream_key, own, number, rows, count, top, reach, skew):
    order = jax.random.permutation(stream_key, count)
    crowded, ordinary = portions_of(count, rows * top, reach, skew, True), portions_of(count, rows * top, reach, skew, False)
    places = jnp.arange(count)

    def named(lengths, turn):
        used = int((lengths > 0).sum())
        fixed = max(1, used // 4)
        passed = fixed + (places - fixed + turn * (used - fixed)) % max(1, count - fixed)
        return jnp.zeros((count,), jnp.int32).at[order[jnp.where(places < fixed, places, passed)]].set(jnp.asarray(lengths, jnp.int32))

    lengths = jnp.where(number % 4 == 0, named(crowded, number // 4), named(ordinary, number - number // 4 - 1))
    mixed = jax.random.permutation(jax.random.fold_in(own, 3), count)
    giver, taker = mixed[0:count // 2 * 2:2], mixed[1:count // 2 * 2:2]
    margin = jnp.minimum(lengths[giver] - 1, reach - lengths[taker]) // 2
    margin = jnp.where((giver == order[0]) | (taker == order[0]) | (lengths[taker] == 0), 0, jnp.maximum(margin, 0))
    passed = jax.random.randint(jax.random.fold_in(own, 4), (count // 2,), 0, 1 << 20) % (margin + 1)
    lengths = lengths.at[giver].add(-passed).at[taker].add(passed)
    members = jnp.searchsorted(jnp.cumsum(lengths), jnp.arange(rows * top), side="right").astype(jnp.int32)
    table = members.reshape(top, rows).T
    table = table[jax.random.permutation(jax.random.fold_in(own, 1), rows)]
    turn = jax.random.randint(jax.random.fold_in(own, 2), (rows, 1), 0, top)
    return jnp.take_along_axis(table, (jnp.arange(top)[None, :] + turn) % top, axis=1)


def portions_of(number_of, total, reach, lean, full):
    loads = [(1 << 20) // math.isqrt(grade ** lean) + 1 for grade in range(1, number_of + 1)]
    largest = reach if full else min(reach, max(-(-total // number_of), total * loads[0] // sum(loads)))
    least = 1 if total - largest >= number_of - 1 else 0
    holding, surplus = [largest] + [least] * (number_of - 1), total - largest - least * (number_of - 1)
    while surplus > 0:
        candidates = [i for i in range(1, number_of) if holding[i] < largest] or [i for i in range(1, number_of) if holding[i] < reach]
        whole, budget = sum([loads[i] for i in candidates]), surplus
        for i in candidates:
            more = min(reach - holding[i], max(1, budget * loads[i] // whole), surplus)
            holding[i] = holding[i] + more
            surplus = surplus - more
    return np.array(holding)


def gaussian(stream_key, shape, width, most, pieces=(), kind=jnp.bfloat16):
    array = jax.random.normal(stream_key, shape, jnp.float32) * width
    if len(pieces) > 0:
        array = block_levels(stream_key, shape, pieces, -0.22, 0.18) * array
    return jnp.clip(array, min=-most, max=most).astype(kind)


def setup_inputs(seed: int = 0) -> dict:
    arg_keys = jax.random.split(jax.random.key(seed), 7)
    object_field = gaussian(arg_keys[0], (2, ROWS, WIDTH), 0.7, 4.0, ((2, 8),), jnp.float32)
    probe = gaussian(arg_keys[1], (2, PATCH, PATCH), 1.0, 6.0, (), jnp.float32)
    amplitude = jnp.clip(jnp.exp(math.log(3.0) - 3.4011974 * jax.random.uniform(arg_keys[2], (PATTERNS, PATCH, PATCH), jnp.float32) ** block_levels(arg_keys[2], (PATTERNS, PATCH, PATCH), ((0, 128),), -0.2, 0.2)), 0.1, 3.0)
    tile_owner_keys = jax.random.split(jax.random.fold_in(arg_keys[3], 1), PATTERNS // PAT_DEV)
    tile_owner_turns = jax.random.permutation(jax.random.fold_in(arg_keys[3], 3), PATTERNS // PAT_DEV)
    tile_owner = jax.vmap(lambda own, number: shared_out(jax.random.fold_in(arg_keys[3], 2), own, number, PAT_DEV, N_OBJ, 1, CAP, 2))(tile_owner_keys, tile_owner_turns).reshape((PATTERNS, 1))
    row_start = draw_row_start(jax.random.fold_in(arg_keys[6], 71), 0)
    col_start = plant(jax.random.randint(arg_keys[5], (PATTERNS,), 0, TILE_W - PATCH + 1), jax.random.fold_in(arg_keys[5], 1), 0, TILE_W - PATCH).astype(jnp.int32)
    return dict(object_field=object_field, probe=probe, amplitude=amplitude, tile_owner=tile_owner, row_start=row_start, col_start=col_start)


soften = 0.25

def reference(object_field, probe, amplitude, tile_owner, row_start, col_start):
    object_wave = object_field[0].astype(jnp.float32) + 1j * object_field[1].astype(jnp.float32)
    lighting = probe[0] + 1j * probe[1]
    columns = (tile_owner[:, 0] * TILE_W + col_start).astype(jnp.int32)
    top_rows = row_start.astype(jnp.int32)

    def visit_one(totals, inputs):
        gradient, probe_total = totals
        pattern, top_row, column = inputs
        window = lax.dynamic_slice(object_wave, (top_row, column), (PATCH, PATCH))
        exit_wave = lighting * window
        spectrum = jnp.fft.fft2(exit_wave, norm='ortho')
        magnitude = jnp.sqrt(jnp.real(spectrum) ** 2 + jnp.imag(spectrum) ** 2 + soften)
        residual = jnp.fft.ifft2(pattern * spectrum / magnitude, norm='ortho') - exit_wave
        before = lax.dynamic_slice(gradient, (top_row, column), (PATCH, PATCH))
        gradient = lax.dynamic_update_slice(gradient, before + jnp.conj(lighting) * residual, (top_row, column))
        return ((gradient, probe_total + jnp.conj(window) * residual), None)
    start_state = (jnp.zeros(object_wave.shape, object_wave.dtype), jnp.zeros(lighting.shape, object_wave.dtype))
    final_state, unused = lax.scan(visit_one, start_state, (amplitude.astype(jnp.float32), top_rows, columns))
    gradient, probe_total = final_state
    object_grad = jnp.stack([jnp.real(gradient), jnp.imag(gradient)])
    probe_grad = jnp.stack([jnp.real(probe_total), jnp.imag(probe_total)]) / jnp.sqrt(jnp.float32(PATTERNS))
    return (object_grad, probe_grad)
```

```python
import math

import jax
import jax.numpy as jnp
import numpy as np
from jax import lax
from jax.experimental import pallas as pl
from jax.experimental.pallas import tpu as pltpu
from jax.sharding import PartitionSpec as P

MESH = pl.DeviceIdType.MESH
CAP = 2
SIDE = 256
HALF = 128
STRIP = 64
SPAN = 320
TILE = 2048
BLOCKS = TILE // HALF
SOFTEN = 0.25
OWNERS = 8
COUNT = 8
SLOTS = OWNERS * CAP
NX = 4
NY = 4
CHUNKS = 8
CHUNK = BLOCKS // CHUNKS
F32 = jnp.float32
BF16 = jnp.bfloat16
ANY = pl.BlockSpec(memory_space=pl.ANY)
VMEM = pl.BlockSpec(memory_space=pltpu.VMEM)
SMEM = pl.BlockSpec(memory_space=pltpu.SMEM)


def dft_tables():
    index = np.arange(SIDE)
    full = np.exp(-2j * np.pi * (np.outer(index, index) % SIDE) / SIDE) / math.sqrt(SIDE)

    def right(table):
        return np.block([[table.real, table.imag], [-table.imag, table.real]])

    swap = np.roll(np.arange(HALF), -HALF // 2)
    half = [full[:HALF, 0::2], full[:HALF, 1::2]]
    lane = [half[0], half[1][:, swap]]
    tables = [
        right(lane[0]),
        right(lane[1]),
        right(half[0]).T,
        right(half[1]).T,
        right(half[0].conj().T).T,
        right(half[1].conj().T).T,
        right(lane[0].conj().T),
        right(lane[1].conj().T),
    ]
    exact = np.stack(tables).astype(np.float32)
    high = exact.astype(BF16)
    low = (exact - high.astype(np.float32)).astype(BF16)
    return np.stack([high, low], axis=1)


def split(value):
    high = value.astype(BF16)
    return high, (value - high.astype(F32)).astype(BF16)


def times_table(data, table):
    high, low = split(data)
    left = jnp.concatenate([high, low, high], axis=1)
    right = jnp.concatenate([table[0], table[0], table[1]], axis=0)
    return jnp.dot(left, right, preferred_element_type=F32)


def table_times(table, data):
    high, low = split(data)
    left = jnp.concatenate([table[0], table[0], table[1]], axis=1)
    right = jnp.concatenate([high, low, high], axis=0)
    return jnp.dot(left, right, preferred_element_type=F32)


def beside(*parts):
    return jnp.concatenate(parts, axis=1)


def above(*parts):
    return jnp.concatenate(parts, axis=0)


def by_parity(rows):
    lane = lax.broadcasted_iota(jnp.int32, (HALF, HALF), 1)
    front = lane < HALF // 2
    first = jnp.take_along_axis(
        rows[:, :HALF], jnp.where(front, 2 * lane, 2 * lane - HALF + 1), axis=1, mode="promise_in_bounds"
    )
    second = jnp.take_along_axis(
        rows[:, HALF:], jnp.where(front, 2 * lane + 1, 2 * lane - HALF), axis=1, mode="promise_in_bounds"
    )
    return beside(jnp.where(front, first, second), jnp.where(front, second, first))


def residual_wave(exit_re, exit_im, wanted_rows, tables):
    front = slice(0, HALF)
    back = slice(HALF, SIDE)
    even = times_table(
        beside(exit_re[:, front] + exit_re[:, back], exit_im[:, front] + exit_im[:, back]), tables(0)
    )
    odd = times_table(
        beside(exit_re[:, front] - exit_re[:, back], exit_im[:, front] - exit_im[:, back]), tables(1)
    )
    re = beside(even[:, front], odd[:, front])
    im = beside(even[:, back], odd[:, back])
    spectrum = [
        table_times(tables(2), above(re[front] + re[back], im[front] + im[back])),
        table_times(tables(3), above(re[front] - re[back], im[front] - im[back])),
    ]
    scaled = []
    for parity in range(2):
        re, im = spectrum[parity][front], spectrum[parity][back]
        ratio = wanted_rows(parity) * lax.rsqrt(re * re + im * im + SOFTEN)
        scaled.append(above(re * ratio, im * ratio))
    even = table_times(tables(4), scaled[0])
    odd = table_times(tables(5), scaled[1])
    re = above(even[front] + odd[front], even[front] - odd[front])
    im = above(even[back] + odd[back], even[back] - odd[back])
    even = times_table(beside(re[:, front], im[:, front]), tables(6))
    odd = times_table(beside(re[:, back], im[:, back]), tables(7))
    back_re = beside(even[:, front] + odd[:, front], even[:, front] - odd[:, front])
    back_im = beside(even[:, back] + odd[:, back], even[:, back] - odd[:, back])
    return back_re - exit_re, back_im - exit_im


def pack_kernel(owner_ref, row_ref, col_ref, amp_ref, packed_ref, meta_ref, sems):
    ranks = []
    copies = []
    for j in range(COUNT):
        rank = jnp.int32(0)
        for i in range(j):
            rank = rank + (owner_ref[i, 0] == owner_ref[j, 0]).astype(jnp.int32)
        ranks.append(rank)
        for side in range(2):
            copy = pltpu.make_async_copy(
                amp_ref.at[j, :, pl.ds(side * HALF, HALF)],
                packed_ref.at[owner_ref[j, 0], rank, side],
                sems.at[j, side],
            )
            copy.start()
            copies.append(copy)
    meta_ref[...] = jnp.zeros_like(meta_ref)
    sub = lax.broadcasted_iota(jnp.int32, (8, 128), 0)
    for j in range(COUNT):
        shape = (sub // 4 == ranks[j]) & (sub % 4 < 3)
        value = jnp.where(
            sub % 4 == 0, 1, jnp.where(sub % 4 == 1, row_ref[j], col_ref[j])
        )
        tile = meta_ref[owner_ref[j, 0]]
        meta_ref[owner_ref[j, 0]] = jnp.where(shape, value, tile)
    for copy in copies:
        copy.wait()


def pack(tile_owner, row_start, col_start, amplitude):
    return pl.pallas_call(
        pack_kernel,
        out_shape=(
            jax.ShapeDtypeStruct((OWNERS, CAP, 2, SIDE, HALF), F32),
            jax.ShapeDtypeStruct((OWNERS, 8, 128), jnp.int32),
        ),
        in_specs=[SMEM, SMEM, SMEM, ANY],
        out_specs=(ANY, VMEM),
        scratch_shapes=[pltpu.SemaphoreType.DMA((COUNT, 2))],
        name="pack",
    )(tile_owner, row_start, col_start, amplitude)


def exchange_kernel(packed_ref, meta_ref, got_ref, got_meta_ref, here, send, recv, send_meta, recv_meta):
    me = lax.axis_index("obj")
    barrier = pltpu.get_barrier_semaphore()
    for k in range(1, OWNERS):
        pl.semaphore_signal(
            barrier, inc=1, device_id={"obj": lax.rem(me + k, OWNERS)}, device_id_type=MESH
        )
    pl.semaphore_wait(barrier, OWNERS - 1)
    copies = []
    for k in range(1, OWNERS):
        there = lax.rem(me + k, OWNERS)
        copies.append(
            pltpu.make_async_remote_copy(
                src_ref=meta_ref.at[there],
                dst_ref=got_meta_ref.at[me],
                send_sem=send_meta.at[k],
                recv_sem=recv_meta.at[k],
                device_id={"obj": there},
                device_id_type=MESH,
            )
        )
        copies.append(
            pltpu.make_async_remote_copy(
                src_ref=packed_ref.at[there],
                dst_ref=got_ref.at[me],
                send_sem=send.at[k],
                recv_sem=recv.at[k],
                device_id={"obj": there},
                device_id_type=MESH,
            )
        )
    copies.append(pltpu.make_async_copy(packed_ref.at[me], got_ref.at[me], here.at[0]))
    copies.append(pltpu.make_async_copy(meta_ref.at[me], got_meta_ref.at[me], here.at[1]))
    for copy in copies:
        copy.start()
    for copy in copies:
        copy.wait()


def exchange(packed, meta):
    return pl.pallas_call(
        exchange_kernel,
        out_shape=(
            jax.ShapeDtypeStruct(packed.shape, F32),
            jax.ShapeDtypeStruct(meta.shape, jnp.int32),
        ),
        in_specs=[ANY, ANY],
        out_specs=(ANY, ANY),
        scratch_shapes=[pltpu.SemaphoreType.DMA((2,))] + [pltpu.SemaphoreType.DMA((OWNERS,))] * 4,
        compiler_params=pltpu.CompilerParams(collective_id=0, has_side_effects=True),
        name="exchange",
    )(packed, meta)


def update_kernel(meta_ref, amp_ref, object_ref, probe_ref, tables_ref, grad_ref, part_ref, strip, sem):
    slot = pl.program_id(0)
    group = lax.axis_index("pat")
    base = pl.multiple_of(jnp.minimum(group, 11) * STRIP, STRIP)

    @pl.when(slot == 0)
    def _():
        copies = []
        for block in range(BLOCKS):
            copies.append(
                pltpu.make_async_copy(
                    object_ref.at[:, pl.ds(base, SPAN), pl.ds(block * HALF, HALF)], strip.at[:, block], sem.at[block]
                )
            )
        for copy in copies:
            copy.start()
        grad_ref[...] = jnp.zeros_like(grad_ref)
        part_ref[...] = jnp.zeros_like(part_ref)
        for copy in copies:
            copy.wait()

    sender = slot // CAP
    place = 4 * (slot % CAP)

    @pl.when(meta_ref[sender, place, 0] > 0)
    def _():
        row = jnp.clip(meta_ref[sender, place + 1, 0] - base, 0, STRIP)
        col = meta_ref[sender, place + 2, 0]
        start = jnp.minimum(col // HALF, BLOCKS - 3)
        shift = col - start * HALF
        unshift = lax.rem(HALF - shift, HALF)
        lane = lax.broadcasted_iota(jnp.int32, (SIDE, HALF), 1)

        def window(part):
            turned = [
                pltpu.roll(strip[part, start + n, pl.ds(row, SIDE), :], unshift, axis=1) for n in range(3)
            ]
            inner = lane < HALF - shift
            return beside(jnp.where(inner, turned[0], turned[1]), jnp.where(inner, turned[1], turned[2]))

        probe_re = probe_ref[0]
        probe_im = probe_ref[1]
        window_re = window(0)
        window_im = window(1)
        exit_re = probe_re * window_re - probe_im * window_im
        exit_im = probe_re * window_im + probe_im * window_re

        def wanted_rows(parity):
            return by_parity(
                beside(
                    amp_ref[0, 0, 0, pl.ds(parity, HALF, stride=2), :],
                    amp_ref[0, 0, 1, pl.ds(parity, HALF, stride=2), :],
                )
            )

        res_re, res_im = residual_wave(
            exit_re, exit_im, wanted_rows, lambda i: (tables_ref[i, 0], tables_ref[i, 1])
        )
        part_ref[0] += window_re * res_re + window_im * res_im
        part_ref[1] += window_re * res_im - window_im * res_re

        def add(part, value):
            turn = lax.rem(shift, HALF)
            first = pltpu.roll(value[:, :HALF], turn, axis=1)
            second = pltpu.roll(value[:, HALF:], turn, axis=1)
            outer = lane >= shift
            grad_ref[part, start, pl.ds(row, SIDE), :] += jnp.where(outer, first, 0.0)
            grad_ref[part, start + 1, pl.ds(row, SIDE), :] += jnp.where(outer, second, first)
            grad_ref[part, start + 2, pl.ds(row, SIDE), :] += jnp.where(outer, 0.0, second)

        add(0, probe_re * res_re + probe_im * res_im)
        add(1, probe_re * res_im - probe_im * res_re)


def update(meta, amplitude, object_field, probe, tables):
    return pl.pallas_call(
        update_kernel,
        grid=(SLOTS,),
        out_shape=(
            jax.ShapeDtypeStruct((2, BLOCKS, SPAN, HALF), F32),
            jax.ShapeDtypeStruct((2, SIDE, SIDE), F32),
        ),
        in_specs=[
            SMEM,
            pl.BlockSpec((1, 1, 2, SIDE, HALF), lambda s: (s // CAP, s % CAP, 0, 0, 0)),
            ANY,
            pl.BlockSpec((2, SIDE, SIDE), lambda s: (0, 0, 0)),
            pl.BlockSpec(tables.shape, lambda s: (0, 0, 0, 0)),
        ],
        out_specs=(
            pl.BlockSpec((2, BLOCKS, SPAN, HALF), lambda s: (0, 0, 0, 0)),
            pl.BlockSpec((2, SIDE, SIDE), lambda s: (0, 0, 0)),
        ),
        scratch_shapes=[pltpu.VMEM((2, BLOCKS, SPAN, HALF), F32), pltpu.SemaphoreType.DMA((BLOCKS,))],
        compiler_params=pltpu.CompilerParams(
            vmem_limit_bytes=48 * 2**20, dimension_semantics=("arbitrary",)
        ),
        name="update",
    )(meta, amplitude, object_field, probe, tables)


def combine_kernel(
    grad_ref, part_ref, out_ref, probe_ref,
    own, rise, got_x, got_y, near, quarter, sixteenth,
    load, send_x, recv_x, send_y, recv_y,
    send_a, recv_a, send_b, recv_b, send_c, recv_c, send_d, recv_d, send_e, recv_e,
):
    me = lax.axis_index("obj")
    group = lax.axis_index("pat")
    x = lax.rem(group, NX)
    y = group // NX
    last = y == NY - 1

    def obj_peer(k):
        return {"obj": lax.rem(me + k, OWNERS)}

    def x_peer(k):
        return {"pat": y * NX + lax.rem(x + k, NX)}

    def y_peer(k):
        return {"pat": lax.rem(y + k, NY) * NX + x}

    peers = [obj_peer(k) for k in range(1, OWNERS)]
    peers += [x_peer(k) for k in range(1, NX)] + [y_peer(k) for k in range(1, NY)]
    barrier = pltpu.get_barrier_semaphore()
    for peer in peers:
        pl.semaphore_signal(barrier, inc=1, device_id=peer, device_id_type=MESH)

    def block(number):
        return pl.ds(pl.multiple_of(number * STRIP, STRIP), STRIP)

    def lanes(c):
        return pl.ds(c * CHUNK, CHUNK)

    own_block = jnp.where(last, x + 1, 0)
    load_own = pltpu.make_async_copy(grad_ref.at[:, :, block(own_block), :], own, load.at[0])
    load_rise = pltpu.make_async_copy(grad_ref.at[:, :, block(4), :], rise, load.at[1])
    load_own.start()
    load_rise.start()
    pl.semaphore_wait(barrier, len(peers))

    def remote(src, dst, send, recv, peer):
        return pltpu.make_async_remote_copy(
            src_ref=src, dst_ref=dst, send_sem=send, recv_sem=recv, device_id=peer, device_id_type=MESH
        )

    def eighth(number):
        return pl.ds(pl.multiple_of(number * 64, 64), 64)

    stage_a = []
    for k in range(1, OWNERS):
        there = lax.rem(me + k, OWNERS)
        stage_a.append(
            remote(part_ref.at[eighth(there)], near.at[k], send_a.at[k], recv_a.at[k], obj_peer(k))
        )
    for copy in stage_a:
        copy.start()

    stage_x = {}
    for c in range(CHUNKS):
        for k in range(1, NX):
            there = lax.rem(x + k, NX)
            number = jnp.where(last, there + 1, k)
            stage_x[c, k] = remote(
                grad_ref.at[:, lanes(c), block(number), :],
                got_x.at[k - 1, :, lanes(c)],
                send_x.at[k - 1, c],
                recv_x.at[k - 1, c],
                x_peer(k),
            )
            stage_x[c, k].start()

    for copy in stage_a:
        copy.wait()
    total = part_ref[eighth(me), :]
    for k in range(1, OWNERS):
        total = total + near[k]
    near[0] = total

    def sixteen(number):
        return pl.ds(pl.multiple_of(number * 16, 16), 16)

    stage_b = []
    for k in range(1, NX):
        there = lax.rem(x + k, NX)
        stage_b.append(
            remote(near.at[0, sixteen(there), :], quarter.at[k], send_b.at[k], recv_b.at[k], x_peer(k))
        )
    for copy in stage_b:
        copy.start()
    for copy in stage_b:
        copy.wait()
    total = near[0, sixteen(x), :]
    for k in range(1, NX):
        total = total + quarter[k]
    sixteenth[y] = total
    stage_c = []
    for k in range(1, NY):
        stage_c.append(
            remote(sixteenth.at[y], sixteenth.at[y], send_c.at[k], recv_c.at[k], y_peer(k))
        )
    for copy in stage_c:
        copy.start()
    for copy in stage_c:
        copy.wait()
    total = (sixteenth[0] + sixteenth[1]) + (sixteenth[2] + sixteenth[3])
    mine = pl.ds(pl.multiple_of(me * 64 + x * 16, 16), 16)
    probe_ref[mine, :] = total * (1.0 / math.sqrt(1024.0))
    stage_d = []
    for k in range(1, NX):
        stage_d.append(
            remote(probe_ref.at[mine], probe_ref.at[mine], send_d.at[k], recv_d.at[k], x_peer(k))
        )
    for copy in stage_d:
        copy.start()
    for copy in stage_d:
        copy.wait()
    stage_e = []
    for k in range(1, OWNERS):
        stage_e.append(
            remote(
                probe_ref.at[eighth(me)], probe_ref.at[eighth(me)], send_e.at[k], recv_e.at[k], obj_peer(k)
            )
        )
    for copy in stage_e:
        copy.start()

    load_own.wait()
    load_rise.wait()
    stage_y = []
    for c in range(CHUNKS):
        for k in range(1, NX):
            stage_x[c, k].wait()
        mine_too = own[:, lanes(c)]
        above_too = rise[:, lanes(c)]
        for k in range(1, NX):
            arrived = got_x[k - 1, :, lanes(c)]
            here = (k <= x) | last
            mine_too = mine_too + jnp.where(here, arrived, 0.0)
            above_too = above_too + jnp.where(here, 0.0, arrived)
        own[:, lanes(c)] = mine_too
        rise[:, lanes(c)] = above_too
        copy = remote(
            rise.at[:, lanes(c)], got_y.at[:, lanes(c)], send_y.at[c], recv_y.at[c], y_peer(1)
        )
        stage_y.append(copy)

        @pl.when(y < NY - 1)
        def _():
            copy.start()

    for c in range(CHUNKS):

        @pl.when(y > 0)
        def _():
            stage_y[c].wait_recv()
            for n in range(c * CHUNK, (c + 1) * CHUNK):
                out_ref[:, :, pl.ds(n * HALF, HALF)] = own[:, n] + got_y[:, n]

        @pl.when(y == 0)
        def _():
            for n in range(c * CHUNK, (c + 1) * CHUNK):
                out_ref[:, :, pl.ds(n * HALF, HALF)] = own[:, n]

    @pl.when(y < NY - 1)
    def _():
        for copy in stage_y:
            copy.wait_send()

    for copy in stage_e:
        copy.wait()


def combine(gradient, probe_part):
    dma = pltpu.SemaphoreType.DMA
    return pl.pallas_call(
        combine_kernel,
        out_shape=(
            jax.ShapeDtypeStruct((2, STRIP, TILE), F32),
            jax.ShapeDtypeStruct((2 * SIDE, SIDE), F32),
        ),
        in_specs=[ANY, VMEM],
        out_specs=(VMEM, VMEM),
        scratch_shapes=[
            pltpu.VMEM((2, BLOCKS, STRIP, HALF), F32),
            pltpu.VMEM((2, BLOCKS, STRIP, HALF), F32),
            pltpu.VMEM((NX - 1, 2, BLOCKS, STRIP, HALF), F32),
            pltpu.VMEM((2, BLOCKS, STRIP, HALF), F32),
            pltpu.VMEM((OWNERS, 64, SIDE), F32),
            pltpu.VMEM((NX, 16, SIDE), F32),
            pltpu.VMEM((NY, 16, SIDE), F32),
            dma((2,)),
            dma((NX - 1, CHUNKS)),
            dma((NX - 1, CHUNKS)),
            dma((CHUNKS,)),
            dma((CHUNKS,)),
            dma((OWNERS,)),
            dma((OWNERS,)),
            dma((NX,)),
            dma((NX,)),
            dma((NY,)),
            dma((NY,)),
            dma((NX,)),
            dma((NX,)),
            dma((OWNERS,)),
            dma((OWNERS,)),
        ],
        compiler_params=pltpu.CompilerParams(
            collective_id=1, has_side_effects=True, vmem_limit_bytes=32 * 2**20
        ),
        name="combine",
    )(gradient, probe_part.reshape(2 * SIDE, SIDE))


def on_device(object_field, probe, amplitude, tile_owner, row_start, col_start):
    tables = jnp.asarray(dft_tables())
    packed, meta = pack(tile_owner, row_start, col_start, amplitude)
    got, got_meta = exchange(packed, meta)
    gradient, probe_part = update(got_meta, got, object_field, probe, tables)
    object_grad, probe_grad = combine(gradient, probe_part)
    return object_grad, probe_grad.reshape(2, SIDE, SIDE)


def solution(mesh):
    return jax.shard_map(
        on_device,
        mesh=mesh,
        in_specs=(
            P(None, None, "obj"),
            P(),
            P(("pat", "obj"), None, None),
            P(("pat", "obj"), None),
            P(("pat", "obj")),
            P(("pat", "obj")),
        ),
        out_specs=(P(None, "pat", "obj"), P()),
        check_vma=False,
    )
```

```python
import math

import jax
import jax.numpy as jnp
import numpy as np
from jax import lax
from jax.experimental import pallas as pl
from jax.experimental.pallas import tpu as pltpu
from jax.sharding import PartitionSpec as P

MESH = pl.DeviceIdType.MESH
CAP = 2
SIDE = 256
HALF = 128
STRIP = 64
SPAN = 320
TILE = 2048
BLOCKS = TILE // HALF
SOFTEN = 0.25
OWNERS = 8
COUNT = 8
SLOTS = OWNERS * CAP
NX = 4
NY = 4
CHUNKS = 8
CHUNK = BLOCKS // CHUNKS
F32 = jnp.float32
BF16 = jnp.bfloat16
ANY = pl.BlockSpec(memory_space=pl.ANY)
VMEM = pl.BlockSpec(memory_space=pltpu.VMEM)
SMEM = pl.BlockSpec(memory_space=pltpu.SMEM)


def dft_tables():
    index = np.arange(SIDE)
    full = np.exp(-2j * np.pi * (np.outer(index, index) % SIDE) / SIDE) / math.sqrt(SIDE)

    def right(table):
        return np.block([[table.real, table.imag], [-table.imag, table.real]])

    swap = np.roll(np.arange(HALF), -HALF // 2)
    half = [full[:HALF, 0::2], full[:HALF, 1::2]]
    lane = [half[0], half[1][:, swap]]
    tables = [
        right(lane[0]),
        right(lane[1]),
        right(half[0]).T,
        right(half[1]).T,
        right(half[0].conj().T).T,
        right(half[1].conj().T).T,
        right(lane[0].conj().T),
        right(lane[1].conj().T),
    ]
    exact = np.stack(tables).astype(np.float32)
    high = exact.astype(BF16)
    low = (exact - high.astype(np.float32)).astype(BF16)
    return np.stack([high, low], axis=1)


def split(value):
    high = value.astype(BF16)
    return high, (value - high.astype(F32)).astype(BF16)


def times_table(data, table):
    high, low = split(data)
    left = jnp.concatenate([high, low, high], axis=1)
    right = jnp.concatenate([table[0], table[0], table[1]], axis=0)
    return jnp.dot(left, right, preferred_element_type=F32)


def table_times(table, data):
    high, low = split(data)
    left = jnp.concatenate([table[0], table[0], table[1]], axis=1)
    right = jnp.concatenate([high, low, high], axis=0)
    return jnp.dot(left, right, preferred_element_type=F32)


def beside(*parts):
    return jnp.concatenate(parts, axis=1)


def above(*parts):
    return jnp.concatenate(parts, axis=0)


def by_parity(rows):
    lane = lax.broadcasted_iota(jnp.int32, (HALF, HALF), 1)
    front = lane < HALF // 2
    first = jnp.take_along_axis(
        rows[:, :HALF], jnp.where(front, 2 * lane, 2 * lane - HALF + 1), axis=1, mode="promise_in_bounds"
    )
    second = jnp.take_along_axis(
        rows[:, HALF:], jnp.where(front, 2 * lane + 1, 2 * lane - HALF), axis=1, mode="promise_in_bounds"
    )
    return beside(jnp.where(front, first, second), jnp.where(front, second, first))


FRONT = slice(0, HALF)
BACK = slice(HALF, SIDE)


def residual_waves(exits, wanted_rows, tables):
    count = len(exits)

    def from_right(waves, number):
        out = times_table(above(*waves), tables(number))
        return [out[SIDE * j : SIDE * (j + 1)] for j in range(count)]

    def from_left(number, waves):
        out = table_times(tables(number), beside(*waves))
        return [out[:, SIDE * j : SIDE * (j + 1)] for j in range(count)]

    even = from_right(
        [beside(re[:, FRONT] + re[:, BACK], im[:, FRONT] + im[:, BACK]) for re, im in exits], 0
    )
    odd = from_right(
        [beside(re[:, FRONT] - re[:, BACK], im[:, FRONT] - im[:, BACK]) for re, im in exits], 1
    )
    half_re = [beside(e[:, FRONT], o[:, FRONT]) for e, o in zip(even, odd)]
    half_im = [beside(e[:, BACK], o[:, BACK]) for e, o in zip(even, odd)]
    pairs = list(zip(half_re, half_im))
    spectrum = [
        from_left(2, [above(re[FRONT] + re[BACK], im[FRONT] + im[BACK]) for re, im in pairs]),
        from_left(3, [above(re[FRONT] - re[BACK], im[FRONT] - im[BACK]) for re, im in pairs]),
    ]
    returned = []
    for parity in range(2):
        scaled = []
        for j in range(count):
            re, im = spectrum[parity][j][FRONT], spectrum[parity][j][BACK]
            ratio = wanted_rows(j, parity) * lax.rsqrt(re * re + im * im + SOFTEN)
            scaled.append(above(re * ratio, im * ratio))
        returned.append(from_left(4 + parity, scaled))
    pairs = []
    for e, o in zip(*returned):
        re = above(e[FRONT] + o[FRONT], e[FRONT] - o[FRONT])
        im = above(e[BACK] + o[BACK], e[BACK] - o[BACK])
        pairs.append((re, im))
    even = from_right([beside(re[:, FRONT], im[:, FRONT]) for re, im in pairs], 6)
    odd = from_right([beside(re[:, BACK], im[:, BACK]) for re, im in pairs], 7)
    residuals = []
    for (re, im), e, o in zip(exits, even, odd):
        back_re = beside(e[:, FRONT] + o[:, FRONT], e[:, FRONT] - o[:, FRONT])
        back_im = beside(e[:, BACK] + o[:, BACK], e[:, BACK] - o[:, BACK])
        residuals.append((back_re - re, back_im - im))
    return residuals


def pack_kernel(owner_ref, row_ref, col_ref, amp_ref, packed_ref, meta_ref, held, come, leave):
    def arriving(j, side):
        return pltpu.make_async_copy(
            amp_ref.at[j, :, pl.ds(side * HALF, HALF)], held.at[j, side], come.at[j, side]
        )

    for j in range(COUNT):
        for side in range(2):
            arriving(j, side).start()
    ranks = []
    for j in range(COUNT):
        rank = jnp.int32(0)
        for i in range(j):
            rank = rank + (owner_ref[i, 0] == owner_ref[j, 0]).astype(jnp.int32)
        ranks.append(rank)
    leaving = []
    for j in range(COUNT):
        for side in range(2):
            arriving(j, side).wait()
        copy = pltpu.make_async_copy(held.at[j], packed_ref.at[owner_ref[j, 0], ranks[j]], leave.at[j])
        copy.start()
        leaving.append(copy)
    meta_ref[...] = jnp.zeros_like(meta_ref)
    sub = lax.broadcasted_iota(jnp.int32, (8, 128), 0)
    for j in range(COUNT):
        mine = (sub // 4 == ranks[j]) & (sub % 4 < 3)
        value = jnp.where(sub % 4 == 0, 1, jnp.where(sub % 4 == 1, row_ref[j], col_ref[j]))
        meta_ref[owner_ref[j, 0]] = jnp.where(mine, value, meta_ref[owner_ref[j, 0]])
    for copy in leaving:
        copy.wait()


def pack(tile_owner, row_start, col_start, amplitude):
    return pl.pallas_call(
        pack_kernel,
        out_shape=(
            jax.ShapeDtypeStruct((OWNERS, CAP, 2, SIDE, HALF), F32),
            jax.ShapeDtypeStruct((OWNERS, 8, 128), jnp.int32),
        ),
        in_specs=[SMEM, SMEM, SMEM, ANY],
        out_specs=(ANY, VMEM),
        scratch_shapes=[
            pltpu.VMEM((COUNT, 2, SIDE, HALF), F32),
            pltpu.SemaphoreType.DMA((COUNT, 2)),
            pltpu.SemaphoreType.DMA((COUNT,)),
        ],
        name="pack",
    )(tile_owner, row_start, col_start, amplitude)


def step_kernel(
    packed_ref, meta_ref, object_ref, probe_ref, tables_ref, out_ref, total_ref,
    got, got_meta, corners, strip, tables, pads, part, grad, got_x, got_y, own, rise, near, quarter, sixteenth,
    load, send, recv, send_meta, recv_meta, send_x, recv_x, send_y, recv_y,
    send_a, recv_a, send_b, recv_b, send_c, recv_c, send_d, recv_d, send_e, recv_e,
):
    me = lax.axis_index("obj")
    z = me // 2
    core = lax.rem(me, 2)
    group = lax.axis_index("pat")
    x = lax.rem(group, NX)
    y = group // NX
    last = y == NY - 1
    base = pl.multiple_of(jnp.minimum(group, 11) * STRIP, STRIP)

    def obj_at(r):
        return lax.rem(z + r // 2, OWNERS // 2) * 2 + lax.rem(core + lax.rem(r, 2), 2)

    def obj_peer(r):
        return {"obj": obj_at(r)}

    def x_peer(k):
        return {"pat": y * NX + lax.rem(x + k, NX)}

    def y_peer(k):
        return {"pat": lax.rem(y + k, NY) * NX + x}

    def remote(src, dst, send, recv, peer):
        return pltpu.make_async_remote_copy(
            src_ref=src, dst_ref=dst, send_sem=send, recv_sem=recv, device_id=peer, device_id_type=MESH
        )

    peers = [obj_peer(r) for r in range(1, OWNERS)]
    peers += [x_peer(k) for k in range(1, NX)] + [y_peer(k) for k in range(1, NY)]
    barrier = pltpu.get_barrier_semaphore()
    for peer in peers:
        pl.semaphore_signal(barrier, inc=1, device_id=peer, device_id_type=MESH)

    loads = [
        pltpu.make_async_copy(
            object_ref.at[:, pl.ds(base, SPAN), pl.ds(n * HALF, HALF)], strip.at[:, n], load.at[n]
        )
        for n in range(BLOCKS)
    ]
    loads.append(pltpu.make_async_copy(tables_ref, tables, load.at[BLOCKS]))
    load_meta = pltpu.make_async_copy(meta_ref.at[me], got_meta.at[0], load.at[BLOCKS + 1])
    load_own = pltpu.make_async_copy(packed_ref.at[me], got.at[0], load.at[BLOCKS + 2])

    def metas(r):
        return remote(meta_ref.at[obj_at(r)], got_meta.at[r], send_meta.at[r], recv_meta.at[r], obj_peer(r))

    def amplitudes(r):
        return remote(packed_ref.at[obj_at(r)], got.at[r], send.at[r], recv.at[r], obj_peer(r))

    load_meta.start()
    pl.semaphore_wait(barrier, len(peers))
    for r in range(1, OWNERS):
        metas(r).start()
    amplitudes(1).start()
    for dz in (1, 3, 2):
        amplitudes(2 * dz + core).start()
    load_own.start()
    for copy in loads:
        copy.start()
    edge = jnp.zeros((2, STRIP, HALF), F32)
    for n in range(3 * SLOTS):
        pads[n, :, pl.ds(0, STRIP), :] = edge
        pads[n, :, pl.ds(STRIP + SIDE, STRIP), :] = edge
    pads[3 * SLOTS] = jnp.zeros((2, SPAN + STRIP, HALF), F32)
    part[...] = jnp.zeros_like(part)
    load_meta.wait()
    for r in range(1, OWNERS):
        metas(r).wait_recv()
    load_corners = pltpu.make_async_copy(got_meta, corners, load.at[BLOCKS + 3])
    load_corners.start()
    load_corners.wait()
    for copy in loads:
        copy.wait()
    load_own.wait()

    lane = lax.broadcasted_iota(jnp.int32, (SIDE, HALF), 1)

    def corner(slot):
        r = slot // CAP
        at = 4 * lax.rem(slot, CAP)
        row = jnp.clip(corners[r, at + 1, 0] - base, 0, STRIP)
        col = jnp.clip(corners[r, at + 2, 0], 0, TILE - SIDE)
        start = jnp.minimum(col // HALF, BLOCKS - 3)
        return row, start, col - start * HALF

    def window(slot, part):
        row, start, shift = corner(slot)
        unshift = lax.rem(HALF - shift, HALF)
        turned = [
            pltpu.roll(strip[part, start + n, pl.ds(row, SIDE), :], unshift, axis=1) for n in range(3)
        ]
        inner = lane < HALF - shift
        return beside(jnp.where(inner, turned[0], turned[1]), jnp.where(inner, turned[1], turned[2]))

    def from_source(k, carry):
        r = jnp.where(k < 4, k, jnp.where(k < 6, k + 2, k - 2))

        @pl.when(k == jnp.where(core == 0, 6, 2))
        def _():
            for dz in (1, 3, 2):
                amplitudes(2 * dz + core).wait_send()
            for dz in (1, 3, 2):
                amplitudes(2 * dz + 1 - core).start()

        @pl.when(k > 0)
        def _():
            amplitudes(r).wait_recv()

        slots = [CAP * r + n for n in range(CAP)]
        probe_re = probe_ref[0]
        probe_im = probe_ref[1]
        windows = [(window(slot, 0), window(slot, 1)) for slot in slots]
        exits = [
            (probe_re * re - probe_im * im, probe_re * im + probe_im * re) for re, im in windows
        ]

        def wanted_rows(j, parity):
            return by_parity(
                beside(
                    got[r, j, 0, pl.ds(parity, HALF, stride=2), :],
                    got[r, j, 1, pl.ds(parity, HALF, stride=2), :],
                )
            )

        residuals = residual_waves(exits, wanted_rows, lambda i: (tables[i, 0], tables[i, 1]))
        part_re = part[pl.ds(0, SIDE), :]
        part_im = part[pl.ds(SIDE, SIDE), :]
        for j, slot in enumerate(slots):
            keep = corners[r, 4 * j, 0] > 0
            res_re = jnp.where(keep, residuals[j][0], 0.0)
            res_im = jnp.where(keep, residuals[j][1], 0.0)
            window_re, window_im = windows[j]
            part_re = part_re + (window_re * res_re + window_im * res_im)
            part_im = part_im + (window_re * res_im - window_im * res_re)
            shift = corner(slot)[2]
            turn = lax.rem(shift, HALF)
            outer = lane >= shift
            rows = pl.ds(STRIP, SIDE)
            for c, value in (
                (0, probe_re * res_re + probe_im * res_im),
                (1, probe_re * res_im - probe_im * res_re),
            ):
                first = pltpu.roll(value[:, FRONT], turn, axis=1)
                second = pltpu.roll(value[:, BACK], turn, axis=1)
                pads[3 * slot, c, rows, :] = jnp.where(outer, first, 0.0)
                pads[3 * slot + 1, c, rows, :] = jnp.where(outer, second, first)
                pads[3 * slot + 2, c, rows, :] = jnp.where(outer, 0.0, second)
        part[pl.ds(0, SIDE), :] = part_re
        part[pl.ds(SIDE, SIDE), :] = part_im
        return carry

    lax.fori_loop(0, OWNERS, from_source, 0)

    def eighth(number):
        return pl.ds(pl.multiple_of(number * 64, 64), 64)

    def sixteen(number):
        return pl.ds(pl.multiple_of(number * 16, 16), 16)

    mine = pl.ds(pl.multiple_of(me * 64 + y * 16, 16), 16)

    def stage_a(r):
        return remote(part.at[eighth(obj_at(r))], near.at[r], send_a.at[r], recv_a.at[r], obj_peer(r))

    def stage_b(k):
        there = lax.rem(y + k, NY)
        return remote(near.at[0, sixteen(there)], quarter.at[k], send_b.at[k], recv_b.at[k], y_peer(k))

    def stage_c(k):
        return remote(sixteenth.at[x], sixteenth.at[x], send_c.at[k], recv_c.at[k], x_peer(k))

    def stage_d(k):
        return remote(total_ref.at[mine], total_ref.at[mine], send_d.at[k], recv_d.at[k], y_peer(k))

    def stage_e(r):
        return remote(
            total_ref.at[eighth(me)], total_ref.at[eighth(me)], send_e.at[r], recv_e.at[r], obj_peer(r)
        )

    def probe_step(number):
        if number == 0:
            for r in range(1, OWNERS):
                stage_a(r).wait()
            value = part[eighth(me), :]
            for r in range(1, OWNERS):
                value = value + near[r]
            near[0] = value
            for k in range(1, NY):
                stage_b(k).start()
        elif number == 1:
            for k in range(1, NY):
                stage_b(k).wait()
            value = near[0, sixteen(y), :]
            for k in range(1, NY):
                value = value + quarter[k]
            sixteenth[x] = value
            for k in range(1, NX):
                stage_c(k).start()
        elif number == 2:
            for k in range(1, NX):
                stage_c(k).wait()
            value = (sixteenth[0] + sixteenth[1]) + (sixteenth[2] + sixteenth[3])
            total_ref[mine, :] = value * (1.0 / math.sqrt(1024.0))
            for k in range(1, NY):
                stage_d(k).start()
        elif number == 3:
            for k in range(1, NY):
                stage_d(k).wait()
            for r in range(1, OWNERS):
                stage_e(r).start()
        else:
            for r in range(1, OWNERS):
                stage_e(r).wait()

    for r in range(1, OWNERS):
        stage_a(r).start()

    def block(number):
        return pl.ds(pl.multiple_of(number * STRIP, STRIP), STRIP)

    def along_x(c, k):
        number = jnp.where(last, lax.rem(x + k, NX) + 1, k)
        columns = pl.ds(c * CHUNK, CHUNK)
        return remote(
            grad.at[:, columns, block(number)],
            got_x.at[k - 1, :, columns],
            send_x.at[k - 1, c],
            recv_x.at[k - 1, c],
            x_peer(k),
        )

    def along_y(c):
        columns = pl.ds(c * CHUNK, CHUNK)
        return remote(rise.at[:, columns], got_y.at[:, columns], send_y.at[c], recv_y.at[c], y_peer(1))

    def gather_chunk(c, carry):
        def gather_block(b, carry):
            for part in range(2):
                value = None
                for slot in range(SLOTS):
                    row, start, _ = corner(slot)
                    n = b - start
                    at = jnp.where((n >= 0) & (n < 3), 3 * slot + n, 3 * SLOTS)
                    term = pads[at, part, pl.ds(STRIP - row, SPAN), :]
                    value = term if value is None else value + term
                grad[part, b] = value
            return carry

        lax.fori_loop(c * CHUNK, (c + 1) * CHUNK, gather_block, 0)
        for k in range(1, NX):
            along_x(c, k).start()
        return carry

    lax.fori_loop(0, CHUNKS, gather_chunk, 0)

    own_block = block(jnp.where(last, x + 1, 0))
    for c in range(CHUNKS):
        columns = pl.ds(c * CHUNK, CHUNK)
        for k in range(1, NX):
            along_x(c, k).wait_recv()
        here_too = grad[:, columns, own_block, :]
        above_too = grad[:, columns, block(4), :]
        for k in range(1, NX):
            arrived = got_x[k - 1, :, columns]
            here = (k <= x) | last
            here_too = here_too + jnp.where(here, arrived, 0.0)
            above_too = above_too + jnp.where(here, 0.0, arrived)
        own[:, columns] = here_too
        rise[:, columns] = above_too

        @pl.when(y < NY - 1)
        def _():
            along_y(c).start()

        if c in (1, 3, 5, 6):

            @pl.when(core == 1)
            def _():
                probe_step((1, 3, 5, 6).index(c))

    for c in range(CHUNKS):

        @pl.when(y > 0)
        def _():
            along_y(c).wait_recv()
            for n in range(c * CHUNK, (c + 1) * CHUNK):
                out_ref[:, :, pl.ds(n * HALF, HALF)] = own[:, n] + got_y[:, n]

        @pl.when(y == 0)
        def _():
            for n in range(c * CHUNK, (c + 1) * CHUNK):
                out_ref[:, :, pl.ds(n * HALF, HALF)] = own[:, n]

        @pl.when(y < NY - 1)
        def _():
            along_y(c).wait_send()

    @pl.when(core == 0)
    def _():
        for number in range(4):
            probe_step(number)

    for r in range(1, OWNERS):
        metas(r).wait_send()
    amplitudes(1).wait_send()
    for dz in (1, 3, 2):
        amplitudes(2 * dz + 1 - core).wait_send()
    for c in range(CHUNKS):
        for k in range(1, NX):
            along_x(c, k).wait_send()
    probe_step(4)


def step(packed, meta, object_field, probe, tables):
    dma = pltpu.SemaphoreType.DMA
    return pl.pallas_call(
        step_kernel,
        out_shape=(
            jax.ShapeDtypeStruct((2, STRIP, TILE), F32),
            jax.ShapeDtypeStruct((2 * SIDE, SIDE), F32),
        ),
        in_specs=[ANY, VMEM, ANY, VMEM, ANY],
        out_specs=(VMEM, VMEM),
        scratch_shapes=[
            pltpu.VMEM((OWNERS, CAP, 2, SIDE, HALF), F32),
            pltpu.VMEM((OWNERS, 8, 128), jnp.int32),
            pltpu.SMEM((OWNERS, 8, 128), jnp.int32),
            pltpu.VMEM((2, BLOCKS, SPAN, HALF), F32),
            pltpu.VMEM(tables.shape, BF16),
            pltpu.VMEM((3 * SLOTS + 1, 2, SPAN + STRIP, HALF), F32),
            pltpu.VMEM((2 * SIDE, SIDE), F32),
            pltpu.VMEM((2, BLOCKS, SPAN, HALF), F32),
            pltpu.VMEM((NX - 1, 2, BLOCKS, STRIP, HALF), F32),
            pltpu.VMEM((2, BLOCKS, STRIP, HALF), F32),
            pltpu.VMEM((2, BLOCKS, STRIP, HALF), F32),
            pltpu.VMEM((2, BLOCKS, STRIP, HALF), F32),
            pltpu.VMEM((OWNERS, 64, SIDE), F32),
            pltpu.VMEM((NY, 16, SIDE), F32),
            pltpu.VMEM((NX, 16, SIDE), F32),
            dma((BLOCKS + 4,)),
            dma((OWNERS,)),
            dma((OWNERS,)),
            dma((OWNERS,)),
            dma((OWNERS,)),
            dma((NX - 1, CHUNKS)),
            dma((NX - 1, CHUNKS)),
            dma((CHUNKS,)),
            dma((CHUNKS,)),
            dma((OWNERS,)),
            dma((OWNERS,)),
            dma((NY,)),
            dma((NY,)),
            dma((NX,)),
            dma((NX,)),
            dma((NY,)),
            dma((NY,)),
            dma((OWNERS,)),
            dma((OWNERS,)),
        ],
        compiler_params=pltpu.CompilerParams(
            collective_id=0, has_side_effects=True, vmem_limit_bytes=56 * 2**20
        ),
        name="step",
    )(packed, meta, object_field, probe, tables)


def on_device(object_field, probe, amplitude, tile_owner, row_start, col_start):
    tables = jnp.asarray(dft_tables())
    packed, meta = pack(tile_owner, row_start, col_start, amplitude)
    object_grad, probe_grad = step(packed, meta, object_field, probe, tables)
    return object_grad, probe_grad.reshape(2, SIDE, SIDE)


def solution(mesh):
    return jax.shard_map(
        on_device,
        mesh=mesh,
        in_specs=(
            P(None, None, "obj"),
            P(),
            P(("pat", "obj"), None, None),
            P(("pat", "obj"), None),
            P(("pat", "obj")),
            P(("pat", "obj")),
        ),
        out_specs=(P(None, "pat", "obj"), P()),
        check_vma=False,
    )
```

```python
import math

import jax
import jax.numpy as jnp
import numpy as np
from jax import lax
from jax.experimental import pallas as pl
from jax.experimental.pallas import tpu as pltpu
from jax.sharding import PartitionSpec as P

MESH = pl.DeviceIdType.MESH
CAP = 2
SIDE = 256
HALF = 128
STRIP = 64
SPAN = 320
TILE = 2048
BLOCKS = TILE // HALF
SOFTEN = 0.25
OWNERS = 8
COUNT = 8
SLOTS = OWNERS * CAP
NX = 4
NY = 4
CHUNKS = 8
CHUNK = BLOCKS // CHUNKS
F32 = jnp.float32
BF16 = jnp.bfloat16
HBM = pl.BlockSpec(memory_space=pltpu.HBM)
VMEM = pl.BlockSpec(memory_space=pltpu.VMEM)
SMEM = pl.BlockSpec(memory_space=pltpu.SMEM)


def dft_tables():
    index = np.arange(SIDE)
    full = np.exp(-2j * np.pi * (np.outer(index, index) % SIDE) / SIDE) / math.sqrt(SIDE)

    def right(table):
        return np.block([[table.real, table.imag], [-table.imag, table.real]])

    swap = np.roll(np.arange(HALF), -HALF // 2)
    half = [full[:HALF, 0::2], full[:HALF, 1::2]]
    lane = [half[0], half[1][:, swap]]
    tables = [
        right(lane[0]),
        right(lane[1]),
        right(half[0]).T,
        right(half[1]).T,
        right(half[0].conj().T).T,
        right(half[1].conj().T).T,
        right(lane[0].conj().T),
        right(lane[1].conj().T),
    ]
    exact = np.stack(tables).astype(np.float32)
    high = exact.astype(BF16)
    low = (exact - high.astype(np.float32)).astype(BF16)
    return np.stack([high, low], axis=1)


def split(value):
    high = value.astype(BF16)
    return high, (value - high.astype(F32)).astype(BF16)


def times_table(data, table):
    high, low = split(data)
    left = jnp.concatenate([high, low, high], axis=1)
    right = jnp.concatenate([table[0], table[0], table[1]], axis=0)
    return jnp.dot(left, right, preferred_element_type=F32)


def table_times(table, data):
    high, low = split(data)
    left = jnp.concatenate([table[0], table[0], table[1]], axis=1)
    right = jnp.concatenate([high, low, high], axis=0)
    return jnp.dot(left, right, preferred_element_type=F32)


def beside(*parts):
    return jnp.concatenate(parts, axis=1)


def above(*parts):
    return jnp.concatenate(parts, axis=0)


def by_parity(rows):
    lane = lax.broadcasted_iota(jnp.int32, (HALF, HALF), 1)
    front = lane < HALF // 2
    first = jnp.take_along_axis(
        rows[:, :HALF], jnp.where(front, 2 * lane, 2 * lane - HALF + 1), axis=1, mode="promise_in_bounds"
    )
    second = jnp.take_along_axis(
        rows[:, HALF:], jnp.where(front, 2 * lane + 1, 2 * lane - HALF), axis=1, mode="promise_in_bounds"
    )
    return beside(jnp.where(front, first, second), jnp.where(front, second, first))


FRONT = slice(0, HALF)
BACK = slice(HALF, SIDE)


def residual_waves(exits, wanted_rows, tables):
    count = len(exits)

    def from_right(waves, number):
        out = times_table(above(*waves), tables(number))
        return [out[SIDE * j : SIDE * (j + 1)] for j in range(count)]

    def from_left(number, waves):
        out = table_times(tables(number), beside(*waves))
        return [out[:, SIDE * j : SIDE * (j + 1)] for j in range(count)]

    even = from_right(
        [beside(re[:, FRONT] + re[:, BACK], im[:, FRONT] + im[:, BACK]) for re, im in exits], 0
    )
    odd = from_right(
        [beside(re[:, FRONT] - re[:, BACK], im[:, FRONT] - im[:, BACK]) for re, im in exits], 1
    )
    half_re = [beside(e[:, FRONT], o[:, FRONT]) for e, o in zip(even, odd)]
    half_im = [beside(e[:, BACK], o[:, BACK]) for e, o in zip(even, odd)]
    pairs = list(zip(half_re, half_im))
    spectrum = [
        from_left(2, [above(re[FRONT] + re[BACK], im[FRONT] + im[BACK]) for re, im in pairs]),
        from_left(3, [above(re[FRONT] - re[BACK], im[FRONT] - im[BACK]) for re, im in pairs]),
    ]
    returned = []
    for parity in range(2):
        scaled = []
        for j in range(count):
            re, im = spectrum[parity][j][FRONT], spectrum[parity][j][BACK]
            ratio = wanted_rows(j, parity) * lax.rsqrt(re * re + im * im + SOFTEN)
            scaled.append(above(re * ratio, im * ratio))
        returned.append(from_left(4 + parity, scaled))
    pairs = []
    for e, o in zip(*returned):
        re = above(e[FRONT] + o[FRONT], e[FRONT] - o[FRONT])
        im = above(e[BACK] + o[BACK], e[BACK] - o[BACK])
        pairs.append((re, im))
    even = from_right([beside(re[:, FRONT], im[:, FRONT]) for re, im in pairs], 6)
    odd = from_right([beside(re[:, BACK], im[:, BACK]) for re, im in pairs], 7)
    residuals = []
    for (re, im), e, o in zip(exits, even, odd):
        back_re = beside(e[:, FRONT] + o[:, FRONT], e[:, FRONT] - o[:, FRONT])
        back_im = beside(e[:, BACK] + o[:, BACK], e[:, BACK] - o[:, BACK])
        residuals.append((back_re - re, back_im - im))
    return residuals


def pack_kernel(owner_ref, row_ref, col_ref, amp_ref, packed_ref, meta_ref, held, come, leave):
    def arriving(j, side):
        return pltpu.make_async_copy(
            amp_ref.at[j, :, pl.ds(side * HALF, HALF)], held.at[j, side], come.at[j, side]
        )

    for j in range(COUNT):
        for side in range(2):
            arriving(j, side).start()
    ranks = []
    for j in range(COUNT):
        rank = jnp.int32(0)
        for i in range(j):
            rank = rank + (owner_ref[0, i] == owner_ref[0, j]).astype(jnp.int32)
        ranks.append(rank)
    leaving = []
    for j in range(COUNT):
        for side in range(2):
            arriving(j, side).wait()
        copy = pltpu.make_async_copy(held.at[j], packed_ref.at[owner_ref[0, j], ranks[j]], leave.at[j])
        copy.start()
        leaving.append(copy)
    meta_ref[...] = jnp.zeros_like(meta_ref)
    sub = lax.broadcasted_iota(jnp.int32, (8, 128), 0)
    for j in range(COUNT):
        mine = (sub // 4 == ranks[j]) & (sub % 4 < 3)
        value = jnp.where(sub % 4 == 0, 1, jnp.where(sub % 4 == 1, row_ref[j], col_ref[j]))
        meta_ref[owner_ref[0, j]] = jnp.where(mine, value, meta_ref[owner_ref[0, j]])
    for copy in leaving:
        copy.wait()


def pack(tile_owner, row_start, col_start, amplitude):
    return pl.pallas_call(
        pack_kernel,
        out_shape=(
            jax.ShapeDtypeStruct((OWNERS, CAP, 2, SIDE, HALF), F32),
            jax.ShapeDtypeStruct((OWNERS, 8, 128), jnp.int32),
        ),
        in_specs=[SMEM, SMEM, SMEM, HBM],
        out_specs=(HBM, VMEM),
        scratch_shapes=[
            pltpu.VMEM((COUNT, 2, SIDE, HALF), F32),
            pltpu.SemaphoreType.DMA((COUNT, 2)),
            pltpu.SemaphoreType.DMA((COUNT,)),
        ],
        name="pack",
    )(tile_owner.T, row_start, col_start, amplitude)


def step_kernel(
    packed_ref, meta_ref, object_ref, probe_ref, tables_ref, out_ref, total_ref,
    got, got_meta, corners, strip, tables, pads, part, grad, got_x, got_y, own, rise, near, quarter, sixteenth,
    load, send, recv, send_meta, recv_meta, send_x, recv_x, send_y, recv_y,
    send_a, recv_a, send_b, recv_b, send_c, recv_c, send_d, recv_d, send_e, recv_e,
):
    me = lax.axis_index("obj")
    z = me // 2
    core = lax.rem(me, 2)
    group = lax.axis_index("pat")
    x = lax.rem(group, NX)
    y = group // NX
    last = y == NY - 1
    base = pl.multiple_of(jnp.minimum(group, 11) * STRIP, STRIP)

    def obj_at(r):
        return lax.rem(z + r // 2, OWNERS // 2) * 2 + lax.rem(core + lax.rem(r, 2), 2)

    def obj_peer(r):
        return {"obj": obj_at(r)}

    def x_peer(k):
        return {"pat": y * NX + lax.rem(x + k, NX)}

    def y_peer(k):
        return {"pat": lax.rem(y + k, NY) * NX + x}

    def remote(src, dst, send, recv, peer):
        return pltpu.make_async_remote_copy(
            src_ref=src, dst_ref=dst, send_sem=send, recv_sem=recv, device_id=peer, device_id_type=MESH
        )

    peers = [obj_peer(r) for r in range(1, OWNERS)]
    peers += [x_peer(k) for k in range(1, NX)] + [y_peer(k) for k in range(1, NY)]
    barrier = pltpu.get_barrier_semaphore()
    for peer in peers:
        pl.semaphore_signal(barrier, inc=1, device_id=peer, device_id_type=MESH)

    loads = [
        pltpu.make_async_copy(
            object_ref.at[:, pl.ds(base, SPAN), pl.ds(n * HALF, HALF)], strip.at[:, n], load.at[n]
        )
        for n in range(BLOCKS)
    ]
    loads.append(pltpu.make_async_copy(tables_ref, tables, load.at[BLOCKS]))
    load_meta = pltpu.make_async_copy(meta_ref.at[me], got_meta.at[0], load.at[BLOCKS + 1])
    load_own = pltpu.make_async_copy(packed_ref.at[me], got.at[0], load.at[BLOCKS + 2])

    def metas(r):
        return remote(meta_ref.at[obj_at(r)], got_meta.at[r], send_meta.at[r], recv_meta.at[r], obj_peer(r))

    def amplitudes(slot):
        r = slot // CAP
        n = lax.rem(slot, CAP)
        return remote(
            packed_ref.at[obj_at(r), n], got.at[r, n], send.at[slot], recv.at[slot], obj_peer(r)
        )

    stages = [
        [2 * (2 * dz + side) + n for n in range(CAP) for dz in distances]
        for side in (core, 1 - core)
        for distances in ((1, 3), (2,))
    ]

    def start_stage(number):
        for slot in stages[number]:
            amplitudes(slot).start()

    def end_stage(number):
        for slot in stages[number]:
            amplitudes(slot).wait_send()

    load_meta.start()
    load_own.start()
    for copy in loads:
        copy.start()
    pl.semaphore_wait(barrier, len(peers))
    for r in range(1, OWNERS):
        metas(r).start()
    for slot in (2, 3):
        amplitudes(slot).start()
    start_stage(0)
    edge = jnp.zeros((2, STRIP, HALF), F32)
    for n in range(3 * SLOTS):
        pads[n, :, pl.ds(0, STRIP), :] = edge
        pads[n, :, pl.ds(STRIP + SIDE, STRIP), :] = edge
    pads[3 * SLOTS] = jnp.zeros((2, SPAN + STRIP, HALF), F32)
    part[...] = jnp.zeros_like(part)

    def take_corners(pair):
        if pair:
            metas(2 * pair).wait_recv()
            metas(2 * pair + 1).wait_recv()
        else:
            load_meta.wait()
            metas(1).wait_recv()
        rows = pl.ds(2 * pair, 2)
        copy = pltpu.make_async_copy(got_meta.at[rows], corners.at[rows], load.at[BLOCKS + 3])
        copy.start()
        copy.wait()

    take_corners(0)
    for copy in loads:
        copy.wait()
    load_own.wait()

    lane = lax.broadcasted_iota(jnp.int32, (SIDE, HALF), 1)

    def corner(slot):
        r = slot // CAP
        at = 4 * lax.rem(slot, CAP)
        row = jnp.clip(corners[r, at + 1, 0] - base, 0, STRIP)
        col = jnp.clip(corners[r, at + 2, 0], 0, TILE - SIDE)
        start = jnp.minimum(col // HALF, BLOCKS - 3)
        return row, start, col - start * HALF

    def window(slot, part):
        row, start, shift = corner(slot)
        unshift = lax.rem(HALF - shift, HALF)
        turned = [
            pltpu.roll(strip[part, start + n, pl.ds(row, SIDE), :], unshift, axis=1) for n in range(3)
        ]
        inner = lane < HALF - shift
        return beside(jnp.where(inner, turned[0], turned[1]), jnp.where(inner, turned[1], turned[2]))

    def from_pair(k, carry):
        dz = jnp.where(k >= 6, 2, jnp.where(lax.rem(k, 2) == 0, 1, 3))
        n = jnp.where(k >= 6, k - 6, (k - 2) // 2)
        one = jnp.where(k < 2, 2 * k, 4 * dz + n)
        two = jnp.where(k < 2, 2 * k + 1, 4 * dz + 2 + n)

        for side, turn, number in ((0, 4, 0), (0, 7, 1), (1, 2, 0), (1, 2, 1), (1, 4, 2)):

            @pl.when((core == side) & (k == turn))
            def _():
                end_stage(number)
                start_stage(number + 1)

        for pair, turn in ((1, 2), (3, 3), (2, 6)):

            @pl.when(k == turn)
            def _():
                take_corners(pair)

        @pl.when(k > 0)
        def _():
            amplitudes(one).wait_recv()
            amplitudes(two).wait_recv()

        slots = [one, two]
        probe_re = probe_ref[0]
        probe_im = probe_ref[1]
        windows = [(window(slot, 0), window(slot, 1)) for slot in slots]
        exits = [
            (probe_re * re - probe_im * im, probe_re * im + probe_im * re) for re, im in windows
        ]

        def wanted_rows(j, parity):
            return by_parity(
                beside(
                    got[slots[j] // CAP, lax.rem(slots[j], CAP), 0, pl.ds(parity, HALF, stride=2), :],
                    got[slots[j] // CAP, lax.rem(slots[j], CAP), 1, pl.ds(parity, HALF, stride=2), :],
                )
            )

        residuals = residual_waves(exits, wanted_rows, lambda i: (tables[i, 0], tables[i, 1]))
        part_re = part[pl.ds(0, SIDE), :]
        part_im = part[pl.ds(SIDE, SIDE), :]
        for j, slot in enumerate(slots):
            keep = corners[slot // CAP, 4 * lax.rem(slot, CAP), 0] > 0
            res_re = jnp.where(keep, residuals[j][0], 0.0)
            res_im = jnp.where(keep, residuals[j][1], 0.0)
            window_re, window_im = windows[j]
            part_re = part_re + (window_re * res_re + window_im * res_im)
            part_im = part_im + (window_re * res_im - window_im * res_re)
            shift = corner(slot)[2]
            turn = lax.rem(shift, HALF)
            outer = lane >= shift
            rows = pl.ds(STRIP, SIDE)
            for c, value in (
                (0, probe_re * res_re + probe_im * res_im),
                (1, probe_re * res_im - probe_im * res_re),
            ):
                first = pltpu.roll(value[:, FRONT], turn, axis=1)
                second = pltpu.roll(value[:, BACK], turn, axis=1)
                pads[3 * slot, c, rows, :] = jnp.where(outer, first, 0.0)
                pads[3 * slot + 1, c, rows, :] = jnp.where(outer, second, first)
                pads[3 * slot + 2, c, rows, :] = jnp.where(outer, 0.0, second)
        part[pl.ds(0, SIDE), :] = part_re
        part[pl.ds(SIDE, SIDE), :] = part_im
        return carry

    lax.fori_loop(0, OWNERS, from_pair, 0)

    def eighth(number):
        return pl.ds(pl.multiple_of(number * 64, 64), 64)

    def sixteen(number):
        return pl.ds(pl.multiple_of(number * 16, 16), 16)

    mine = pl.ds(pl.multiple_of(me * 64 + y * 16, 16), 16)

    def stage_a(r):
        return remote(part.at[eighth(obj_at(r))], near.at[r], send_a.at[r], recv_a.at[r], obj_peer(r))

    def stage_b(k):
        there = lax.rem(y + k, NY)
        return remote(near.at[0, sixteen(there)], quarter.at[k], send_b.at[k], recv_b.at[k], y_peer(k))

    def stage_c(k):
        return remote(sixteenth.at[x], sixteenth.at[x], send_c.at[k], recv_c.at[k], x_peer(k))

    def stage_d(k):
        return remote(total_ref.at[mine], total_ref.at[mine], send_d.at[k], recv_d.at[k], y_peer(k))

    def stage_e(r):
        return remote(
            total_ref.at[eighth(me)], total_ref.at[eighth(me)], send_e.at[r], recv_e.at[r], obj_peer(r)
        )

    def probe_step(number):
        if number == 0:
            for r in range(1, OWNERS):
                stage_a(r).wait()
            value = part[eighth(me), :]
            for r in range(1, OWNERS):
                value = value + near[r]
            near[0] = value
            for k in range(1, NY):
                stage_b(k).start()
        elif number == 1:
            for k in range(1, NY):
                stage_b(k).wait()
            value = near[0, sixteen(y), :]
            for k in range(1, NY):
                value = value + quarter[k]
            sixteenth[x] = value
            for k in range(1, NX):
                stage_c(k).start()
        elif number == 2:
            for k in range(1, NX):
                stage_c(k).wait()
            value = (sixteenth[0] + sixteenth[1]) + (sixteenth[2] + sixteenth[3])
            total_ref[mine, :] = value * (1.0 / math.sqrt(1024.0))
            for k in range(1, NY):
                stage_d(k).start()
        elif number == 3:
            for k in range(1, NY):
                stage_d(k).wait()
            for r in range(1, OWNERS):
                stage_e(r).start()
        else:
            for r in range(1, OWNERS):
                stage_e(r).wait()

    for r in range(1, OWNERS):
        stage_a(r).start()

    def block(number):
        return pl.ds(pl.multiple_of(number * STRIP, STRIP), STRIP)

    def along_x(c, k):
        number = jnp.where(last, lax.rem(x + k, NX) + 1, k)
        columns = pl.ds(c * CHUNK, CHUNK)
        return remote(
            grad.at[:, columns, block(number)],
            got_x.at[k - 1, :, columns],
            send_x.at[k - 1, c],
            recv_x.at[k - 1, c],
            x_peer(k),
        )

    def along_y(c):
        columns = pl.ds(c * CHUNK, CHUNK)
        return remote(rise.at[:, columns], got_y.at[:, columns], send_y.at[c], recv_y.at[c], y_peer(1))

    def gather_chunk(c, carry):
        def gather_block(b, carry):
            for part in range(2):
                value = None
                for slot in range(SLOTS):
                    row, start, _ = corner(slot)
                    n = b - start
                    at = jnp.where((n >= 0) & (n < 3), 3 * slot + n, 3 * SLOTS)
                    term = pads[at, part, pl.ds(STRIP - row, SPAN), :]
                    value = term if value is None else value + term
                grad[part, b] = value
            return carry

        lax.fori_loop(c * CHUNK, (c + 1) * CHUNK, gather_block, 0)
        for k in range(1, NX):
            along_x(c, k).start()
        return carry

    lax.fori_loop(0, CHUNKS // 2, gather_chunk, 0)

    @pl.when(core == 1)
    def _():
        probe_step(0)
        probe_step(1)

    lax.fori_loop(CHUNKS // 2, CHUNKS, gather_chunk, 0)

    @pl.when(core == 0)
    def _():
        end_stage(2)
        start_stage(3)

    own_block = block(jnp.where(last, x + 1, 0))
    for c in range(CHUNKS):
        columns = pl.ds(c * CHUNK, CHUNK)
        for k in range(1, NX):
            along_x(c, k).wait_recv()
        here_too = grad[:, columns, own_block, :]
        above_too = grad[:, columns, block(4), :]
        for k in range(1, NX):
            arrived = got_x[k - 1, :, columns]
            here = (k <= x) | last
            here_too = here_too + jnp.where(here, arrived, 0.0)
            above_too = above_too + jnp.where(here, 0.0, arrived)
        own[:, columns] = here_too
        rise[:, columns] = above_too

        @pl.when(y < NY - 1)
        def _():
            along_y(c).start()

        if c in (3, 4):

            @pl.when(core == 1)
            def _():
                probe_step(c - 1)

    for c in range(CHUNKS):

        @pl.when(y > 0)
        def _():
            along_y(c).wait_recv()
            for n in range(c * CHUNK, (c + 1) * CHUNK):
                out_ref[:, :, pl.ds(n * HALF, HALF)] = own[:, n] + got_y[:, n]

        @pl.when(y == 0)
        def _():
            for n in range(c * CHUNK, (c + 1) * CHUNK):
                out_ref[:, :, pl.ds(n * HALF, HALF)] = own[:, n]

        @pl.when(y < NY - 1)
        def _():
            along_y(c).wait_send()

    @pl.when(core == 0)
    def _():
        for number in range(4):
            probe_step(number)

    for r in range(1, OWNERS):
        metas(r).wait_send()
    for slot in (2, 3):
        amplitudes(slot).wait_send()
    end_stage(3)
    for c in range(CHUNKS):
        for k in range(1, NX):
            along_x(c, k).wait_send()
    probe_step(4)


def step(packed, meta, object_field, probe, tables):
    dma = pltpu.SemaphoreType.DMA
    return pl.pallas_call(
        step_kernel,
        out_shape=(
            jax.ShapeDtypeStruct((2, STRIP, TILE), F32),
            jax.ShapeDtypeStruct((2 * SIDE, SIDE), F32),
        ),
        in_specs=[HBM, VMEM, HBM, VMEM, HBM],
        out_specs=(VMEM, VMEM),
        scratch_shapes=[
            pltpu.VMEM((OWNERS, CAP, 2, SIDE, HALF), F32),
            pltpu.VMEM((OWNERS, 8, 128), jnp.int32),
            pltpu.SMEM((OWNERS, 8, 128), jnp.int32),
            pltpu.VMEM((2, BLOCKS, SPAN, HALF), F32),
            pltpu.VMEM(tables.shape, BF16),
            pltpu.VMEM((3 * SLOTS + 1, 2, SPAN + STRIP, HALF), F32),
            pltpu.VMEM((2 * SIDE, SIDE), F32),
            pltpu.VMEM((2, BLOCKS, SPAN, HALF), F32),
            pltpu.VMEM((NX - 1, 2, BLOCKS, STRIP, HALF), F32),
            pltpu.VMEM((2, BLOCKS, STRIP, HALF), F32),
            pltpu.VMEM((2, BLOCKS, STRIP, HALF), F32),
            pltpu.VMEM((2, BLOCKS, STRIP, HALF), F32),
            pltpu.VMEM((OWNERS, 64, SIDE), F32),
            pltpu.VMEM((NY, 16, SIDE), F32),
            pltpu.VMEM((NX, 16, SIDE), F32),
            dma((BLOCKS + 4,)),
            dma((SLOTS,)),
            dma((SLOTS,)),
            dma((OWNERS,)),
            dma((OWNERS,)),
            dma((NX - 1, CHUNKS)),
            dma((NX - 1, CHUNKS)),
            dma((CHUNKS,)),
            dma((CHUNKS,)),
            dma((OWNERS,)),
            dma((OWNERS,)),
            dma((NY,)),
            dma((NY,)),
            dma((NX,)),
            dma((NX,)),
            dma((NY,)),
            dma((NY,)),
            dma((OWNERS,)),
            dma((OWNERS,)),
        ],
        compiler_params=pltpu.CompilerParams(
            collective_id=0, has_side_effects=True, vmem_limit_bytes=48 * 2**20
        ),
        name="step",
    )(packed, meta, object_field, probe, tables)


def on_device(object_field, probe, amplitude, tile_owner, row_start, col_start):
    tables = jnp.asarray(dft_tables())
    packed, meta = pack(tile_owner, row_start, col_start, amplitude)
    object_grad, probe_grad = step(packed, meta, object_field, probe, tables)
    return object_grad, probe_grad.reshape(2, SIDE, SIDE)


def solution(mesh):
    return jax.shard_map(
        on_device,
        mesh=mesh,
        in_specs=(
            P(None, None, "obj"),
            P(),
            P(("pat", "obj"), None, None),
            P(("pat", "obj"), None),
            P(("pat", "obj")),
            P(("pat", "obj")),
        ),
        out_specs=(P(None, "pat", "obj"), P()),
        check_vma=False,
    )
```

```python
import math

import jax
import jax.numpy as jnp
import numpy as np
from jax import lax
from jax.experimental import pallas as pl
from jax.experimental.pallas import tpu as pltpu
from jax.sharding import PartitionSpec as P

MESH = pl.DeviceIdType.MESH
CAP = 2
SIDE = 256
HALF = 128
STRIP = 64
SPAN = 320
TILE = 2048
BLOCKS = TILE // HALF
SOFTEN = 0.25
OWNERS = 8
COUNT = 8
SLOTS = OWNERS * CAP
NX = 4
NY = 4
CHUNKS = 16
CHUNK = BLOCKS // CHUNKS
F32 = jnp.float32
BF16 = jnp.bfloat16
HBM = pl.BlockSpec(memory_space=pltpu.HBM)
VMEM = pl.BlockSpec(memory_space=pltpu.VMEM)
SMEM = pl.BlockSpec(memory_space=pltpu.SMEM)


def dft_tables():
    index = np.arange(SIDE)
    full = np.exp(-2j * np.pi * (np.outer(index, index) % SIDE) / SIDE) / math.sqrt(SIDE)

    def right(table):
        return np.block([[table.real, table.imag], [-table.imag, table.real]])

    swap = np.roll(np.arange(HALF), -HALF // 2)
    half = [full[:HALF, 0::2], full[:HALF, 1::2]]
    lane = [half[0], half[1][:, swap]]
    tables = [
        right(lane[0]),
        right(lane[1]),
        right(half[0]).T,
        right(half[1]).T,
        right(half[0].conj().T).T,
        right(half[1].conj().T).T,
        right(lane[0].conj().T),
        right(lane[1].conj().T),
    ]
    exact = np.stack(tables).astype(np.float32)
    high = exact.astype(BF16)
    low = (exact - high.astype(np.float32)).astype(BF16)
    return np.stack([high, low], axis=1)


def split(value):
    high = value.astype(BF16)
    return high, (value - high.astype(F32)).astype(BF16)


def times_table(data, table):
    high, low = split(data)
    left = jnp.concatenate([high, low, high], axis=1)
    right = jnp.concatenate([table[0], table[0], table[1]], axis=0)
    return jnp.dot(left, right, preferred_element_type=F32)


def table_times(table, data):
    high, low = split(data)
    left = jnp.concatenate([table[0], table[0], table[1]], axis=1)
    right = jnp.concatenate([high, low, high], axis=0)
    return jnp.dot(left, right, preferred_element_type=F32)


def beside(*parts):
    return jnp.concatenate(parts, axis=1)


def above(*parts):
    return jnp.concatenate(parts, axis=0)


def by_parity(rows):
    lane = lax.broadcasted_iota(jnp.int32, (HALF, HALF), 1)
    front = lane < HALF // 2
    first = jnp.take_along_axis(
        rows[:, :HALF], jnp.where(front, 2 * lane, 2 * lane - HALF + 1), axis=1, mode="promise_in_bounds"
    )
    second = jnp.take_along_axis(
        rows[:, HALF:], jnp.where(front, 2 * lane + 1, 2 * lane - HALF), axis=1, mode="promise_in_bounds"
    )
    return beside(jnp.where(front, first, second), jnp.where(front, second, first))


FRONT = slice(0, HALF)
BACK = slice(HALF, SIDE)


def residual_waves(exits, wanted_rows, tables):
    count = len(exits)

    def from_right(waves, number):
        out = times_table(above(*waves), tables(number))
        return [out[SIDE * j : SIDE * (j + 1)] for j in range(count)]

    def from_left(number, waves):
        out = table_times(tables(number), beside(*waves))
        return [out[:, SIDE * j : SIDE * (j + 1)] for j in range(count)]

    even = from_right(
        [beside(re[:, FRONT] + re[:, BACK], im[:, FRONT] + im[:, BACK]) for re, im in exits], 0
    )
    odd = from_right(
        [beside(re[:, FRONT] - re[:, BACK], im[:, FRONT] - im[:, BACK]) for re, im in exits], 1
    )
    half_re = [beside(e[:, FRONT], o[:, FRONT]) for e, o in zip(even, odd)]
    half_im = [beside(e[:, BACK], o[:, BACK]) for e, o in zip(even, odd)]
    pairs = list(zip(half_re, half_im))
    spectrum = [
        from_left(2, [above(re[FRONT] + re[BACK], im[FRONT] + im[BACK]) for re, im in pairs]),
        from_left(3, [above(re[FRONT] - re[BACK], im[FRONT] - im[BACK]) for re, im in pairs]),
    ]
    returned = []
    for parity in range(2):
        scaled = []
        for j in range(count):
            re, im = spectrum[parity][j][FRONT], spectrum[parity][j][BACK]
            ratio = wanted_rows(j, parity) * lax.rsqrt(re * re + im * im + SOFTEN)
            scaled.append(above(re * ratio, im * ratio))
        returned.append(from_left(4 + parity, scaled))
    pairs = []
    for e, o in zip(*returned):
        re = above(e[FRONT] + o[FRONT], e[FRONT] - o[FRONT])
        im = above(e[BACK] + o[BACK], e[BACK] - o[BACK])
        pairs.append((re, im))
    even = from_right([beside(re[:, FRONT], im[:, FRONT]) for re, im in pairs], 6)
    odd = from_right([beside(re[:, BACK], im[:, BACK]) for re, im in pairs], 7)
    residuals = []
    for (re, im), e, o in zip(exits, even, odd):
        back_re = beside(e[:, FRONT] + o[:, FRONT], e[:, FRONT] - o[:, FRONT])
        back_im = beside(e[:, BACK] + o[:, BACK], e[:, BACK] - o[:, BACK])
        residuals.append((back_re - re, back_im - im))
    return residuals


def pack_kernel(owner_ref, row_ref, col_ref, amp_ref, packed_ref, meta_ref, held, come, leave):
    def arriving(j, side):
        return pltpu.make_async_copy(
            amp_ref.at[j, :, pl.ds(side * HALF, HALF)], held.at[j, side], come.at[j, side]
        )

    for j in range(COUNT):
        for side in range(2):
            arriving(j, side).start()
    ranks = []
    for j in range(COUNT):
        rank = jnp.int32(0)
        for i in range(j):
            rank = rank + (owner_ref[0, i] == owner_ref[0, j]).astype(jnp.int32)
        ranks.append(rank)
    leaving = []
    for j in range(COUNT):
        for side in range(2):
            arriving(j, side).wait()
        copy = pltpu.make_async_copy(held.at[j], packed_ref.at[owner_ref[0, j], ranks[j]], leave.at[j])
        copy.start()
        leaving.append(copy)
    meta_ref[...] = jnp.zeros_like(meta_ref)
    sub = lax.broadcasted_iota(jnp.int32, (8, 128), 0)
    for j in range(COUNT):
        mine = (sub // 4 == ranks[j]) & (sub % 4 < 3)
        value = jnp.where(sub % 4 == 0, 1, jnp.where(sub % 4 == 1, row_ref[j], col_ref[j]))
        meta_ref[owner_ref[0, j]] = jnp.where(mine, value, meta_ref[owner_ref[0, j]])
    for copy in leaving:
        copy.wait()


def pack(tile_owner, row_start, col_start, amplitude):
    return pl.pallas_call(
        pack_kernel,
        out_shape=(
            jax.ShapeDtypeStruct((OWNERS, CAP, 2, SIDE, HALF), F32),
            jax.ShapeDtypeStruct((OWNERS, 8, 128), jnp.int32),
        ),
        in_specs=[SMEM, SMEM, SMEM, HBM],
        out_specs=(HBM, VMEM),
        scratch_shapes=[
            pltpu.VMEM((COUNT, 2, SIDE, HALF), F32),
            pltpu.SemaphoreType.DMA((COUNT, 2)),
            pltpu.SemaphoreType.DMA((COUNT,)),
        ],
        name="pack",
    )(tile_owner.T, row_start, col_start, amplitude)


def step_kernel(
    packed_ref, meta_ref, object_ref, probe_hbm, tables_ref, out_ref, total_ref,
    probe_ref, got, got_meta, corners, strip, tables, pads, part, grad, got_x, got_y, own, rise, near, quarter, sixteenth,
    load, send, recv, send_meta, recv_meta, send_x, recv_x, send_y, recv_y,
    send_a, recv_a, send_b, recv_b, send_c, recv_c, send_d, recv_d, send_e, recv_e,
):
    me = lax.axis_index("obj")
    z = me // 2
    core = lax.rem(me, 2)
    group = lax.axis_index("pat")
    x = lax.rem(group, NX)
    y = group // NX
    last = y == NY - 1
    base = pl.multiple_of(jnp.minimum(group, 11) * STRIP, STRIP)

    def obj_at(r):
        return lax.rem(z + r // 2, OWNERS // 2) * 2 + lax.rem(core + lax.rem(r, 2), 2)

    def obj_peer(r):
        return {"obj": obj_at(r)}

    def x_peer(k):
        return {"pat": y * NX + lax.rem(x + k, NX)}

    def y_peer(k):
        return {"pat": lax.rem(y + k, NY) * NX + x}

    def remote(src, dst, send, recv, peer):
        return pltpu.make_async_remote_copy(
            src_ref=src, dst_ref=dst, send_sem=send, recv_sem=recv, device_id=peer, device_id_type=MESH
        )

    peers = [obj_peer(r) for r in range(1, OWNERS)]
    peers += [x_peer(k) for k in range(1, NX)] + [y_peer(k) for k in range(1, NY)]
    barrier = pltpu.get_barrier_semaphore()
    for peer in peers:
        pl.semaphore_signal(barrier, inc=1, device_id=peer, device_id_type=MESH)

    loads = [
        pltpu.make_async_copy(
            object_ref.at[:, pl.ds(base, SPAN), pl.ds(n * HALF, HALF)], strip.at[:, n], load.at[n]
        )
        for n in range(BLOCKS)
    ]
    loads.append(pltpu.make_async_copy(tables_ref, tables, load.at[BLOCKS]))
    loads.append(pltpu.make_async_copy(probe_hbm, probe_ref, load.at[BLOCKS + 4]))
    load_meta = pltpu.make_async_copy(meta_ref.at[me], got_meta.at[0], load.at[BLOCKS + 1])
    load_own = pltpu.make_async_copy(packed_ref.at[me], got.at[0], load.at[BLOCKS + 2])

    def metas(r):
        return remote(meta_ref.at[obj_at(r)], got_meta.at[r], send_meta.at[r], recv_meta.at[r], obj_peer(r))

    def amplitudes(slot):
        r = slot // CAP
        n = lax.rem(slot, CAP)
        return remote(
            packed_ref.at[obj_at(r), n], got.at[r, n], send.at[slot], recv.at[slot], obj_peer(r)
        )

    stages = [
        [2 * (2 * dz + side) + n for n in range(CAP) for dz in distances]
        for side in (core, 1 - core)
        for distances in ((1, 3), (2,))
    ]

    def start_stage(number):
        for slot in stages[number]:
            amplitudes(slot).start()

    def end_stage(number):
        for slot in stages[number]:
            amplitudes(slot).wait_send()

    load_meta.start()
    load_own.start()
    for copy in loads:
        copy.start()
    pl.semaphore_wait(barrier, len(peers))
    for r in range(1, OWNERS):
        metas(r).start()
    for slot in (2, 3):
        amplitudes(slot).start()
    start_stage(0)
    edge = jnp.zeros((2, STRIP, HALF), F32)
    for n in range(3 * SLOTS):
        pads[n, :, pl.ds(0, STRIP), :] = edge
        pads[n, :, pl.ds(STRIP + SIDE, STRIP), :] = edge
    pads[3 * SLOTS] = jnp.zeros((2, SPAN + STRIP, HALF), F32)
    part[...] = jnp.zeros_like(part)

    def take_corners(pair):
        if pair:
            metas(2 * pair).wait_recv()
            metas(2 * pair + 1).wait_recv()
        else:
            load_meta.wait()
            metas(1).wait_recv()
        rows = pl.ds(2 * pair, 2)
        copy = pltpu.make_async_copy(got_meta.at[rows], corners.at[rows], load.at[BLOCKS + 3])
        copy.start()
        copy.wait()

    take_corners(0)
    for copy in loads:
        copy.wait()
    load_own.wait()

    lane = lax.broadcasted_iota(jnp.int32, (SIDE, HALF), 1)

    def corner(slot):
        r = slot // CAP
        at = 4 * lax.rem(slot, CAP)
        row = jnp.clip(corners[r, at + 1, 0] - base, 0, STRIP)
        col = jnp.clip(corners[r, at + 2, 0], 0, TILE - SIDE)
        start = jnp.minimum(col // HALF, BLOCKS - 3)
        return row, start, col - start * HALF

    def window(slot, part):
        row, start, shift = corner(slot)
        unshift = lax.rem(HALF - shift, HALF)
        turned = [
            pltpu.roll(strip[part, start + n, pl.ds(row, SIDE), :], unshift, axis=1) for n in range(3)
        ]
        inner = lane < HALF - shift
        return beside(jnp.where(inner, turned[0], turned[1]), jnp.where(inner, turned[1], turned[2]))

    def from_pair(k, carry):
        dz = jnp.where(k >= 6, 2, jnp.where(lax.rem(k, 2) == 0, 1, 3))
        n = jnp.where(k >= 6, k - 6, (k - 2) // 2)
        one = jnp.where(k < 2, 2 * k, 4 * dz + n)
        two = jnp.where(k < 2, 2 * k + 1, 4 * dz + 2 + n)

        for side, turn, number in ((0, 4, 0), (1, 2, 0), (1, 2, 1), (1, 4, 2)):

            @pl.when((core == side) & (k == turn))
            def _():
                end_stage(number)
                start_stage(number + 1)

        @pl.when((core == 0) & (k == 6))
        def _():
            start_stage(2)

        for pair, turn in ((1, 2), (3, 3), (2, 6)):

            @pl.when(k == turn)
            def _():
                take_corners(pair)

        @pl.when(k > 0)
        def _():
            amplitudes(one).wait_recv()
            amplitudes(two).wait_recv()

        slots = [one, two]
        probe_re = probe_ref[0]
        probe_im = probe_ref[1]
        windows = [(window(slot, 0), window(slot, 1)) for slot in slots]
        exits = [
            (probe_re * re - probe_im * im, probe_re * im + probe_im * re) for re, im in windows
        ]

        def wanted_rows(j, parity):
            return by_parity(
                beside(
                    got[slots[j] // CAP, lax.rem(slots[j], CAP), 0, pl.ds(parity, HALF, stride=2), :],
                    got[slots[j] // CAP, lax.rem(slots[j], CAP), 1, pl.ds(parity, HALF, stride=2), :],
                )
            )

        residuals = residual_waves(exits, wanted_rows, lambda i: (tables[i, 0], tables[i, 1]))
        part_re = part[pl.ds(0, SIDE), :]
        part_im = part[pl.ds(SIDE, SIDE), :]
        for j, slot in enumerate(slots):
            keep = corners[slot // CAP, 4 * lax.rem(slot, CAP), 0] > 0
            res_re = jnp.where(keep, residuals[j][0], 0.0)
            res_im = jnp.where(keep, residuals[j][1], 0.0)
            window_re, window_im = windows[j]
            part_re = part_re + (window_re * res_re + window_im * res_im)
            part_im = part_im + (window_re * res_im - window_im * res_re)
            shift = corner(slot)[2]
            turn = lax.rem(shift, HALF)
            outer = lane >= shift
            rows = pl.ds(STRIP, SIDE)
            for c, value in (
                (0, probe_re * res_re + probe_im * res_im),
                (1, probe_re * res_im - probe_im * res_re),
            ):
                first = pltpu.roll(value[:, FRONT], turn, axis=1)
                second = pltpu.roll(value[:, BACK], turn, axis=1)
                pads[3 * slot, c, rows, :] = jnp.where(outer, first, 0.0)
                pads[3 * slot + 1, c, rows, :] = jnp.where(outer, second, first)
                pads[3 * slot + 2, c, rows, :] = jnp.where(outer, 0.0, second)
        part[pl.ds(0, SIDE), :] = part_re
        part[pl.ds(SIDE, SIDE), :] = part_im
        return carry

    lax.fori_loop(0, OWNERS, from_pair, 0)

    def eighth(number):
        return pl.ds(pl.multiple_of(number * 64, 64), 64)

    def sixteen(number):
        return pl.ds(pl.multiple_of(number * 16, 16), 16)

    mine = pl.ds(pl.multiple_of(me * 64 + y * 16, 16), 16)

    def stage_a(r):
        return remote(part.at[eighth(obj_at(r))], near.at[r], send_a.at[r], recv_a.at[r], obj_peer(r))

    def stage_b(k):
        there = lax.rem(y + k, NY)
        return remote(near.at[0, sixteen(there)], quarter.at[k], send_b.at[k], recv_b.at[k], y_peer(k))

    def stage_c(k):
        return remote(sixteenth.at[x], sixteenth.at[x], send_c.at[k], recv_c.at[k], x_peer(k))

    def stage_d(k):
        return remote(total_ref.at[mine], total_ref.at[mine], send_d.at[k], recv_d.at[k], y_peer(k))

    def stage_e(r):
        return remote(
            total_ref.at[eighth(me)], total_ref.at[eighth(me)], send_e.at[r], recv_e.at[r], obj_peer(r)
        )

    def probe_step(number):
        if number == 0:
            for r in range(1, OWNERS):
                stage_a(r).wait()
            value = part[eighth(me), :]
            for r in range(1, OWNERS):
                value = value + near[r]
            near[0] = value
            for k in range(1, NY):
                stage_b(k).start()
        elif number == 1:
            for k in range(1, NY):
                stage_b(k).wait()
            value = near[0, sixteen(y), :]
            for k in range(1, NY):
                value = value + quarter[k]
            sixteenth[x] = value
            for k in range(1, NX):
                stage_c(k).start()
        elif number == 2:
            for k in range(1, NX):
                stage_c(k).wait()
            value = (sixteenth[0] + sixteenth[1]) + (sixteenth[2] + sixteenth[3])
            total_ref[mine, :] = value * (1.0 / math.sqrt(1024.0))
            for k in range(1, NY):
                stage_d(k).start()
        elif number == 3:
            for k in range(1, NY):
                stage_d(k).wait()
            for r in range(1, OWNERS):
                stage_e(r).start()
        else:
            for r in range(1, OWNERS):
                stage_e(r).wait()

    for r in range(1, OWNERS):
        stage_a(r).start()

    def block(number):
        return pl.ds(pl.multiple_of(number * STRIP, STRIP), STRIP)

    def along_x(c, k):
        number = jnp.where(last, lax.rem(x + k, NX) + 1, k)
        columns = pl.ds(c * CHUNK, CHUNK)
        return remote(
            grad.at[:, columns, block(number)],
            got_x.at[k - 1, :, columns],
            send_x.at[k - 1, c],
            recv_x.at[k - 1, c],
            x_peer(k),
        )

    def along_y(c):
        columns = pl.ds(c * CHUNK, CHUNK)
        return remote(rise.at[:, columns], got_y.at[:, columns], send_y.at[c], recv_y.at[c], y_peer(1))

    def gather_chunk(c, carry):
        def gather_block(b, carry):
            for part in range(2):
                value = None
                for slot in range(SLOTS):
                    row, start, _ = corner(slot)
                    n = b - start
                    at = jnp.where((n >= 0) & (n < 3), 3 * slot + n, 3 * SLOTS)
                    term = pads[at, part, pl.ds(STRIP - row, SPAN), :]
                    value = term if value is None else value + term
                grad[part, b] = value
            return carry

        lax.fori_loop(c * CHUNK, (c + 1) * CHUNK, gather_block, 0)
        for k in range(1, NX):
            along_x(c, k).start()
        return carry

    lax.fori_loop(0, CHUNKS // 2, gather_chunk, 0)

    @pl.when(core == 0)
    def _():
        end_stage(1)
        end_stage(2)
        start_stage(3)

    @pl.when(core == 1)
    def _():
        probe_step(0)
        probe_step(1)

    lax.fori_loop(CHUNKS // 2, CHUNKS, gather_chunk, 0)


    own_block = block(jnp.where(last, x + 1, 0))
    for c in range(CHUNKS):
        columns = pl.ds(c * CHUNK, CHUNK)
        for k in range(1, NX):
            along_x(c, k).wait_recv()
        here_too = grad[:, columns, own_block, :]
        above_too = grad[:, columns, block(4), :]
        for k in range(1, NX):
            arrived = got_x[k - 1, :, columns]
            here = (k <= x) | last
            here_too = here_too + jnp.where(here, arrived, 0.0)
            above_too = above_too + jnp.where(here, 0.0, arrived)
        own[:, columns] = here_too
        rise[:, columns] = above_too

        @pl.when(y < NY - 1)
        def _():
            along_y(c).start()

        if c in (6, 8):

            @pl.when(core == 1)
            def _():
                probe_step(c // 2 - 1)

    for c in range(CHUNKS):

        @pl.when(y > 0)
        def _():
            along_y(c).wait_recv()
            for n in range(c * CHUNK, (c + 1) * CHUNK):
                out_ref[:, :, pl.ds(n * HALF, HALF)] = own[:, n] + got_y[:, n]

        @pl.when(y == 0)
        def _():
            for n in range(c * CHUNK, (c + 1) * CHUNK):
                out_ref[:, :, pl.ds(n * HALF, HALF)] = own[:, n]

        @pl.when(y < NY - 1)
        def _():
            along_y(c).wait_send()

    @pl.when(core == 0)
    def _():
        for number in range(4):
            probe_step(number)

    for r in range(1, OWNERS):
        metas(r).wait_send()
    for slot in (2, 3):
        amplitudes(slot).wait_send()
    end_stage(3)
    for c in range(CHUNKS):
        for k in range(1, NX):
            along_x(c, k).wait_send()
    probe_step(4)


def step(packed, meta, object_field, probe, tables):
    dma = pltpu.SemaphoreType.DMA
    return pl.pallas_call(
        step_kernel,
        out_shape=(
            jax.ShapeDtypeStruct((2, STRIP, TILE), F32),
            jax.ShapeDtypeStruct((2 * SIDE, SIDE), F32),
        ),
        in_specs=[HBM, VMEM, HBM, HBM, HBM],
        out_specs=(VMEM, VMEM),
        scratch_shapes=[
            pltpu.VMEM((2, SIDE, SIDE), F32),
            pltpu.VMEM((OWNERS, CAP, 2, SIDE, HALF), F32),
            pltpu.VMEM((OWNERS, 8, 128), jnp.int32),
            pltpu.SMEM((OWNERS, 8, 128), jnp.int32),
            pltpu.VMEM((2, BLOCKS, SPAN, HALF), F32),
            pltpu.VMEM(tables.shape, BF16),
            pltpu.VMEM((3 * SLOTS + 1, 2, SPAN + STRIP, HALF), F32),
            pltpu.VMEM((2 * SIDE, SIDE), F32),
            pltpu.VMEM((2, BLOCKS, SPAN, HALF), F32),
            pltpu.VMEM((NX - 1, 2, BLOCKS, STRIP, HALF), F32),
            pltpu.VMEM((2, BLOCKS, STRIP, HALF), F32),
            pltpu.VMEM((2, BLOCKS, STRIP, HALF), F32),
            pltpu.VMEM((2, BLOCKS, STRIP, HALF), F32),
            pltpu.VMEM((OWNERS, 64, SIDE), F32),
            pltpu.VMEM((NY, 16, SIDE), F32),
            pltpu.VMEM((NX, 16, SIDE), F32),
            dma((BLOCKS + 5,)),
            dma((SLOTS,)),
            dma((SLOTS,)),
            dma((OWNERS,)),
            dma((OWNERS,)),
            dma((NX - 1, CHUNKS)),
            dma((NX - 1, CHUNKS)),
            dma((CHUNKS,)),
            dma((CHUNKS,)),
            dma((OWNERS,)),
            dma((OWNERS,)),
            dma((NY,)),
            dma((NY,)),
            dma((NX,)),
            dma((NX,)),
            dma((NY,)),
            dma((NY,)),
            dma((OWNERS,)),
            dma((OWNERS,)),
        ],
        compiler_params=pltpu.CompilerParams(
            collective_id=0, has_side_effects=True, vmem_limit_bytes=48 * 2**20
        ),
        name="step",
    )(packed, meta, object_field, probe, tables)


def on_device(object_field, probe, amplitude, tile_owner, row_start, col_start):
    tables = jnp.asarray(dft_tables())
    packed, meta = pack(tile_owner, row_start, col_start, amplitude)
    object_grad, probe_grad = step(packed, meta, object_field, probe, tables)
    return object_grad, probe_grad.reshape(2, SIDE, SIDE)


def solution(mesh):
    return jax.shard_map(
        on_device,
        mesh=mesh,
        in_specs=(
            P(None, None, "obj"),
            P(),
            P(("pat", "obj"), None, None),
            P(("pat", "obj"), None),
            P(("pat", "obj")),
            P(("pat", "obj")),
        ),
        out_specs=(P(None, "pat", "obj"), P()),
        check_vma=False,
    )
```

```python
import math

import jax
import jax.numpy as jnp
import numpy as np
from jax import lax
from jax.experimental import pallas as pl
from jax.experimental.pallas import tpu as pltpu
from jax.sharding import PartitionSpec as P

MESH = pl.DeviceIdType.MESH
CAP = 2
SIDE = 256
HALF = 128
STRIP = 64
SPAN = 320
TILE = 2048
BLOCKS = TILE // HALF
SOFTEN = 0.25
OWNERS = 8
COUNT = 8
SLOTS = OWNERS * CAP
NX = 4
NY = 4
CHUNKS = 16
CHUNK = BLOCKS // CHUNKS
F32 = jnp.float32
BF16 = jnp.bfloat16
HBM = pl.BlockSpec(memory_space=pltpu.HBM)
VMEM = pl.BlockSpec(memory_space=pltpu.VMEM)
SMEM = pl.BlockSpec(memory_space=pltpu.SMEM)


def dft_tables():
    index = np.arange(SIDE)
    full = np.exp(-2j * np.pi * (np.outer(index, index) % SIDE) / SIDE) / math.sqrt(SIDE)

    def right(table):
        return np.block([[table.real, table.imag], [-table.imag, table.real]])

    swap = np.roll(np.arange(HALF), -HALF // 2)
    half = [full[:HALF, 0::2], full[:HALF, 1::2]]
    lane = [half[0], half[1][:, swap]]
    tables = [
        right(lane[0]),
        right(lane[1]),
        right(half[0]).T,
        right(half[1]).T,
        right(half[0].conj().T).T,
        right(half[1].conj().T).T,
        right(lane[0].conj().T),
        right(lane[1].conj().T),
    ]
    exact = np.stack(tables).astype(np.float32)
    high = exact.astype(BF16)
    low = (exact - high.astype(np.float32)).astype(BF16)
    return np.stack([high, low], axis=1)


def split(value):
    high = value.astype(BF16)
    return high, (value - high.astype(F32)).astype(BF16)


def times_table(data, table):
    high, low = split(data)
    left = jnp.concatenate([high, low, high], axis=1)
    right = jnp.concatenate([table[0], table[0], table[1]], axis=0)
    return jnp.dot(left, right, preferred_element_type=F32)


def table_times(table, data):
    high, low = split(data)
    left = jnp.concatenate([table[0], table[0], table[1]], axis=1)
    right = jnp.concatenate([high, low, high], axis=0)
    return jnp.dot(left, right, preferred_element_type=F32)


def beside(*parts):
    return jnp.concatenate(parts, axis=1)


def above(*parts):
    return jnp.concatenate(parts, axis=0)


def by_parity(rows):
    lane = lax.broadcasted_iota(jnp.int32, (HALF, HALF), 1)
    front = lane < HALF // 2
    first = jnp.take_along_axis(
        rows[:, :HALF], jnp.where(front, 2 * lane, 2 * lane - HALF + 1), axis=1, mode="promise_in_bounds"
    )
    second = jnp.take_along_axis(
        rows[:, HALF:], jnp.where(front, 2 * lane + 1, 2 * lane - HALF), axis=1, mode="promise_in_bounds"
    )
    return beside(jnp.where(front, first, second), jnp.where(front, second, first))


FRONT = slice(0, HALF)
BACK = slice(HALF, SIDE)


def residual_waves(exits, wanted_rows, tables):
    count = len(exits)

    def from_right(waves, number):
        out = times_table(above(*waves), tables(number))
        return [out[SIDE * j : SIDE * (j + 1)] for j in range(count)]

    def from_left(number, waves):
        out = table_times(tables(number), beside(*waves))
        return [out[:, SIDE * j : SIDE * (j + 1)] for j in range(count)]

    even = from_right(
        [beside(re[:, FRONT] + re[:, BACK], im[:, FRONT] + im[:, BACK]) for re, im in exits], 0
    )
    odd = from_right(
        [beside(re[:, FRONT] - re[:, BACK], im[:, FRONT] - im[:, BACK]) for re, im in exits], 1
    )
    half_re = [beside(e[:, FRONT], o[:, FRONT]) for e, o in zip(even, odd)]
    half_im = [beside(e[:, BACK], o[:, BACK]) for e, o in zip(even, odd)]
    pairs = list(zip(half_re, half_im))
    spectrum = [
        from_left(2, [above(re[FRONT] + re[BACK], im[FRONT] + im[BACK]) for re, im in pairs]),
        from_left(3, [above(re[FRONT] - re[BACK], im[FRONT] - im[BACK]) for re, im in pairs]),
    ]
    returned = []
    for parity in range(2):
        scaled = []
        for j in range(count):
            re, im = spectrum[parity][j][FRONT], spectrum[parity][j][BACK]
            ratio = wanted_rows(j, parity) * lax.rsqrt(re * re + im * im + SOFTEN)
            scaled.append(above(re * ratio, im * ratio))
        returned.append(from_left(4 + parity, scaled))
    pairs = []
    for e, o in zip(*returned):
        re = above(e[FRONT] + o[FRONT], e[FRONT] - o[FRONT])
        im = above(e[BACK] + o[BACK], e[BACK] - o[BACK])
        pairs.append((re, im))
    even = from_right([beside(re[:, FRONT], im[:, FRONT]) for re, im in pairs], 6)
    odd = from_right([beside(re[:, BACK], im[:, BACK]) for re, im in pairs], 7)
    residuals = []
    for (re, im), e, o in zip(exits, even, odd):
        back_re = beside(e[:, FRONT] + o[:, FRONT], e[:, FRONT] - o[:, FRONT])
        back_im = beside(e[:, BACK] + o[:, BACK], e[:, BACK] - o[:, BACK])
        residuals.append((back_re - re, back_im - im))
    return residuals


def pack_kernel(owner_ref, row_ref, col_ref, amp_ref, packed_ref, meta_ref, held, come, leave):
    def arriving(j, side):
        return pltpu.make_async_copy(
            amp_ref.at[j, :, pl.ds(side * HALF, HALF)], held.at[j, side], come.at[j, side]
        )

    for j in range(COUNT):
        for side in range(2):
            arriving(j, side).start()
    ranks = []
    for j in range(COUNT):
        rank = jnp.int32(0)
        for i in range(j):
            rank = rank + (owner_ref[0, i] == owner_ref[0, j]).astype(jnp.int32)
        ranks.append(rank)
    leaving = []
    for j in range(COUNT):
        for side in range(2):
            arriving(j, side).wait()
        copy = pltpu.make_async_copy(held.at[j], packed_ref.at[owner_ref[0, j], ranks[j]], leave.at[j])
        copy.start()
        leaving.append(copy)
    meta_ref[...] = jnp.zeros_like(meta_ref)
    sub = lax.broadcasted_iota(jnp.int32, (8, 128), 0)
    for j in range(COUNT):
        mine = (sub // 4 == ranks[j]) & (sub % 4 < 3)
        value = jnp.where(sub % 4 == 0, 1, jnp.where(sub % 4 == 1, row_ref[j], col_ref[j]))
        meta_ref[owner_ref[0, j]] = jnp.where(mine, value, meta_ref[owner_ref[0, j]])
    for copy in leaving:
        copy.wait()


def pack(tile_owner, row_start, col_start, amplitude):
    return pl.pallas_call(
        pack_kernel,
        out_shape=(
            jax.ShapeDtypeStruct((OWNERS, CAP, 2, SIDE, HALF), F32),
            jax.ShapeDtypeStruct((OWNERS, 8, 128), jnp.int32),
        ),
        in_specs=[SMEM, SMEM, SMEM, HBM],
        out_specs=(HBM, VMEM),
        scratch_shapes=[
            pltpu.VMEM((COUNT, 2, SIDE, HALF), F32),
            pltpu.SemaphoreType.DMA((COUNT, 2)),
            pltpu.SemaphoreType.DMA((COUNT,)),
        ],
        name="pack",
    )(tile_owner.T, row_start, col_start, amplitude)


def step_kernel(
    packed_ref, meta_ref, object_ref, probe_hbm, tables_ref, out_ref, total_ref,
    probe_ref, got, got_meta, corners, strip, tables, pads, part, grad, got_x, got_y, own, rise, near, quarter, sixteenth,
    load, send, recv, send_meta, recv_meta, send_x, recv_x, send_y, recv_y,
    send_a, recv_a, send_b, recv_b, send_c, recv_c, send_d, recv_d, send_e, recv_e,
):
    me = lax.axis_index("obj")
    z = me // 2
    core = lax.rem(me, 2)
    group = lax.axis_index("pat")
    x = lax.rem(group, NX)
    y = group // NX
    last = y == NY - 1
    base = pl.multiple_of(jnp.minimum(group, 11) * STRIP, STRIP)

    def obj_at(r):
        return lax.rem(z + r // 2, OWNERS // 2) * 2 + lax.rem(core + lax.rem(r, 2), 2)

    def obj_peer(r):
        return {"obj": obj_at(r)}

    def x_peer(k):
        return {"pat": y * NX + lax.rem(x + k, NX)}

    def y_peer(k):
        return {"pat": lax.rem(y + k, NY) * NX + x}

    def remote(src, dst, send, recv, peer):
        return pltpu.make_async_remote_copy(
            src_ref=src, dst_ref=dst, send_sem=send, recv_sem=recv, device_id=peer, device_id_type=MESH
        )

    peers = [obj_peer(r) for r in range(1, OWNERS)]
    peers += [x_peer(k) for k in range(1, NX)] + [y_peer(k) for k in range(1, NY)]
    barrier = pltpu.get_barrier_semaphore()
    for peer in peers:
        pl.semaphore_signal(barrier, inc=1, device_id=peer, device_id_type=MESH)

    loads = [
        pltpu.make_async_copy(
            object_ref.at[:, pl.ds(base, SPAN), pl.ds(n * HALF, HALF)], strip.at[:, n], load.at[n]
        )
        for n in range(BLOCKS)
    ]
    loads.append(pltpu.make_async_copy(tables_ref, tables, load.at[BLOCKS]))
    loads.append(pltpu.make_async_copy(probe_hbm, probe_ref, load.at[BLOCKS + 4]))
    load_meta = pltpu.make_async_copy(meta_ref.at[me], got_meta.at[0], load.at[BLOCKS + 1])
    load_own = pltpu.make_async_copy(packed_ref.at[me], got.at[0], load.at[BLOCKS + 2])

    def metas(r):
        return remote(meta_ref.at[obj_at(r)], got_meta.at[r], send_meta.at[r], recv_meta.at[r], obj_peer(r))

    def amplitudes(slot):
        r = slot // CAP
        n = lax.rem(slot, CAP)
        return remote(
            packed_ref.at[obj_at(r), n], got.at[r, n], send.at[slot], recv.at[slot], obj_peer(r)
        )

    stages = [
        [2 * (2 * dz + side) + n for n in range(CAP) for dz in distances]
        for side in (core, 1 - core)
        for distances in ((1, 3), (2,))
    ]

    def start_stage(number):
        for slot in stages[number]:
            amplitudes(slot).start()

    def end_stage(number):
        for slot in stages[number]:
            amplitudes(slot).wait_send()

    load_meta.start()
    load_own.start()
    for copy in loads:
        copy.start()
    pl.semaphore_wait(barrier, len(peers))
    for r in range(1, OWNERS):
        metas(r).start()
    for slot in (2, 3):
        amplitudes(slot).start()
    start_stage(0)
    edge = jnp.zeros((2, STRIP, HALF), F32)
    for n in range(3 * SLOTS):
        pads[n, :, pl.ds(0, STRIP), :] = edge
        pads[n, :, pl.ds(STRIP + SIDE, STRIP), :] = edge
    pads[3 * SLOTS] = jnp.zeros((2, SPAN + STRIP, HALF), F32)
    part[...] = jnp.zeros_like(part)

    def take_corners(pair):
        if pair:
            metas(2 * pair).wait_recv()
            metas(2 * pair + 1).wait_recv()
        else:
            load_meta.wait()
            metas(1).wait_recv()
        rows = pl.ds(2 * pair, 2)
        copy = pltpu.make_async_copy(got_meta.at[rows], corners.at[rows], load.at[BLOCKS + 3])
        copy.start()
        copy.wait()

    take_corners(0)
    for copy in loads:
        copy.wait()
    load_own.wait()

    lane = lax.broadcasted_iota(jnp.int32, (SIDE, HALF), 1)

    def corner(slot):
        r = slot // CAP
        at = 4 * lax.rem(slot, CAP)
        row = jnp.clip(corners[r, at + 1, 0] - base, 0, STRIP)
        col = jnp.clip(corners[r, at + 2, 0], 0, TILE - SIDE)
        start = jnp.minimum(col // HALF, BLOCKS - 3)
        return row, start, col - start * HALF

    def window(slot, part):
        row, start, shift = corner(slot)
        unshift = lax.rem(HALF - shift, HALF)
        turned = [
            pltpu.roll(strip[part, start + n, pl.ds(row, SIDE), :], unshift, axis=1) for n in range(3)
        ]
        inner = lane < HALF - shift
        return beside(jnp.where(inner, turned[0], turned[1]), jnp.where(inner, turned[1], turned[2]))

    def from_pair(k, carry):
        dz = jnp.where(k >= 6, 2, jnp.where(lax.rem(k, 2) == 0, 1, 3))
        n = jnp.where(k >= 6, k - 6, (k - 2) // 2)
        one = jnp.where(k < 2, 2 * k, 4 * dz + n)
        two = jnp.where(k < 2, 2 * k + 1, 4 * dz + 2 + n)

        for side, turn, number in ((0, 4, 0), (1, 2, 0), (1, 2, 1), (1, 4, 2)):

            @pl.when((core == side) & (k == turn))
            def _():
                end_stage(number)
                start_stage(number + 1)

        @pl.when((core == 0) & (k == 6))
        def _():
            start_stage(2)

        for pair, turn in ((1, 2), (3, 3), (2, 6)):

            @pl.when(k == turn)
            def _():
                take_corners(pair)

        @pl.when(k > 0)
        def _():
            amplitudes(one).wait_recv()
            amplitudes(two).wait_recv()

        slots = [one, two]
        probe_re = probe_ref[0]
        probe_im = probe_ref[1]
        windows = [(window(slot, 0), window(slot, 1)) for slot in slots]
        exits = [
            (probe_re * re - probe_im * im, probe_re * im + probe_im * re) for re, im in windows
        ]

        def wanted_rows(j, parity):
            return by_parity(
                beside(
                    got[slots[j] // CAP, lax.rem(slots[j], CAP), 0, pl.ds(parity, HALF, stride=2), :],
                    got[slots[j] // CAP, lax.rem(slots[j], CAP), 1, pl.ds(parity, HALF, stride=2), :],
                )
            )

        residuals = residual_waves(exits, wanted_rows, lambda i: (tables[i, 0], tables[i, 1]))
        part_re = part[pl.ds(0, SIDE), :]
        part_im = part[pl.ds(SIDE, SIDE), :]
        for j, slot in enumerate(slots):
            keep = corners[slot // CAP, 4 * lax.rem(slot, CAP), 0] > 0
            res_re = jnp.where(keep, residuals[j][0], 0.0)
            res_im = jnp.where(keep, residuals[j][1], 0.0)
            window_re, window_im = windows[j]
            part_re = part_re + (window_re * res_re + window_im * res_im)
            part_im = part_im + (window_re * res_im - window_im * res_re)
            shift = corner(slot)[2]
            turn = lax.rem(shift, HALF)
            outer = lane >= shift
            rows = pl.ds(STRIP, SIDE)
            for c, value in (
                (0, probe_re * res_re + probe_im * res_im),
                (1, probe_re * res_im - probe_im * res_re),
            ):
                first = pltpu.roll(value[:, FRONT], turn, axis=1)
                second = pltpu.roll(value[:, BACK], turn, axis=1)
                pads[3 * slot, c, rows, :] = jnp.where(outer, first, 0.0)
                pads[3 * slot + 1, c, rows, :] = jnp.where(outer, second, first)
                pads[3 * slot + 2, c, rows, :] = jnp.where(outer, 0.0, second)
        part[pl.ds(0, SIDE), :] = part_re
        part[pl.ds(SIDE, SIDE), :] = part_im
        return carry

    lax.fori_loop(0, OWNERS, from_pair, 0)

    def eighth(number):
        return pl.ds(pl.multiple_of(number * 64, 64), 64)

    def sixteen(number):
        return pl.ds(pl.multiple_of(number * 16, 16), 16)

    mine = pl.ds(pl.multiple_of(me * 64 + y * 16, 16), 16)

    def stage_a(r):
        return remote(part.at[eighth(obj_at(r))], near.at[r], send_a.at[r], recv_a.at[r], obj_peer(r))

    def stage_b(k):
        there = lax.rem(y + k, NY)
        return remote(near.at[0, sixteen(there)], quarter.at[k], send_b.at[k], recv_b.at[k], y_peer(k))

    def stage_c(k):
        return remote(sixteenth.at[x], sixteenth.at[x], send_c.at[k], recv_c.at[k], x_peer(k))

    def stage_d(k):
        return remote(total_ref.at[mine], total_ref.at[mine], send_d.at[k], recv_d.at[k], y_peer(k))

    def stage_e(r):
        return remote(
            total_ref.at[eighth(me)], total_ref.at[eighth(me)], send_e.at[r], recv_e.at[r], obj_peer(r)
        )

    def probe_step(number):
        if number == 0:
            for r in range(1, OWNERS):
                stage_a(r).wait()
            value = part[eighth(me), :]
            for r in range(1, OWNERS):
                value = value + near[r]
            near[0] = value
            for k in range(1, NY):
                stage_b(k).start()
        elif number == 1:
            for k in range(1, NY):
                stage_b(k).wait()
            value = near[0, sixteen(y), :]
            for k in range(1, NY):
                value = value + quarter[k]
            sixteenth[x] = value
            for k in range(1, NX):
                stage_c(k).start()
        elif number == 2:
            for k in range(1, NX):
                stage_c(k).wait()
            value = (sixteenth[0] + sixteenth[1]) + (sixteenth[2] + sixteenth[3])
            total_ref[mine, :] = value * (1.0 / math.sqrt(1024.0))
            for k in range(1, NY):
                stage_d(k).start()
        elif number == 3:
            for k in range(1, NY):
                stage_d(k).wait()
            for r in range(1, OWNERS):
                stage_e(r).start()
        else:
            for r in range(1, OWNERS):
                stage_e(r).wait()

    for r in range(1, OWNERS):
        stage_a(r).start()

    def block(number):
        return pl.ds(pl.multiple_of(number * STRIP, STRIP), STRIP)

    def along_x(c, k):
        number = jnp.where(last, lax.rem(x + k, NX) + 1, k)
        columns = pl.ds(c * CHUNK, CHUNK)
        return remote(
            grad.at[:, columns, block(number)],
            got_x.at[k - 1, :, columns],
            send_x.at[k - 1, c],
            recv_x.at[k - 1, c],
            x_peer(k),
        )

    def along_y(c):
        columns = pl.ds(c * CHUNK, CHUNK)
        return remote(rise.at[:, columns], got_y.at[:, columns], send_y.at[c], recv_y.at[c], y_peer(1))

    def gather_chunk(c, carry):
        def gather_block(b, carry):
            for part in range(2):
                value = None
                for slot in range(SLOTS):
                    row, start, _ = corner(slot)
                    n = b - start
                    at = jnp.where((n >= 0) & (n < 3), 3 * slot + n, 3 * SLOTS)
                    term = pads[at, part, pl.ds(STRIP - row, SPAN), :]
                    value = term if value is None else value + term
                grad[part, b] = value
            return carry

        lax.fori_loop(c * CHUNK, (c + 1) * CHUNK, gather_block, 0)
        for k in range(1, NX):
            along_x(c, k).start()
        return carry

    lax.fori_loop(0, CHUNKS // 2, gather_chunk, 0)

    @pl.when(core == 0)
    def _():
        end_stage(1)
        end_stage(2)
        start_stage(3)

    @pl.when(core == 1)
    def _():
        probe_step(0)
        probe_step(1)

    lax.fori_loop(CHUNKS // 2, CHUNKS, gather_chunk, 0)


    own_block = block(jnp.where(last, x + 1, 0))
    for c in range(CHUNKS):
        columns = pl.ds(c * CHUNK, CHUNK)
        for k in range(1, NX):
            along_x(c, k).wait_recv()
        here_too = grad[:, columns, own_block, :]
        above_too = grad[:, columns, block(4), :]
        for k in range(1, NX):
            arrived = got_x[k - 1, :, columns]
            here = (k <= x) | last
            here_too = here_too + jnp.where(here, arrived, 0.0)
            above_too = above_too + jnp.where(here, 0.0, arrived)
        own[:, columns] = here_too
        rise[:, columns] = above_too

        @pl.when(y < NY - 1)
        def _():
            along_y(c).start()

        if c in (6, 8):

            @pl.when(core == 1)
            def _():
                probe_step(c // 2 - 1)

    for c in range(CHUNKS):

        @pl.when(y > 0)
        def _():
            along_y(c).wait_recv()
            for n in range(c * CHUNK, (c + 1) * CHUNK):
                out_ref[:, :, pl.ds(n * HALF, HALF)] = own[:, n] + got_y[:, n]

        @pl.when(y == 0)
        def _():
            for n in range(c * CHUNK, (c + 1) * CHUNK):
                out_ref[:, :, pl.ds(n * HALF, HALF)] = own[:, n]

        @pl.when(y < NY - 1)
        def _():
            along_y(c).wait_send()

    @pl.when(core == 0)
    def _():
        for number in range(4):
            probe_step(number)

    for r in range(1, OWNERS):
        metas(r).wait_send()
    for slot in (2, 3):
        amplitudes(slot).wait_send()
    end_stage(3)
    for c in range(CHUNKS):
        for k in range(1, NX):
            along_x(c, k).wait_send()
    probe_step(4)


def step(packed, meta, object_field, probe, tables):
    dma = pltpu.SemaphoreType.DMA
    return pl.pallas_call(
        step_kernel,
        out_shape=(
            jax.ShapeDtypeStruct((2, STRIP, TILE), F32),
            jax.ShapeDtypeStruct((2 * SIDE, SIDE), F32),
        ),
        in_specs=[HBM, HBM, HBM, HBM, HBM],
        out_specs=(VMEM, VMEM),
        scratch_shapes=[
            pltpu.VMEM((2, SIDE, SIDE), F32),
            pltpu.VMEM((OWNERS, CAP, 2, SIDE, HALF), F32),
            pltpu.VMEM((OWNERS, 8, 128), jnp.int32),
            pltpu.SMEM((OWNERS, 8, 128), jnp.int32),
            pltpu.VMEM((2, BLOCKS, SPAN, HALF), F32),
            pltpu.VMEM(tables.shape, BF16),
            pltpu.VMEM((3 * SLOTS + 1, 2, SPAN + STRIP, HALF), F32),
            pltpu.VMEM((2 * SIDE, SIDE), F32),
            pltpu.VMEM((2, BLOCKS, SPAN, HALF), F32),
            pltpu.VMEM((NX - 1, 2, BLOCKS, STRIP, HALF), F32),
            pltpu.VMEM((2, BLOCKS, STRIP, HALF), F32),
            pltpu.VMEM((2, BLOCKS, STRIP, HALF), F32),
            pltpu.VMEM((2, BLOCKS, STRIP, HALF), F32),
            pltpu.VMEM((OWNERS, 64, SIDE), F32),
            pltpu.VMEM((NY, 16, SIDE), F32),
            pltpu.VMEM((NX, 16, SIDE), F32),
            dma((BLOCKS + 5,)),
            dma((SLOTS,)),
            dma((SLOTS,)),
            dma((OWNERS,)),
            dma((OWNERS,)),
            dma((NX - 1, CHUNKS)),
            dma((NX - 1, CHUNKS)),
            dma((CHUNKS,)),
            dma((CHUNKS,)),
            dma((OWNERS,)),
            dma((OWNERS,)),
            dma((NY,)),
            dma((NY,)),
            dma((NX,)),
            dma((NX,)),
            dma((NY,)),
            dma((NY,)),
            dma((OWNERS,)),
            dma((OWNERS,)),
        ],
        compiler_params=pltpu.CompilerParams(
            collective_id=0, has_side_effects=True, vmem_limit_bytes=51 * 2**20
        ),
        name="step",
    )(packed, meta, object_field, probe, tables)


def on_device(object_field, probe, amplitude, tile_owner, row_start, col_start):
    tables = jnp.asarray(dft_tables())
    packed, meta = pack(tile_owner, row_start, col_start, amplitude)
    object_grad, probe_grad = step(packed, meta, object_field, probe, tables)
    return object_grad, probe_grad.reshape(2, SIDE, SIDE)


def solution(mesh):
    return jax.shard_map(
        on_device,
        mesh=mesh,
        in_specs=(
            P(None, None, "obj"),
            P(),
            P(("pat", "obj"), None, None),
            P(("pat", "obj"), None),
            P(("pat", "obj")),
            P(("pat", "obj")),
        ),
        out_specs=(P(None, "pat", "obj"), P()),
        check_vma=False,
    )
```

```python
import math

import jax
import jax.numpy as jnp
import numpy as np
from jax import lax
from jax.experimental import pallas as pl
from jax.experimental.pallas import tpu as pltpu
from jax.sharding import PartitionSpec as P

MESH = pl.DeviceIdType.MESH
CAP = 2
SIDE = 256
HALF = 128
STRIP = 64
SPAN = 320
TILE = 2048
BLOCKS = TILE // HALF
SOFTEN = 0.25
OWNERS = 8
COUNT = 8
SLOTS = OWNERS * CAP
NX = 4
NY = 4
CHUNKS = 16
CHUNK = BLOCKS // CHUNKS
F32 = jnp.float32
BF16 = jnp.bfloat16
HBM = pl.BlockSpec(memory_space=pltpu.HBM)
VMEM = pl.BlockSpec(memory_space=pltpu.VMEM)
SMEM = pl.BlockSpec(memory_space=pltpu.SMEM)


def dft_tables():
    index = np.arange(SIDE)
    full = np.exp(-2j * np.pi * (np.outer(index, index) % SIDE) / SIDE) / math.sqrt(SIDE)

    def right(table):
        return np.block([[table.real, table.imag], [-table.imag, table.real]])

    swap = np.roll(np.arange(HALF), -HALF // 2)
    half = [full[:HALF, 0::2], full[:HALF, 1::2]]
    lane = [half[0], half[1][:, swap]]
    tables = [
        right(lane[0]),
        right(lane[1]),
        right(half[0]).T,
        right(half[1]).T,
        right(half[0].conj().T).T,
        right(half[1].conj().T).T,
        right(lane[0].conj().T),
        right(lane[1].conj().T),
    ]
    exact = np.stack(tables).astype(np.float32)
    high = exact.astype(BF16)
    low = (exact - high.astype(np.float32)).astype(BF16)
    return np.stack([high, low], axis=1)


def split(value):
    high = value.astype(BF16)
    return high, (value - high.astype(F32)).astype(BF16)


def times_table(data, table):
    high, low = split(data)
    left = jnp.concatenate([high, low, high], axis=1)
    right = jnp.concatenate([table[0], table[0], table[1]], axis=0)
    return jnp.dot(left, right, preferred_element_type=F32)


def table_times(table, data):
    high, low = split(data)
    left = jnp.concatenate([table[0], table[0], table[1]], axis=1)
    right = jnp.concatenate([high, low, high], axis=0)
    return jnp.dot(left, right, preferred_element_type=F32)


def beside(*parts):
    return jnp.concatenate(parts, axis=1)


def above(*parts):
    return jnp.concatenate(parts, axis=0)


def by_parity(rows):
    lane = lax.broadcasted_iota(jnp.int32, (HALF, HALF), 1)
    front = lane < HALF // 2
    first = jnp.take_along_axis(
        rows[:, :HALF], jnp.where(front, 2 * lane, 2 * lane - HALF + 1), axis=1, mode="promise_in_bounds"
    )
    second = jnp.take_along_axis(
        rows[:, HALF:], jnp.where(front, 2 * lane + 1, 2 * lane - HALF), axis=1, mode="promise_in_bounds"
    )
    return beside(jnp.where(front, first, second), jnp.where(front, second, first))


FRONT = slice(0, HALF)
BACK = slice(HALF, SIDE)


def residual_waves(exits, wanted_rows, tables):
    count = len(exits)

    def from_right(waves, number):
        out = times_table(above(*waves), tables(number))
        return [out[SIDE * j : SIDE * (j + 1)] for j in range(count)]

    def from_left(number, waves):
        out = table_times(tables(number), beside(*waves))
        return [out[:, SIDE * j : SIDE * (j + 1)] for j in range(count)]

    even = from_right(
        [beside(re[:, FRONT] + re[:, BACK], im[:, FRONT] + im[:, BACK]) for re, im in exits], 0
    )
    odd = from_right(
        [beside(re[:, FRONT] - re[:, BACK], im[:, FRONT] - im[:, BACK]) for re, im in exits], 1
    )
    half_re = [beside(e[:, FRONT], o[:, FRONT]) for e, o in zip(even, odd)]
    half_im = [beside(e[:, BACK], o[:, BACK]) for e, o in zip(even, odd)]
    pairs = list(zip(half_re, half_im))
    spectrum = [
        from_left(2, [above(re[FRONT] + re[BACK], im[FRONT] + im[BACK]) for re, im in pairs]),
        from_left(3, [above(re[FRONT] - re[BACK], im[FRONT] - im[BACK]) for re, im in pairs]),
    ]
    returned = []
    for parity in range(2):
        scaled = []
        for j in range(count):
            re, im = spectrum[parity][j][FRONT], spectrum[parity][j][BACK]
            ratio = wanted_rows(j, parity) * lax.rsqrt(re * re + im * im + SOFTEN)
            scaled.append(above(re * ratio, im * ratio))
        returned.append(from_left(4 + parity, scaled))
    pairs = []
    for e, o in zip(*returned):
        re = above(e[FRONT] + o[FRONT], e[FRONT] - o[FRONT])
        im = above(e[BACK] + o[BACK], e[BACK] - o[BACK])
        pairs.append((re, im))
    even = from_right([beside(re[:, FRONT], im[:, FRONT]) for re, im in pairs], 6)
    odd = from_right([beside(re[:, BACK], im[:, BACK]) for re, im in pairs], 7)
    residuals = []
    for (re, im), e, o in zip(exits, even, odd):
        back_re = beside(e[:, FRONT] + o[:, FRONT], e[:, FRONT] - o[:, FRONT])
        back_im = beside(e[:, BACK] + o[:, BACK], e[:, BACK] - o[:, BACK])
        residuals.append((back_re - re, back_im - im))
    return residuals


def pack_kernel(owner_ref, row_ref, col_ref, amp_ref, packed_ref, meta_ref, held, come, leave):
    def arriving(j, side):
        return pltpu.make_async_copy(
            amp_ref.at[j, :, pl.ds(side * HALF, HALF)], held.at[j, side], come.at[j, side]
        )

    for j in range(COUNT):
        for side in range(2):
            arriving(j, side).start()
    ranks = []
    for j in range(COUNT):
        rank = jnp.int32(0)
        for i in range(j):
            rank = rank + (owner_ref[0, i] == owner_ref[0, j]).astype(jnp.int32)
        ranks.append(rank)
    leaving = []
    for j in range(COUNT):
        for side in range(2):
            arriving(j, side).wait()
        copy = pltpu.make_async_copy(held.at[j], packed_ref.at[owner_ref[0, j], ranks[j]], leave.at[j])
        copy.start()
        leaving.append(copy)
    meta_ref[...] = jnp.zeros_like(meta_ref)
    sub = lax.broadcasted_iota(jnp.int32, (8, 128), 0)
    for j in range(COUNT):
        mine = (sub // 4 == ranks[j]) & (sub % 4 < 3)
        value = jnp.where(sub % 4 == 0, 1, jnp.where(sub % 4 == 1, row_ref[j], col_ref[j]))
        meta_ref[owner_ref[0, j]] = jnp.where(mine, value, meta_ref[owner_ref[0, j]])
    for copy in leaving:
        copy.wait()


def pack(tile_owner, row_start, col_start, amplitude):
    return pl.pallas_call(
        pack_kernel,
        out_shape=(
            jax.ShapeDtypeStruct((OWNERS, CAP, 2, SIDE, HALF), F32),
            jax.ShapeDtypeStruct((OWNERS, 8, 128), jnp.int32),
        ),
        in_specs=[SMEM, SMEM, SMEM, HBM],
        out_specs=(HBM, VMEM),
        scratch_shapes=[
            pltpu.VMEM((COUNT, 2, SIDE, HALF), F32),
            pltpu.SemaphoreType.DMA((COUNT, 2)),
            pltpu.SemaphoreType.DMA((COUNT,)),
        ],
        name="pack",
    )(tile_owner.T, row_start, col_start, amplitude)


def step_kernel(
    packed_ref, meta_ref, object_ref, probe_hbm, tables_ref, out_ref, total_ref,
    probe_ref, got, got_meta, corners, strip, tables, pads, part, grad, got_x, got_y, own, rise, near, quarter, sixteenth,
    load, send, recv, send_meta, recv_meta, send_x, recv_x, send_y, recv_y,
    send_a, recv_a, send_b, recv_b, send_c, recv_c, send_d, recv_d, send_e, recv_e,
):
    me = lax.axis_index("obj")
    z = me // 2
    core = lax.rem(me, 2)
    group = lax.axis_index("pat")
    x = lax.rem(group, NX)
    y = group // NX
    last = y == NY - 1
    base = pl.multiple_of(jnp.minimum(group, 11) * STRIP, STRIP)

    def obj_at(r):
        return lax.rem(z + r // 2, OWNERS // 2) * 2 + lax.rem(core + lax.rem(r, 2), 2)

    def obj_peer(r):
        return {"obj": obj_at(r)}

    def x_peer(k):
        return {"pat": y * NX + lax.rem(x + k, NX)}

    def y_peer(k):
        return {"pat": lax.rem(y + k, NY) * NX + x}

    def remote(src, dst, send, recv, peer):
        return pltpu.make_async_remote_copy(
            src_ref=src, dst_ref=dst, send_sem=send, recv_sem=recv, device_id=peer, device_id_type=MESH
        )

    peers = [obj_peer(r) for r in range(1, OWNERS)]
    peers += [x_peer(k) for k in range(1, NX)] + [y_peer(k) for k in range(1, NY)]
    barrier = pltpu.get_barrier_semaphore()
    for peer in peers:
        pl.semaphore_signal(barrier, inc=1, device_id=peer, device_id_type=MESH)

    loads = [
        pltpu.make_async_copy(
            object_ref.at[:, pl.ds(base, SPAN), pl.ds(n * HALF, HALF)], strip.at[:, n], load.at[n]
        )
        for n in range(BLOCKS)
    ]
    loads.append(pltpu.make_async_copy(tables_ref, tables, load.at[BLOCKS]))
    loads.append(pltpu.make_async_copy(probe_hbm, probe_ref, load.at[BLOCKS + 4]))
    load_meta = pltpu.make_async_copy(meta_ref.at[me], got_meta.at[0], load.at[BLOCKS + 1])
    load_own = pltpu.make_async_copy(packed_ref.at[me], got.at[0], load.at[BLOCKS + 2])

    def metas(r):
        return remote(meta_ref.at[obj_at(r)], got_meta.at[r], send_meta.at[r], recv_meta.at[r], obj_peer(r))

    def amplitudes(slot):
        r = slot // CAP
        n = lax.rem(slot, CAP)
        return remote(
            packed_ref.at[obj_at(r), n], got.at[r, n], send.at[slot], recv.at[slot], obj_peer(r)
        )

    stages = [
        [2 * (2 * dz + side) + n for n in range(CAP) for dz in distances]
        for side in (core, 1 - core)
        for distances in ((1, 3), (2,))
    ]

    def start_stage(number):
        for slot in stages[number]:
            amplitudes(slot).start()

    def end_stage(number):
        for slot in stages[number]:
            amplitudes(slot).wait_send()

    load_meta.start()
    pl.semaphore_wait(barrier, len(peers))
    for r in range(1, OWNERS):
        metas(r).start()
    start_stage(0)
    for slot in (2, 3):
        amplitudes(slot).start()
    load_own.start()
    for copy in loads:
        copy.start()
    edge = jnp.zeros((2, STRIP, HALF), F32)
    for n in range(3 * SLOTS):
        pads[n, :, pl.ds(0, STRIP), :] = edge
        pads[n, :, pl.ds(STRIP + SIDE, STRIP), :] = edge
    pads[3 * SLOTS] = jnp.zeros((2, SPAN + STRIP, HALF), F32)
    part[...] = jnp.zeros_like(part)

    def take_corners(pair):
        if pair:
            metas(2 * pair).wait_recv()
            metas(2 * pair + 1).wait_recv()
        else:
            load_meta.wait()
            metas(1).wait_recv()
        rows = pl.ds(2 * pair, 2)
        copy = pltpu.make_async_copy(got_meta.at[rows], corners.at[rows], load.at[BLOCKS + 3])
        copy.start()
        copy.wait()

    take_corners(0)
    for copy in loads:
        copy.wait()
    load_own.wait()

    lane = lax.broadcasted_iota(jnp.int32, (SIDE, HALF), 1)

    def corner(slot):
        r = slot // CAP
        at = 4 * lax.rem(slot, CAP)
        row = jnp.clip(corners[r, at + 1, 0] - base, 0, STRIP)
        col = jnp.clip(corners[r, at + 2, 0], 0, TILE - SIDE)
        start = jnp.minimum(col // HALF, BLOCKS - 3)
        return row, start, col - start * HALF

    def window(slot, part):
        row, start, shift = corner(slot)
        unshift = lax.rem(HALF - shift, HALF)
        turned = [
            pltpu.roll(strip[part, start + n, pl.ds(row, SIDE), :], unshift, axis=1) for n in range(3)
        ]
        inner = lane < HALF - shift
        return beside(jnp.where(inner, turned[0], turned[1]), jnp.where(inner, turned[1], turned[2]))

    def from_pair(k, carry):
        dz = jnp.where(k >= 6, 2, jnp.where(lax.rem(k, 2) == 0, 1, 3))
        n = jnp.where(k >= 6, k - 6, (k - 2) // 2)
        one = jnp.where(k < 2, 2 * k, 4 * dz + n)
        two = jnp.where(k < 2, 2 * k + 1, 4 * dz + 2 + n)

        for side, turn, number in ((0, 4, 0), (1, 2, 0), (1, 2, 1), (1, 4, 2)):

            @pl.when((core == side) & (k == turn))
            def _():
                end_stage(number)
                start_stage(number + 1)

        @pl.when((core == 0) & (k == 6))
        def _():
            start_stage(2)

        for pair, turn in ((1, 2), (3, 3), (2, 6)):

            @pl.when(k == turn)
            def _():
                take_corners(pair)

        @pl.when(k > 0)
        def _():
            amplitudes(one).wait_recv()
            amplitudes(two).wait_recv()

        slots = [one, two]
        probe_re = probe_ref[0]
        probe_im = probe_ref[1]
        windows = [(window(slot, 0), window(slot, 1)) for slot in slots]
        exits = [
            (probe_re * re - probe_im * im, probe_re * im + probe_im * re) for re, im in windows
        ]

        def wanted_rows(j, parity):
            return by_parity(
                beside(
                    got[slots[j] // CAP, lax.rem(slots[j], CAP), 0, pl.ds(parity, HALF, stride=2), :],
                    got[slots[j] // CAP, lax.rem(slots[j], CAP), 1, pl.ds(parity, HALF, stride=2), :],
                )
            )

        residuals = residual_waves(exits, wanted_rows, lambda i: (tables[i, 0], tables[i, 1]))
        part_re = part[pl.ds(0, SIDE), :]
        part_im = part[pl.ds(SIDE, SIDE), :]
        for j, slot in enumerate(slots):
            keep = corners[slot // CAP, 4 * lax.rem(slot, CAP), 0] > 0
            res_re = jnp.where(keep, residuals[j][0], 0.0)
            res_im = jnp.where(keep, residuals[j][1], 0.0)
            window_re, window_im = windows[j]
            part_re = part_re + (window_re * res_re + window_im * res_im)
            part_im = part_im + (window_re * res_im - window_im * res_re)
            shift = corner(slot)[2]
            turn = lax.rem(shift, HALF)
            outer = lane >= shift
            rows = pl.ds(STRIP, SIDE)
            for c, value in (
                (0, probe_re * res_re + probe_im * res_im),
                (1, probe_re * res_im - probe_im * res_re),
            ):
                first = pltpu.roll(value[:, FRONT], turn, axis=1)
                second = pltpu.roll(value[:, BACK], turn, axis=1)
                pads[3 * slot, c, rows, :] = jnp.where(outer, first, 0.0)
                pads[3 * slot + 1, c, rows, :] = jnp.where(outer, second, first)
                pads[3 * slot + 2, c, rows, :] = jnp.where(outer, 0.0, second)
        part[pl.ds(0, SIDE), :] = part_re
        part[pl.ds(SIDE, SIDE), :] = part_im
        return carry

    lax.fori_loop(0, OWNERS, from_pair, 0)

    def eighth(number):
        return pl.ds(pl.multiple_of(number * 64, 64), 64)

    def sixteen(number):
        return pl.ds(pl.multiple_of(number * 16, 16), 16)

    mine = pl.ds(pl.multiple_of(me * 64 + y * 16, 16), 16)

    def stage_a(r):
        return remote(part.at[eighth(obj_at(r))], near.at[r], send_a.at[r], recv_a.at[r], obj_peer(r))

    def stage_b(k):
        there = lax.rem(y + k, NY)
        return remote(near.at[0, sixteen(there)], quarter.at[k], send_b.at[k], recv_b.at[k], y_peer(k))

    def stage_c(k):
        return remote(sixteenth.at[x], sixteenth.at[x], send_c.at[k], recv_c.at[k], x_peer(k))

    def stage_d(k):
        return remote(total_ref.at[mine], total_ref.at[mine], send_d.at[k], recv_d.at[k], y_peer(k))

    def stage_e(r):
        return remote(
            total_ref.at[eighth(me)], total_ref.at[eighth(me)], send_e.at[r], recv_e.at[r], obj_peer(r)
        )

    def probe_step(number):
        if number == 0:
            for r in range(1, OWNERS):
                stage_a(r).wait()
            value = part[eighth(me), :]
            for r in range(1, OWNERS):
                value = value + near[r]
            near[0] = value
            for k in range(1, NY):
                stage_b(k).start()
        elif number == 1:
            for k in range(1, NY):
                stage_b(k).wait()
            value = near[0, sixteen(y), :]
            for k in range(1, NY):
                value = value + quarter[k]
            sixteenth[x] = value
            for k in range(1, NX):
                stage_c(k).start()
        elif number == 2:
            for k in range(1, NX):
                stage_c(k).wait()
            value = (sixteenth[0] + sixteenth[1]) + (sixteenth[2] + sixteenth[3])
            total_ref[mine, :] = value * (1.0 / math.sqrt(1024.0))
            for k in range(1, NY):
                stage_d(k).start()
        elif number == 3:
            for k in range(1, NY):
                stage_d(k).wait()
            for r in range(1, OWNERS):
                stage_e(r).start()
        else:
            for r in range(1, OWNERS):
                stage_e(r).wait()

    for r in range(1, OWNERS):
        stage_a(r).start()

    def block(number):
        return pl.ds(pl.multiple_of(number * STRIP, STRIP), STRIP)

    def along_x(c, k):
        number = jnp.where(last, lax.rem(x + k, NX) + 1, k)
        columns = pl.ds(c * CHUNK, CHUNK)
        return remote(
            grad.at[:, columns, block(number)],
            got_x.at[k - 1, :, columns],
            send_x.at[k - 1, c],
            recv_x.at[k - 1, c],
            x_peer(k),
        )

    def along_y(c):
        columns = pl.ds(c * CHUNK, CHUNK)
        return remote(rise.at[:, columns], got_y.at[:, columns], send_y.at[c], recv_y.at[c], y_peer(1))

    def gather_chunk(c, carry):
        def gather_block(b, carry):
            for part in range(2):
                value = None
                for slot in range(SLOTS):
                    row, start, _ = corner(slot)
                    n = b - start
                    at = jnp.where((n >= 0) & (n < 3), 3 * slot + n, 3 * SLOTS)
                    term = pads[at, part, pl.ds(STRIP - row, SPAN), :]
                    value = term if value is None else value + term
                grad[part, b] = value
            return carry

        lax.fori_loop(c * CHUNK, (c + 1) * CHUNK, gather_block, 0)
        for k in (2, 1, 3):
            along_x(c, k).start()
        return carry

    lax.fori_loop(0, CHUNKS // 2, gather_chunk, 0)

    @pl.when(core == 0)
    def _():
        end_stage(1)
        end_stage(2)
        start_stage(3)

    @pl.when(core == 1)
    def _():
        probe_step(0)
        probe_step(1)

    lax.fori_loop(CHUNKS // 2, CHUNKS, gather_chunk, 0)


    own_block = block(jnp.where(last, x + 1, 0))
    for c in range(CHUNKS):
        columns = pl.ds(c * CHUNK, CHUNK)
        for k in range(1, NX):
            along_x(c, k).wait_recv()
        here_too = grad[:, columns, own_block, :]
        above_too = grad[:, columns, block(4), :]
        for k in range(1, NX):
            arrived = got_x[k - 1, :, columns]
            here = (k <= x) | last
            here_too = here_too + jnp.where(here, arrived, 0.0)
            above_too = above_too + jnp.where(here, 0.0, arrived)
        own[:, columns] = here_too
        rise[:, columns] = above_too

        @pl.when(y < NY - 1)
        def _():
            along_y(c).start()

        if c in (6, 8):

            @pl.when(core == 1)
            def _():
                probe_step(c // 2 - 1)

    for c in range(CHUNKS):

        @pl.when(y > 0)
        def _():
            along_y(c).wait_recv()
            for n in range(c * CHUNK, (c + 1) * CHUNK):
                out_ref[:, :, pl.ds(n * HALF, HALF)] = own[:, n] + got_y[:, n]

        @pl.when(y == 0)
        def _():
            for n in range(c * CHUNK, (c + 1) * CHUNK):
                out_ref[:, :, pl.ds(n * HALF, HALF)] = own[:, n]

        @pl.when(y < NY - 1)
        def _():
            along_y(c).wait_send()

    @pl.when(core == 0)
    def _():
        for number in range(4):
            probe_step(number)

    for r in range(1, OWNERS):
        metas(r).wait_send()
    for slot in (2, 3):
        amplitudes(slot).wait_send()
    end_stage(3)
    for c in range(CHUNKS):
        for k in range(1, NX):
            along_x(c, k).wait_send()
    probe_step(4)


def step(packed, meta, object_field, probe, tables):
    dma = pltpu.SemaphoreType.DMA
    return pl.pallas_call(
        step_kernel,
        out_shape=(
            jax.ShapeDtypeStruct((2, STRIP, TILE), F32),
            jax.ShapeDtypeStruct((2 * SIDE, SIDE), F32),
        ),
        in_specs=[HBM, HBM, HBM, HBM, HBM],
        out_specs=(VMEM, VMEM),
        scratch_shapes=[
            pltpu.VMEM((2, SIDE, SIDE), F32),
            pltpu.VMEM((OWNERS, CAP, 2, SIDE, HALF), F32),
            pltpu.VMEM((OWNERS, 8, 128), jnp.int32),
            pltpu.SMEM((OWNERS, 8, 128), jnp.int32),
            pltpu.VMEM((2, BLOCKS, SPAN, HALF), F32),
            pltpu.VMEM(tables.shape, BF16),
            pltpu.VMEM((3 * SLOTS + 1, 2, SPAN + STRIP, HALF), F32),
            pltpu.VMEM((2 * SIDE, SIDE), F32),
            pltpu.VMEM((2, BLOCKS, SPAN, HALF), F32),
            pltpu.VMEM((NX - 1, 2, BLOCKS, STRIP, HALF), F32),
            pltpu.VMEM((2, BLOCKS, STRIP, HALF), F32),
            pltpu.VMEM((2, BLOCKS, STRIP, HALF), F32),
            pltpu.VMEM((2, BLOCKS, STRIP, HALF), F32),
            pltpu.VMEM((OWNERS, 64, SIDE), F32),
            pltpu.VMEM((NY, 16, SIDE), F32),
            pltpu.VMEM((NX, 16, SIDE), F32),
            dma((BLOCKS + 5,)),
            dma((SLOTS,)),
            dma((SLOTS,)),
            dma((OWNERS,)),
            dma((OWNERS,)),
            dma((NX - 1, CHUNKS)),
            dma((NX - 1, CHUNKS)),
            dma((CHUNKS,)),
            dma((CHUNKS,)),
            dma((OWNERS,)),
            dma((OWNERS,)),
            dma((NY,)),
            dma((NY,)),
            dma((NX,)),
            dma((NX,)),
            dma((NY,)),
            dma((NY,)),
            dma((OWNERS,)),
            dma((OWNERS,)),
        ],
        compiler_params=pltpu.CompilerParams(
            collective_id=0, has_side_effects=True, vmem_limit_bytes=51 * 2**20
        ),
        name="step",
    )(packed, meta, object_field, probe, tables)


def on_device(object_field, probe, amplitude, tile_owner, row_start, col_start):
    tables = jnp.asarray(dft_tables())
    packed, meta = pack(tile_owner, row_start, col_start, amplitude)
    object_grad, probe_grad = step(packed, meta, object_field, probe, tables)
    return object_grad, probe_grad.reshape(2, SIDE, SIDE)


def solution(mesh):
    return jax.shard_map(
        on_device,
        mesh=mesh,
        in_specs=(
            P(None, None, "obj"),
            P(),
            P(("pat", "obj"), None, None),
            P(("pat", "obj"), None),
            P(("pat", "obj")),
            P(("pat", "obj")),
        ),
        out_specs=(P(None, "pat", "obj"), P()),
        check_vma=False,
    )
```

```python
import math

import jax
import jax.numpy as jnp
import numpy as np
from jax import lax
from jax.experimental import pallas as pl
from jax.experimental.pallas import tpu as pltpu
from jax.sharding import PartitionSpec as P

MESH = pl.DeviceIdType.MESH
CAP = 2
SIDE = 256
HALF = 128
STRIP = 64
SPAN = 320
TILE = 2048
BLOCKS = TILE // HALF
SOFTEN = 0.25
OWNERS = 8
COUNT = 8
SPARE = 4096
SLOTS = OWNERS * CAP
NX = 4
NY = 4
CHUNKS = 16
CHUNK = BLOCKS // CHUNKS
F32 = jnp.float32
BF16 = jnp.bfloat16
HBM = pl.BlockSpec(memory_space=pltpu.HBM)
VMEM = pl.BlockSpec(memory_space=pltpu.VMEM)
SMEM = pl.BlockSpec(memory_space=pltpu.SMEM)


def dft_tables():
    index = np.arange(SIDE)
    full = np.exp(-2j * np.pi * (np.outer(index, index) % SIDE) / SIDE) / math.sqrt(SIDE)

    def right(table):
        return np.block([[table.real, table.imag], [-table.imag, table.real]])

    swap = np.roll(np.arange(HALF), -HALF // 2)
    half = [full[:HALF, 0::2], full[:HALF, 1::2]]
    lane = [half[0], half[1][:, swap]]
    tables = [
        right(lane[0]),
        right(lane[1]),
        right(half[0]).T,
        right(half[1]).T,
        right(half[0].conj().T).T,
        right(half[1].conj().T).T,
        right(lane[0].conj().T),
        right(lane[1].conj().T),
    ]
    exact = np.stack(tables).astype(np.float32)
    high = exact.astype(BF16)
    low = (exact - high.astype(np.float32)).astype(BF16)
    return np.stack([high, low], axis=1)


def split(value):
    high = value.astype(BF16)
    return high, (value - high.astype(F32)).astype(BF16)


def times_table(data, table):
    high, low = split(data)
    left = jnp.concatenate([high, low, high], axis=1)
    right = jnp.concatenate([table[0], table[0], table[1]], axis=0)
    return jnp.dot(left, right, preferred_element_type=F32)


def table_times(table, data):
    high, low = split(data)
    left = jnp.concatenate([table[0], table[0], table[1]], axis=1)
    right = jnp.concatenate([high, low, high], axis=0)
    return jnp.dot(left, right, preferred_element_type=F32)


def beside(*parts):
    return jnp.concatenate(parts, axis=1)


def above(*parts):
    return jnp.concatenate(parts, axis=0)


def by_parity(rows):
    lane = lax.broadcasted_iota(jnp.int32, (HALF, HALF), 1)
    front = lane < HALF // 2
    first = jnp.take_along_axis(
        rows[:, :HALF], jnp.where(front, 2 * lane, 2 * lane - HALF + 1), axis=1, mode="promise_in_bounds"
    )
    second = jnp.take_along_axis(
        rows[:, HALF:], jnp.where(front, 2 * lane + 1, 2 * lane - HALF), axis=1, mode="promise_in_bounds"
    )
    return beside(jnp.where(front, first, second), jnp.where(front, second, first))


FRONT = slice(0, HALF)
BACK = slice(HALF, SIDE)


def residual_waves(exits, wanted_rows, tables):
    count = len(exits)

    def from_right(waves, number):
        out = times_table(above(*waves), tables(number))
        return [out[SIDE * j : SIDE * (j + 1)] for j in range(count)]

    def from_left(number, waves):
        out = table_times(tables(number), beside(*waves))
        return [out[:, SIDE * j : SIDE * (j + 1)] for j in range(count)]

    even = from_right(
        [beside(re[:, FRONT] + re[:, BACK], im[:, FRONT] + im[:, BACK]) for re, im in exits], 0
    )
    odd = from_right(
        [beside(re[:, FRONT] - re[:, BACK], im[:, FRONT] - im[:, BACK]) for re, im in exits], 1
    )
    half_re = [beside(e[:, FRONT], o[:, FRONT]) for e, o in zip(even, odd)]
    half_im = [beside(e[:, BACK], o[:, BACK]) for e, o in zip(even, odd)]
    pairs = list(zip(half_re, half_im))
    spectrum = [
        from_left(2, [above(re[FRONT] + re[BACK], im[FRONT] + im[BACK]) for re, im in pairs]),
        from_left(3, [above(re[FRONT] - re[BACK], im[FRONT] - im[BACK]) for re, im in pairs]),
    ]
    returned = []
    for parity in range(2):
        scaled = []
        for j in range(count):
            re, im = spectrum[parity][j][FRONT], spectrum[parity][j][BACK]
            ratio = wanted_rows(j, parity) * lax.rsqrt(re * re + im * im + SOFTEN)
            scaled.append(above(re * ratio, im * ratio))
        returned.append(from_left(4 + parity, scaled))
    pairs = []
    for e, o in zip(*returned):
        re = above(e[FRONT] + o[FRONT], e[FRONT] - o[FRONT])
        im = above(e[BACK] + o[BACK], e[BACK] - o[BACK])
        pairs.append((re, im))
    even = from_right([beside(re[:, FRONT], im[:, FRONT]) for re, im in pairs], 6)
    odd = from_right([beside(re[:, BACK], im[:, BACK]) for re, im in pairs], 7)
    residuals = []
    for (re, im), e, o in zip(exits, even, odd):
        back_re = beside(e[:, FRONT] + o[:, FRONT], e[:, FRONT] - o[:, FRONT])
        back_im = beside(e[:, BACK] + o[:, BACK], e[:, BACK] - o[:, BACK])
        residuals.append((back_re - re, back_im - im))
    return residuals


def pack_kernel(
    owner_ref, row_ref, col_ref, amp_ref, probe_ref, packed_ref, corners_ref, held, waves, meta_ref, come, leave
):
    def arriving(j, side):
        return pltpu.make_async_copy(
            amp_ref.at[j, :, pl.ds(side * HALF, HALF)], held.at[j, side], come.at[j, side]
        )

    def arriving_probe(part, side):
        return pltpu.make_async_copy(
            probe_ref.at[part, :, pl.ds(side * HALF, HALF)], waves.at[part, side], come.at[COUNT + part, side]
        )

    for j in range(COUNT):
        for side in range(2):
            arriving(j, side).start()
    for part in range(2):
        for side in range(2):
            arriving_probe(part, side).start()
    ranks = []
    for j in range(COUNT):
        rank = jnp.int32(0)
        for i in range(j):
            rank = rank + (owner_ref[0, i] == owner_ref[0, j]).astype(jnp.int32)
        ranks.append(rank)
    meta_ref[...] = jnp.zeros_like(meta_ref)
    sub = lax.broadcasted_iota(jnp.int32, (8, 128), 0)
    for j in range(COUNT):
        mine = (sub // 4 == ranks[j]) & (sub % 4 < 3)
        value = jnp.where(sub % 4 == 0, 1, jnp.where(sub % 4 == 1, row_ref[j], col_ref[j]))
        meta_ref[owner_ref[0, j]] = jnp.where(mine, value, meta_ref[owner_ref[0, j]])
    leaving = [pltpu.make_async_copy(meta_ref, corners_ref.at[pl.ds(0, OWNERS)], leave.at[COUNT])]
    leaving[0].start()
    for j in range(COUNT):
        for side in range(2):
            arriving(j, side).wait()
        copy = pltpu.make_async_copy(held.at[j], packed_ref.at[owner_ref[0, j], ranks[j]], leave.at[j])
        copy.start()
        leaving.append(copy)
    for part in range(2):
        for side in range(2):
            arriving_probe(part, side).wait()
    copy = pltpu.make_async_copy(waves, packed_ref.at[OWNERS], leave.at[COUNT + 1])
    copy.start()
    leaving.append(copy)
    for copy in leaving:
        copy.wait()


def pack(tile_owner, row_start, col_start, amplitude, probe):
    return pl.pallas_call(
        pack_kernel,
        out_shape=(
            jax.ShapeDtypeStruct((OWNERS + 1, CAP, 2, SIDE, HALF), F32),
            jax.ShapeDtypeStruct((SPARE, 8, 128), jnp.int32),
        ),
        in_specs=[SMEM, SMEM, SMEM, HBM, HBM],
        out_specs=(HBM, HBM),
        scratch_shapes=[
            pltpu.VMEM((COUNT, 2, SIDE, HALF), F32),
            pltpu.VMEM((2, 2, SIDE, HALF), F32),
            pltpu.VMEM((OWNERS, 8, 128), jnp.int32),
            pltpu.SemaphoreType.DMA((COUNT + 2, 2)),
            pltpu.SemaphoreType.DMA((COUNT + 2,)),
        ],
        name="pack",
    )(tile_owner.T, row_start, col_start, amplitude, probe)


def step_kernel(
    packed_ref, meta_ref, object_ref, tables_ref, out_ref, total_ref,
    probe_ref, got, got_meta, corners, strip, tables, pads, part, grad, got_x, got_y, own, rise, near, quarter, sixteenth,
    load, send, recv, send_meta, recv_meta, send_x, recv_x, send_y, recv_y,
    send_a, recv_a, send_b, recv_b, send_c, recv_c, send_d, recv_d, send_e, recv_e,
):
    me = lax.axis_index("obj")
    z = me // 2
    core = lax.rem(me, 2)
    group = lax.axis_index("pat")
    x = lax.rem(group, NX)
    y = group // NX
    last = y == NY - 1
    base = pl.multiple_of(jnp.minimum(group, 11) * STRIP, STRIP)

    def obj_at(r):
        return lax.rem(z + r // 2, OWNERS // 2) * 2 + lax.rem(core + lax.rem(r, 2), 2)

    def obj_peer(r):
        return {"obj": obj_at(r)}

    def x_peer(k):
        return {"pat": y * NX + lax.rem(x + k, NX)}

    def y_peer(k):
        return {"pat": lax.rem(y + k, NY) * NX + x}

    def remote(src, dst, send, recv, peer):
        return pltpu.make_async_remote_copy(
            src_ref=src, dst_ref=dst, send_sem=send, recv_sem=recv, device_id=peer, device_id_type=MESH
        )

    peers = [obj_peer(r) for r in range(1, OWNERS)]
    peers += [x_peer(k) for k in range(1, NX)] + [y_peer(k) for k in range(1, NY)]
    barrier = pltpu.get_barrier_semaphore()
    for peer in peers:
        pl.semaphore_signal(barrier, inc=1, device_id=peer, device_id_type=MESH)

    loads = [
        pltpu.make_async_copy(
            object_ref.at[:, pl.ds(base, SPAN), pl.ds(n * HALF, HALF)], strip.at[:, n], load.at[n]
        )
        for n in range(BLOCKS)
    ]
    loads.append(pltpu.make_async_copy(tables_ref, tables, load.at[BLOCKS]))
    loads.append(pltpu.make_async_copy(packed_ref.at[OWNERS], probe_ref, load.at[BLOCKS + 4]))
    load_meta = pltpu.make_async_copy(meta_ref.at[me], got_meta.at[0], load.at[BLOCKS + 1])
    load_own = pltpu.make_async_copy(packed_ref.at[me], got.at[0], load.at[BLOCKS + 2])

    def metas(r):
        return remote(meta_ref.at[obj_at(r)], got_meta.at[r], send_meta.at[r], recv_meta.at[r], obj_peer(r))

    def amplitudes(slot):
        r = slot // CAP
        n = lax.rem(slot, CAP)
        return remote(
            packed_ref.at[obj_at(r), n], got.at[r, n], send.at[slot], recv.at[slot], obj_peer(r)
        )

    stages = [
        [2 * (2 * dz + side) + n for n in range(CAP) for dz in distances]
        for side in (core, 1 - core)
        for distances in ((1, 3), (2,))
    ]

    def start_stage(number):
        for slot in stages[number]:
            amplitudes(slot).start()

    def end_stage(number):
        for slot in stages[number]:
            amplitudes(slot).wait_send()

    load_meta.start()
    pl.semaphore_wait(barrier, len(peers))
    for r in range(1, OWNERS):
        metas(r).start()
    start_stage(0)
    for slot in (2, 3):
        amplitudes(slot).start()
    load_own.start()
    for copy in loads:
        copy.start()
    edge = jnp.zeros((2, STRIP, HALF), F32)
    for n in range(3 * SLOTS):
        pads[n, :, pl.ds(0, STRIP), :] = edge
        pads[n, :, pl.ds(STRIP + SIDE, STRIP), :] = edge
    pads[3 * SLOTS] = jnp.zeros((2, SPAN + STRIP, HALF), F32)
    part[...] = jnp.zeros_like(part)

    def take_corners(pair):
        if pair:
            metas(2 * pair).wait_recv()
            metas(2 * pair + 1).wait_recv()
        else:
            load_meta.wait()
            metas(1).wait_recv()
        rows = pl.ds(2 * pair, 2)
        copy = pltpu.make_async_copy(got_meta.at[rows], corners.at[rows], load.at[BLOCKS + 3])
        copy.start()
        copy.wait()

    take_corners(0)
    for copy in loads:
        copy.wait()
    load_own.wait()

    lane = lax.broadcasted_iota(jnp.int32, (SIDE, HALF), 1)

    def corner(slot):
        r = slot // CAP
        at = 4 * lax.rem(slot, CAP)
        row = jnp.clip(corners[r, at + 1, 0] - base, 0, STRIP)
        col = jnp.clip(corners[r, at + 2, 0], 0, TILE - SIDE)
        start = jnp.minimum(col // HALF, BLOCKS - 3)
        return row, start, col - start * HALF

    def window(slot, part):
        row, start, shift = corner(slot)
        unshift = lax.rem(HALF - shift, HALF)
        turned = [
            pltpu.roll(strip[part, start + n, pl.ds(row, SIDE), :], unshift, axis=1) for n in range(3)
        ]
        inner = lane < HALF - shift
        return beside(jnp.where(inner, turned[0], turned[1]), jnp.where(inner, turned[1], turned[2]))

    def from_pair(k, carry):
        dz = jnp.where(k >= 6, 2, jnp.where(lax.rem(k, 2) == 0, 1, 3))
        n = jnp.where(k >= 6, k - 6, (k - 2) // 2)
        one = jnp.where(k < 2, 2 * k, 4 * dz + n)
        two = jnp.where(k < 2, 2 * k + 1, 4 * dz + 2 + n)

        for side, turn, number in ((0, 4, 0), (1, 2, 0), (1, 2, 1), (1, 4, 2)):

            @pl.when((core == side) & (k == turn))
            def _():
                end_stage(number)
                start_stage(number + 1)

        @pl.when((core == 0) & (k == 6))
        def _():
            start_stage(2)

        for pair, turn in ((1, 2), (3, 3), (2, 6)):

            @pl.when(k == turn)
            def _():
                take_corners(pair)

        @pl.when(k > 0)
        def _():
            amplitudes(one).wait_recv()
            amplitudes(two).wait_recv()

        slots = [one, two]
        probe_re = beside(probe_ref[0, 0], probe_ref[0, 1])
        probe_im = beside(probe_ref[1, 0], probe_ref[1, 1])
        windows = [(window(slot, 0), window(slot, 1)) for slot in slots]
        exits = [
            (probe_re * re - probe_im * im, probe_re * im + probe_im * re) for re, im in windows
        ]

        def wanted_rows(j, parity):
            return by_parity(
                beside(
                    got[slots[j] // CAP, lax.rem(slots[j], CAP), 0, pl.ds(parity, HALF, stride=2), :],
                    got[slots[j] // CAP, lax.rem(slots[j], CAP), 1, pl.ds(parity, HALF, stride=2), :],
                )
            )

        residuals = residual_waves(exits, wanted_rows, lambda i: (tables[i, 0], tables[i, 1]))
        part_re = part[pl.ds(0, SIDE), :]
        part_im = part[pl.ds(SIDE, SIDE), :]
        for j, slot in enumerate(slots):
            keep = corners[slot // CAP, 4 * lax.rem(slot, CAP), 0] > 0
            res_re = jnp.where(keep, residuals[j][0], 0.0)
            res_im = jnp.where(keep, residuals[j][1], 0.0)
            window_re, window_im = windows[j]
            part_re = part_re + (window_re * res_re + window_im * res_im)
            part_im = part_im + (window_re * res_im - window_im * res_re)
            shift = corner(slot)[2]
            turn = lax.rem(shift, HALF)
            outer = lane >= shift
            rows = pl.ds(STRIP, SIDE)
            for c, value in (
                (0, probe_re * res_re + probe_im * res_im),
                (1, probe_re * res_im - probe_im * res_re),
            ):
                first = pltpu.roll(value[:, FRONT], turn, axis=1)
                second = pltpu.roll(value[:, BACK], turn, axis=1)
                pads[3 * slot, c, rows, :] = jnp.where(outer, first, 0.0)
                pads[3 * slot + 1, c, rows, :] = jnp.where(outer, second, first)
                pads[3 * slot + 2, c, rows, :] = jnp.where(outer, 0.0, second)
        part[pl.ds(0, SIDE), :] = part_re
        part[pl.ds(SIDE, SIDE), :] = part_im
        return carry

    lax.fori_loop(0, OWNERS, from_pair, 0)

    def eighth(number):
        return pl.ds(pl.multiple_of(number * 64, 64), 64)

    def sixteen(number):
        return pl.ds(pl.multiple_of(number * 16, 16), 16)

    mine = pl.ds(pl.multiple_of(me * 64 + y * 16, 16), 16)

    def stage_a(r):
        return remote(part.at[eighth(obj_at(r))], near.at[r], send_a.at[r], recv_a.at[r], obj_peer(r))

    def stage_b(k):
        there = lax.rem(y + k, NY)
        return remote(near.at[0, sixteen(there)], quarter.at[k], send_b.at[k], recv_b.at[k], y_peer(k))

    def stage_c(k):
        return remote(sixteenth.at[x], sixteenth.at[x], send_c.at[k], recv_c.at[k], x_peer(k))

    def stage_d(k):
        return remote(total_ref.at[mine], total_ref.at[mine], send_d.at[k], recv_d.at[k], y_peer(k))

    def stage_e(r):
        return remote(
            total_ref.at[eighth(me)], total_ref.at[eighth(me)], send_e.at[r], recv_e.at[r], obj_peer(r)
        )

    def probe_step(number):
        if number == 0:
            for r in range(1, OWNERS):
                stage_a(r).wait()
            value = part[eighth(me), :]
            for r in range(1, OWNERS):
                value = value + near[r]
            near[0] = value
            for k in range(1, NY):
                stage_b(k).start()
        elif number == 1:
            for k in range(1, NY):
                stage_b(k).wait()
            value = near[0, sixteen(y), :]
            for k in range(1, NY):
                value = value + quarter[k]
            sixteenth[x] = value
            for k in range(1, NX):
                stage_c(k).start()
        elif number == 2:
            for k in range(1, NX):
                stage_c(k).wait()
            value = (sixteenth[0] + sixteenth[1]) + (sixteenth[2] + sixteenth[3])
            total_ref[mine, :] = value * (1.0 / math.sqrt(1024.0))
            for k in range(1, NY):
                stage_d(k).start()
        elif number == 3:
            for k in range(1, NY):
                stage_d(k).wait()
            for r in range(1, OWNERS):
                stage_e(r).start()
        else:
            for r in range(1, OWNERS):
                stage_e(r).wait()

    for r in range(1, OWNERS):
        stage_a(r).start()

    def block(number):
        return pl.ds(pl.multiple_of(number * STRIP, STRIP), STRIP)

    def along_x(c, k):
        number = jnp.where(last, lax.rem(x + k, NX) + 1, k)
        columns = pl.ds(c * CHUNK, CHUNK)
        return remote(
            grad.at[:, columns, block(number)],
            got_x.at[k - 1, :, columns],
            send_x.at[k - 1, c],
            recv_x.at[k - 1, c],
            x_peer(k),
        )

    def along_y(c):
        columns = pl.ds(c * CHUNK, CHUNK)
        return remote(rise.at[:, columns], got_y.at[:, columns], send_y.at[c], recv_y.at[c], y_peer(1))

    def gather_chunk(c, carry):
        def gather_block(b, carry):
            for part in range(2):
                value = None
                for slot in range(SLOTS):
                    row, start, _ = corner(slot)
                    n = b - start
                    at = jnp.where((n >= 0) & (n < 3), 3 * slot + n, 3 * SLOTS)
                    term = pads[at, part, pl.ds(STRIP - row, SPAN), :]
                    value = term if value is None else value + term
                grad[part, b] = value
            return carry

        lax.fori_loop(c * CHUNK, (c + 1) * CHUNK, gather_block, 0)
        for k in (2, 1, 3):
            along_x(c, k).start()
        return carry

    lax.fori_loop(0, CHUNKS // 2, gather_chunk, 0)

    @pl.when(core == 0)
    def _():
        end_stage(1)
        end_stage(2)
        start_stage(3)

    @pl.when(core == 1)
    def _():
        probe_step(0)
        probe_step(1)

    lax.fori_loop(CHUNKS // 2, CHUNKS, gather_chunk, 0)


    own_block = block(jnp.where(last, x + 1, 0))
    for c in range(CHUNKS):
        columns = pl.ds(c * CHUNK, CHUNK)
        for k in range(1, NX):
            along_x(c, k).wait_recv()
        here_too = grad[:, columns, own_block, :]
        above_too = grad[:, columns, block(4), :]
        for k in range(1, NX):
            arrived = got_x[k - 1, :, columns]
            here = (k <= x) | last
            here_too = here_too + jnp.where(here, arrived, 0.0)
            above_too = above_too + jnp.where(here, 0.0, arrived)
        own[:, columns] = here_too
        rise[:, columns] = above_too

        @pl.when(y < NY - 1)
        def _():
            along_y(c).start()

        if c in (6, 8):

            @pl.when(core == 1)
            def _():
                probe_step(c // 2 - 1)

    for c in range(CHUNKS):

        @pl.when(y > 0)
        def _():
            along_y(c).wait_recv()
            for n in range(c * CHUNK, (c + 1) * CHUNK):
                out_ref[:, :, pl.ds(n * HALF, HALF)] = own[:, n] + got_y[:, n]

        @pl.when(y == 0)
        def _():
            for n in range(c * CHUNK, (c + 1) * CHUNK):
                out_ref[:, :, pl.ds(n * HALF, HALF)] = own[:, n]

        @pl.when(y < NY - 1)
        def _():
            along_y(c).wait_send()

    @pl.when(core == 0)
    def _():
        for number in range(4):
            probe_step(number)

    for r in range(1, OWNERS):
        metas(r).wait_send()
    for slot in (2, 3):
        amplitudes(slot).wait_send()
    end_stage(3)
    for c in range(CHUNKS):
        for k in range(1, NX):
            along_x(c, k).wait_send()
    probe_step(4)


def step(packed, meta, object_field, tables):
    dma = pltpu.SemaphoreType.DMA
    return pl.pallas_call(
        step_kernel,
        out_shape=(
            jax.ShapeDtypeStruct((2, STRIP, TILE), F32),
            jax.ShapeDtypeStruct((2 * SIDE, SIDE), F32),
        ),
        in_specs=[HBM, HBM, HBM, HBM],
        out_specs=(VMEM, VMEM),
        scratch_shapes=[
            pltpu.VMEM((2, 2, SIDE, HALF), F32),
            pltpu.VMEM((OWNERS, CAP, 2, SIDE, HALF), F32),
            pltpu.VMEM((OWNERS, 8, 128), jnp.int32),
            pltpu.SMEM((OWNERS, 8, 128), jnp.int32),
            pltpu.VMEM((2, BLOCKS, SPAN, HALF), F32),
            pltpu.VMEM(tables.shape, BF16),
            pltpu.VMEM((3 * SLOTS + 1, 2, SPAN + STRIP, HALF), F32),
            pltpu.VMEM((2 * SIDE, SIDE), F32),
            pltpu.VMEM((2, BLOCKS, SPAN, HALF), F32),
            pltpu.VMEM((NX - 1, 2, BLOCKS, STRIP, HALF), F32),
            pltpu.VMEM((2, BLOCKS, STRIP, HALF), F32),
            pltpu.VMEM((2, BLOCKS, STRIP, HALF), F32),
            pltpu.VMEM((2, BLOCKS, STRIP, HALF), F32),
            pltpu.VMEM((OWNERS, 64, SIDE), F32),
            pltpu.VMEM((NY, 16, SIDE), F32),
            pltpu.VMEM((NX, 16, SIDE), F32),
            dma((BLOCKS + 5,)),
            dma((SLOTS,)),
            dma((SLOTS,)),
            dma((OWNERS,)),
            dma((OWNERS,)),
            dma((NX - 1, CHUNKS)),
            dma((NX - 1, CHUNKS)),
            dma((CHUNKS,)),
            dma((CHUNKS,)),
            dma((OWNERS,)),
            dma((OWNERS,)),
            dma((NY,)),
            dma((NY,)),
            dma((NX,)),
            dma((NX,)),
            dma((NY,)),
            dma((NY,)),
            dma((OWNERS,)),
            dma((OWNERS,)),
        ],
        compiler_params=pltpu.CompilerParams(
            collective_id=0, has_side_effects=True, vmem_limit_bytes=51 * 2**20
        ),
        name="step",
    )(packed, meta, object_field, tables)


def on_device(object_field, probe, amplitude, tile_owner, row_start, col_start):
    tables = jnp.asarray(dft_tables())
    packed, meta = pack(tile_owner, row_start, col_start, amplitude, probe)
    object_grad, probe_grad = step(packed, meta, object_field, tables)
    return object_grad, probe_grad.reshape(2, SIDE, SIDE)


def solution(mesh):
    return jax.shard_map(
        on_device,
        mesh=mesh,
        in_specs=(
            P(None, None, "obj"),
            P(),
            P(("pat", "obj"), None, None),
            P(("pat", "obj"), None),
            P(("pat", "obj")),
            P(("pat", "obj")),
        ),
        out_specs=(P(None, "pat", "obj"), P()),
        check_vma=False,
    )
```

```python
import math

import jax
import jax.numpy as jnp
import numpy as np
from jax import lax
from jax.experimental import pallas as pl
from jax.experimental.pallas import tpu as pltpu
from jax.sharding import PartitionSpec as P

MESH = pl.DeviceIdType.MESH
CAP = 2
SIDE = 256
HALF = 128
STRIP = 64
SPAN = 320
TILE = 2048
BLOCKS = TILE // HALF
SOFTEN = 0.25
OWNERS = 8
COUNT = 8
SPARE = 4096
SLOTS = OWNERS * CAP
NX = 4
NY = 4
CHUNKS = 16
CHUNK = BLOCKS // CHUNKS
F32 = jnp.float32
BF16 = jnp.bfloat16
HBM = pl.BlockSpec(memory_space=pltpu.HBM)
VMEM = pl.BlockSpec(memory_space=pltpu.VMEM)
SMEM = pl.BlockSpec(memory_space=pltpu.SMEM)


def dft_tables():
    index = np.arange(SIDE)
    full = np.exp(-2j * np.pi * (np.outer(index, index) % SIDE) / SIDE) / math.sqrt(SIDE)

    def right(table):
        return np.block([[table.real, table.imag], [-table.imag, table.real]])

    swap = np.roll(np.arange(HALF), -HALF // 2)
    half = [full[:HALF, 0::2], full[:HALF, 1::2]]
    lane = [half[0], half[1][:, swap]]
    tables = [
        right(lane[0]),
        right(lane[1]),
        right(half[0]).T,
        right(half[1]).T,
        right(half[0].conj().T).T,
        right(half[1].conj().T).T,
        right(lane[0].conj().T),
        right(lane[1].conj().T),
    ]
    exact = np.stack(tables).astype(np.float32)
    high = exact.astype(BF16)
    low = (exact - high.astype(np.float32)).astype(BF16)
    return np.stack([high, low], axis=1)


def split(value):
    high = value.astype(BF16)
    return high, (value - high.astype(F32)).astype(BF16)


def times_table(data, table):
    high, low = split(data)
    left = jnp.concatenate([high, low, high], axis=1)
    right = jnp.concatenate([table[0], table[0], table[1]], axis=0)
    return jnp.dot(left, right, preferred_element_type=F32)


def table_times(table, data):
    high, low = split(data)
    left = jnp.concatenate([table[0], table[0], table[1]], axis=1)
    right = jnp.concatenate([high, low, high], axis=0)
    return jnp.dot(left, right, preferred_element_type=F32)


def beside(*parts):
    return jnp.concatenate(parts, axis=1)


def above(*parts):
    return jnp.concatenate(parts, axis=0)


def by_parity(rows):
    lane = lax.broadcasted_iota(jnp.int32, (HALF, HALF), 1)
    front = lane < HALF // 2
    first = jnp.take_along_axis(
        rows[:, :HALF], jnp.where(front, 2 * lane, 2 * lane - HALF + 1), axis=1, mode="promise_in_bounds"
    )
    second = jnp.take_along_axis(
        rows[:, HALF:], jnp.where(front, 2 * lane + 1, 2 * lane - HALF), axis=1, mode="promise_in_bounds"
    )
    return beside(jnp.where(front, first, second), jnp.where(front, second, first))


FRONT = slice(0, HALF)
BACK = slice(HALF, SIDE)


def residual_waves(exits, wanted_rows, tables):
    count = len(exits)

    def from_right(waves, number):
        out = times_table(above(*waves), tables(number))
        return [out[SIDE * j : SIDE * (j + 1)] for j in range(count)]

    def from_left(number, waves):
        out = table_times(tables(number), beside(*waves))
        return [out[:, SIDE * j : SIDE * (j + 1)] for j in range(count)]

    even = from_right(
        [beside(re[:, FRONT] + re[:, BACK], im[:, FRONT] + im[:, BACK]) for re, im in exits], 0
    )
    odd = from_right(
        [beside(re[:, FRONT] - re[:, BACK], im[:, FRONT] - im[:, BACK]) for re, im in exits], 1
    )
    half_re = [beside(e[:, FRONT], o[:, FRONT]) for e, o in zip(even, odd)]
    half_im = [beside(e[:, BACK], o[:, BACK]) for e, o in zip(even, odd)]
    pairs = list(zip(half_re, half_im))
    spectrum = [
        from_left(2, [above(re[FRONT] + re[BACK], im[FRONT] + im[BACK]) for re, im in pairs]),
        from_left(3, [above(re[FRONT] - re[BACK], im[FRONT] - im[BACK]) for re, im in pairs]),
    ]
    returned = []
    for parity in range(2):
        scaled = []
        for j in range(count):
            re, im = spectrum[parity][j][FRONT], spectrum[parity][j][BACK]
            ratio = wanted_rows(j, parity) * lax.rsqrt(re * re + im * im + SOFTEN)
            scaled.append(above(re * ratio, im * ratio))
        returned.append(from_left(4 + parity, scaled))
    pairs = []
    for e, o in zip(*returned):
        re = above(e[FRONT] + o[FRONT], e[FRONT] - o[FRONT])
        im = above(e[BACK] + o[BACK], e[BACK] - o[BACK])
        pairs.append((re, im))
    even = from_right([beside(re[:, FRONT], im[:, FRONT]) for re, im in pairs], 6)
    odd = from_right([beside(re[:, BACK], im[:, BACK]) for re, im in pairs], 7)
    residuals = []
    for (re, im), e, o in zip(exits, even, odd):
        back_re = beside(e[:, FRONT] + o[:, FRONT], e[:, FRONT] - o[:, FRONT])
        back_im = beside(e[:, BACK] + o[:, BACK], e[:, BACK] - o[:, BACK])
        residuals.append((back_re - re, back_im - im))
    return residuals


def pack_kernel(
    owner_ref, row_ref, col_ref, amp_ref, probe_ref, packed_ref, corners_ref, held, waves, meta_ref, come, leave
):
    def arriving(j, side):
        return pltpu.make_async_copy(
            amp_ref.at[j, :, pl.ds(side * HALF, HALF)], held.at[j, side], come.at[j, side]
        )

    def arriving_probe(part, side):
        return pltpu.make_async_copy(
            probe_ref.at[part, :, pl.ds(side * HALF, HALF)], waves.at[part, side], come.at[COUNT + part, side]
        )

    for j in range(COUNT):
        for side in range(2):
            arriving(j, side).start()
    for part in range(2):
        for side in range(2):
            arriving_probe(part, side).start()
    ranks = []
    for j in range(COUNT):
        rank = jnp.int32(0)
        for i in range(j):
            rank = rank + (owner_ref[0, i] == owner_ref[0, j]).astype(jnp.int32)
        ranks.append(rank)
    meta_ref[...] = jnp.zeros_like(meta_ref)
    sub = lax.broadcasted_iota(jnp.int32, (8, 128), 0)
    for j in range(COUNT):
        mine = (sub // 4 == ranks[j]) & (sub % 4 < 3)
        value = jnp.where(sub % 4 == 0, 1, jnp.where(sub % 4 == 1, row_ref[j], col_ref[j]))
        meta_ref[owner_ref[0, j]] = jnp.where(mine, value, meta_ref[owner_ref[0, j]])
    leaving = [pltpu.make_async_copy(meta_ref, corners_ref.at[pl.ds(0, OWNERS)], leave.at[COUNT])]
    leaving[0].start()
    for j in range(COUNT):
        for side in range(2):
            arriving(j, side).wait()
        copy = pltpu.make_async_copy(held.at[j], packed_ref.at[owner_ref[0, j], ranks[j]], leave.at[j])
        copy.start()
        leaving.append(copy)
    for part in range(2):
        for side in range(2):
            arriving_probe(part, side).wait()
    copy = pltpu.make_async_copy(waves, packed_ref.at[OWNERS], leave.at[COUNT + 1])
    copy.start()
    leaving.append(copy)
    for copy in leaving:
        copy.wait()


def pack(tile_owner, row_start, col_start, amplitude, probe):
    return pl.pallas_call(
        pack_kernel,
        out_shape=(
            jax.ShapeDtypeStruct((OWNERS + 1, CAP, 2, SIDE, HALF), F32),
            jax.ShapeDtypeStruct((SPARE, 8, 128), jnp.int32),
        ),
        in_specs=[SMEM, SMEM, SMEM, HBM, HBM],
        out_specs=(HBM, HBM),
        scratch_shapes=[
            pltpu.VMEM((COUNT, 2, SIDE, HALF), F32),
            pltpu.VMEM((2, 2, SIDE, HALF), F32),
            pltpu.VMEM((OWNERS, 8, 128), jnp.int32),
            pltpu.SemaphoreType.DMA((COUNT + 2, 2)),
            pltpu.SemaphoreType.DMA((COUNT + 2,)),
        ],
        name="pack",
    )(tile_owner.T, row_start, col_start, amplitude, probe)


def step_kernel(
    packed_ref, meta_ref, object_ref, tables_ref, out_ref, total_ref,
    probe_ref, got, got_meta, corners, strip, tables, pads, part, grad, got_x, got_y, own, rise, near, quarter, sixteenth,
    load, send, recv, send_meta, recv_meta, send_x, recv_x, send_y, recv_y,
    send_a, recv_a, send_b, recv_b, send_c, recv_c, send_d, recv_d, send_e, recv_e,
):
    me = lax.axis_index("obj")
    z = me // 2
    core = lax.rem(me, 2)
    group = lax.axis_index("pat")
    x = lax.rem(group, NX)
    y = group // NX
    last = y == NY - 1
    base = pl.multiple_of(jnp.minimum(group, 11) * STRIP, STRIP)

    def obj_at(r):
        return lax.rem(z + r // 2, OWNERS // 2) * 2 + lax.rem(core + lax.rem(r, 2), 2)

    def obj_peer(r):
        return {"obj": obj_at(r)}

    def x_peer(k):
        return {"pat": y * NX + lax.rem(x + k, NX)}

    def y_peer(k):
        return {"pat": lax.rem(y + k, NY) * NX + x}

    def remote(src, dst, send, recv, peer):
        return pltpu.make_async_remote_copy(
            src_ref=src, dst_ref=dst, send_sem=send, recv_sem=recv, device_id=peer, device_id_type=MESH
        )

    peers = [obj_peer(r) for r in range(1, OWNERS)]
    peers += [x_peer(k) for k in range(1, NX)] + [y_peer(k) for k in range(1, NY)]
    barrier = pltpu.get_barrier_semaphore()
    for peer in peers:
        pl.semaphore_signal(barrier, inc=1, device_id=peer, device_id_type=MESH)

    loads = [
        pltpu.make_async_copy(
            object_ref.at[:, pl.ds(base, SPAN), pl.ds(n * HALF, HALF)], strip.at[:, n], load.at[n]
        )
        for n in range(BLOCKS)
    ]
    loads.append(pltpu.make_async_copy(tables_ref, tables, load.at[BLOCKS]))
    loads.append(pltpu.make_async_copy(packed_ref.at[OWNERS], probe_ref, load.at[BLOCKS + 4]))
    load_meta = pltpu.make_async_copy(meta_ref.at[me], got_meta.at[0], load.at[BLOCKS + 1])
    load_own = pltpu.make_async_copy(packed_ref.at[me], got.at[0], load.at[BLOCKS + 2])

    def metas(r):
        return remote(meta_ref.at[obj_at(r)], got_meta.at[r], send_meta.at[r], recv_meta.at[r], obj_peer(r))

    def amplitudes(slot):
        r = slot // CAP
        n = lax.rem(slot, CAP)
        return remote(
            packed_ref.at[obj_at(r), n], got.at[r, n], send.at[slot], recv.at[slot], obj_peer(r)
        )

    stages = [
        [2 * (2 * dz + side) + n for n in range(CAP) for dz in distances]
        for side in (core, 1 - core)
        for distances in ((1, 3), (2,))
    ]

    def start_stage(number):
        for slot in stages[number]:
            amplitudes(slot).start()

    def end_stage(number):
        for slot in stages[number]:
            amplitudes(slot).wait_send()

    load_meta.start()
    pl.semaphore_wait(barrier, len(peers))
    for r in range(1, OWNERS):
        metas(r).start()
    start_stage(0)
    for slot in (2, 3):
        amplitudes(slot).start()
    load_own.start()
    for copy in loads:
        copy.start()
    edge = jnp.zeros((2, STRIP, HALF), F32)
    for n in range(3 * SLOTS):
        pads[n, :, pl.ds(0, STRIP), :] = edge
        pads[n, :, pl.ds(STRIP + SIDE, STRIP), :] = edge
    pads[3 * SLOTS] = jnp.zeros((2, SPAN + STRIP, HALF), F32)
    part[...] = jnp.zeros_like(part)

    def take_corners(pair):
        if pair:
            metas(2 * pair).wait_recv()
            metas(2 * pair + 1).wait_recv()
        else:
            load_meta.wait()
            metas(1).wait_recv()
        rows = pl.ds(2 * pair, 2)
        copy = pltpu.make_async_copy(got_meta.at[rows], corners.at[rows], load.at[BLOCKS + 3])
        copy.start()
        copy.wait()

    take_corners(0)
    for copy in loads:
        copy.wait()
    load_own.wait()

    lane = lax.broadcasted_iota(jnp.int32, (SIDE, HALF), 1)

    def corner(slot):
        r = slot // CAP
        at = 4 * lax.rem(slot, CAP)
        row = jnp.clip(corners[r, at + 1, 0] - base, 0, STRIP)
        col = jnp.clip(corners[r, at + 2, 0], 0, TILE - SIDE)
        start = jnp.minimum(col // HALF, BLOCKS - 3)
        return row, start, col - start * HALF

    def window(slot, part):
        row, start, shift = corner(slot)
        unshift = lax.rem(HALF - shift, HALF)
        turned = [
            pltpu.roll(strip[part, start + n, pl.ds(row, SIDE), :], unshift, axis=1) for n in range(3)
        ]
        inner = lane < HALF - shift
        return beside(jnp.where(inner, turned[0], turned[1]), jnp.where(inner, turned[1], turned[2]))

    def from_pair(k, carry):
        dz = jnp.where(k >= 6, 2, jnp.where(lax.rem(k, 2) == 0, 1, 3))
        n = jnp.where(k >= 6, k - 6, (k - 2) // 2)
        one = jnp.where(k < 2, 2 * k, 4 * dz + n)
        two = jnp.where(k < 2, 2 * k + 1, 4 * dz + 2 + n)

        for side, turn, number in ((0, 4, 0), (1, 2, 0), (1, 2, 1), (1, 4, 2)):

            @pl.when((core == side) & (k == turn))
            def _():
                end_stage(number)
                start_stage(number + 1)

        @pl.when((core == 0) & (k == 5))
        def _():
            start_stage(2)

        for pair, turn in ((1, 2), (3, 3), (2, 6)):

            @pl.when(k == turn)
            def _():
                take_corners(pair)

        @pl.when(k > 0)
        def _():
            amplitudes(one).wait_recv()
            amplitudes(two).wait_recv()

        slots = [one, two]
        probe_re = beside(probe_ref[0, 0], probe_ref[0, 1])
        probe_im = beside(probe_ref[1, 0], probe_ref[1, 1])
        windows = [(window(slot, 0), window(slot, 1)) for slot in slots]
        exits = [
            (probe_re * re - probe_im * im, probe_re * im + probe_im * re) for re, im in windows
        ]

        def wanted_rows(j, parity):
            return by_parity(
                beside(
                    got[slots[j] // CAP, lax.rem(slots[j], CAP), 0, pl.ds(parity, HALF, stride=2), :],
                    got[slots[j] // CAP, lax.rem(slots[j], CAP), 1, pl.ds(parity, HALF, stride=2), :],
                )
            )

        residuals = residual_waves(exits, wanted_rows, lambda i: (tables[i, 0], tables[i, 1]))
        part_re = part[pl.ds(0, SIDE), :]
        part_im = part[pl.ds(SIDE, SIDE), :]
        for j, slot in enumerate(slots):
            keep = corners[slot // CAP, 4 * lax.rem(slot, CAP), 0] > 0
            res_re = jnp.where(keep, residuals[j][0], 0.0)
            res_im = jnp.where(keep, residuals[j][1], 0.0)
            window_re, window_im = windows[j]
            part_re = part_re + (window_re * res_re + window_im * res_im)
            part_im = part_im + (window_re * res_im - window_im * res_re)
            shift = corner(slot)[2]
            turn = lax.rem(shift, HALF)
            outer = lane >= shift
            rows = pl.ds(STRIP, SIDE)
            for c, value in (
                (0, probe_re * res_re + probe_im * res_im),
                (1, probe_re * res_im - probe_im * res_re),
            ):
                first = pltpu.roll(value[:, FRONT], turn, axis=1)
                second = pltpu.roll(value[:, BACK], turn, axis=1)
                pads[3 * slot, c, rows, :] = jnp.where(outer, first, 0.0)
                pads[3 * slot + 1, c, rows, :] = jnp.where(outer, second, first)
                pads[3 * slot + 2, c, rows, :] = jnp.where(outer, 0.0, second)
        part[pl.ds(0, SIDE), :] = part_re
        part[pl.ds(SIDE, SIDE), :] = part_im
        return carry

    lax.fori_loop(0, OWNERS, from_pair, 0)

    def eighth(number):
        return pl.ds(pl.multiple_of(number * 64, 64), 64)

    def sixteen(number):
        return pl.ds(pl.multiple_of(number * 16, 16), 16)

    mine = pl.ds(pl.multiple_of(me * 64 + y * 16, 16), 16)

    def stage_a(r):
        return remote(part.at[eighth(obj_at(r))], near.at[r], send_a.at[r], recv_a.at[r], obj_peer(r))

    def stage_b(k):
        there = lax.rem(y + k, NY)
        return remote(near.at[0, sixteen(there)], quarter.at[k], send_b.at[k], recv_b.at[k], y_peer(k))

    def stage_c(k):
        return remote(sixteenth.at[x], sixteenth.at[x], send_c.at[k], recv_c.at[k], x_peer(k))

    def stage_d(k):
        return remote(total_ref.at[mine], total_ref.at[mine], send_d.at[k], recv_d.at[k], y_peer(k))

    def stage_e(r):
        return remote(
            total_ref.at[eighth(me)], total_ref.at[eighth(me)], send_e.at[r], recv_e.at[r], obj_peer(r)
        )

    def probe_step(number):
        if number == 0:
            for r in range(1, OWNERS):
                stage_a(r).wait()
            value = part[eighth(me), :]
            for r in range(1, OWNERS):
                value = value + near[r]
            near[0] = value
            for k in range(1, NY):
                stage_b(k).start()
        elif number == 1:
            for k in range(1, NY):
                stage_b(k).wait()
            value = near[0, sixteen(y), :]
            for k in range(1, NY):
                value = value + quarter[k]
            sixteenth[x] = value
            for k in range(1, NX):
                stage_c(k).start()
        elif number == 2:
            for k in range(1, NX):
                stage_c(k).wait()
            value = (sixteenth[0] + sixteenth[1]) + (sixteenth[2] + sixteenth[3])
            total_ref[mine, :] = value * (1.0 / math.sqrt(1024.0))
            for k in range(1, NY):
                stage_d(k).start()
        elif number == 3:
            for k in range(1, NY):
                stage_d(k).wait()
            for r in range(1, OWNERS):
                stage_e(r).start()
        else:
            for r in range(1, OWNERS):
                stage_e(r).wait()

    for r in range(1, OWNERS):
        stage_a(r).start()

    def block(number):
        return pl.ds(pl.multiple_of(number * STRIP, STRIP), STRIP)

    def along_x(c, k):
        number = jnp.where(last, lax.rem(x + k, NX) + 1, k)
        columns = pl.ds(c * CHUNK, CHUNK)
        return remote(
            grad.at[:, columns, block(number)],
            got_x.at[k - 1, :, columns],
            send_x.at[k - 1, c],
            recv_x.at[k - 1, c],
            x_peer(k),
        )

    def along_y(c):
        columns = pl.ds(c * CHUNK, CHUNK)
        return remote(rise.at[:, columns], got_y.at[:, columns], send_y.at[c], recv_y.at[c], y_peer(1))

    def gather_chunk(c, carry):
        def gather_block(b, carry):
            for part in range(2):
                value = None
                for slot in range(SLOTS):
                    row, start, _ = corner(slot)
                    n = b - start
                    at = jnp.where((n >= 0) & (n < 3), 3 * slot + n, 3 * SLOTS)
                    term = pads[at, part, pl.ds(STRIP - row, SPAN), :]
                    value = term if value is None else value + term
                grad[part, b] = value
            return carry

        lax.fori_loop(c * CHUNK, (c + 1) * CHUNK, gather_block, 0)
        for k in (2, 1, 3):
            along_x(c, k).start()
        return carry

    lax.fori_loop(0, CHUNKS // 2, gather_chunk, 0)

    @pl.when(core == 0)
    def _():
        end_stage(1)
        end_stage(2)
        start_stage(3)

    @pl.when(core == 1)
    def _():
        probe_step(0)
        probe_step(1)

    lax.fori_loop(CHUNKS // 2, CHUNKS, gather_chunk, 0)


    own_block = block(jnp.where(last, x + 1, 0))
    for c in range(CHUNKS):
        columns = pl.ds(c * CHUNK, CHUNK)
        for k in range(1, NX):
            along_x(c, k).wait_recv()
        here_too = grad[:, columns, own_block, :]
        above_too = grad[:, columns, block(4), :]
        for k in range(1, NX):
            arrived = got_x[k - 1, :, columns]
            here = (k <= x) | last
            here_too = here_too + jnp.where(here, arrived, 0.0)
            above_too = above_too + jnp.where(here, 0.0, arrived)
        own[:, columns] = here_too
        rise[:, columns] = above_too

        @pl.when(y < NY - 1)
        def _():
            along_y(c).start()

        if c in (6, 8):

            @pl.when(core == 1)
            def _():
                probe_step(c // 2 - 1)

    for c in range(CHUNKS):

        @pl.when(y > 0)
        def _():
            along_y(c).wait_recv()
            for n in range(c * CHUNK, (c + 1) * CHUNK):
                out_ref[:, :, pl.ds(n * HALF, HALF)] = own[:, n] + got_y[:, n]

        @pl.when(y == 0)
        def _():
            for n in range(c * CHUNK, (c + 1) * CHUNK):
                out_ref[:, :, pl.ds(n * HALF, HALF)] = own[:, n]

        @pl.when(y < NY - 1)
        def _():
            along_y(c).wait_send()

    @pl.when(core == 0)
    def _():
        for number in range(4):
            probe_step(number)

    for r in range(1, OWNERS):
        metas(r).wait_send()
    for slot in (2, 3):
        amplitudes(slot).wait_send()
    end_stage(3)
    for c in range(CHUNKS):
        for k in range(1, NX):
            along_x(c, k).wait_send()
    probe_step(4)


def step(packed, meta, object_field, tables):
    dma = pltpu.SemaphoreType.DMA
    return pl.pallas_call(
        step_kernel,
        out_shape=(
            jax.ShapeDtypeStruct((2, STRIP, TILE), F32),
            jax.ShapeDtypeStruct((2 * SIDE, SIDE), F32),
        ),
        in_specs=[HBM, HBM, HBM, HBM],
        out_specs=(VMEM, VMEM),
        scratch_shapes=[
            pltpu.VMEM((2, 2, SIDE, HALF), F32),
            pltpu.VMEM((OWNERS, CAP, 2, SIDE, HALF), F32),
            pltpu.VMEM((OWNERS, 8, 128), jnp.int32),
            pltpu.SMEM((OWNERS, 8, 128), jnp.int32),
            pltpu.VMEM((2, BLOCKS, SPAN, HALF), F32),
            pltpu.VMEM(tables.shape, BF16),
            pltpu.VMEM((3 * SLOTS + 1, 2, SPAN + STRIP, HALF), F32),
            pltpu.VMEM((2 * SIDE, SIDE), F32),
            pltpu.VMEM((2, BLOCKS, SPAN, HALF), F32),
            pltpu.VMEM((NX - 1, 2, BLOCKS, STRIP, HALF), F32),
            pltpu.VMEM((2, BLOCKS, STRIP, HALF), F32),
            pltpu.VMEM((2, BLOCKS, STRIP, HALF), F32),
            pltpu.VMEM((2, BLOCKS, STRIP, HALF), F32),
            pltpu.VMEM((OWNERS, 64, SIDE), F32),
            pltpu.VMEM((NY, 16, SIDE), F32),
            pltpu.VMEM((NX, 16, SIDE), F32),
            dma((BLOCKS + 5,)),
            dma((SLOTS,)),
            dma((SLOTS,)),
            dma((OWNERS,)),
            dma((OWNERS,)),
            dma((NX - 1, CHUNKS)),
            dma((NX - 1, CHUNKS)),
            dma((CHUNKS,)),
            dma((CHUNKS,)),
            dma((OWNERS,)),
            dma((OWNERS,)),
            dma((NY,)),
            dma((NY,)),
            dma((NX,)),
            dma((NX,)),
            dma((NY,)),
            dma((NY,)),
            dma((OWNERS,)),
            dma((OWNERS,)),
        ],
        compiler_params=pltpu.CompilerParams(
            collective_id=0, has_side_effects=True, vmem_limit_bytes=51 * 2**20
        ),
        name="step",
    )(packed, meta, object_field, tables)


def on_device(object_field, probe, amplitude, tile_owner, row_start, col_start):
    tables = jnp.asarray(dft_tables())
    packed, meta = pack(tile_owner, row_start, col_start, amplitude, probe)
    object_grad, probe_grad = step(packed, meta, object_field, tables)
    return object_grad, probe_grad.reshape(2, SIDE, SIDE)


def solution(mesh):
    return jax.shard_map(
        on_device,
        mesh=mesh,
        in_specs=(
            P(None, None, "obj"),
            P(),
            P(("pat", "obj"), None, None),
            P(("pat", "obj"), None),
            P(("pat", "obj")),
            P(("pat", "obj")),
        ),
        out_specs=(P(None, "pat", "obj"), P()),
        check_vma=False,
    )
```
